128 devices in a mesh: dp: 4 (over x), ctx: 32 (over z, y, core).
Axes of the slice: x: 4, y: 4, z: 4, core: 2. Of those that a mesh axis runs over, the one named last changes fastest.
Arguments:
- queries: bfloat16 [16384, 4096], P(('dp', 'ctx')), parts along dimension 0, may hold values from -8 to 8
- keys: bfloat16 [16384, 512], P(('dp', 'ctx')), parts along dimension 0, may hold values from -8 to 8
- values: bfloat16 [16384, 512], P(('dp', 'ctx')), parts along dimension 0, may hold values from -6 to 6
- grad_out: bfloat16 [16384, 4096], P(('dp', 'ctx')), parts along dimension 0, may hold values from -6 to 6
- lengths: int32 [32], P('dp'), parts along dimension 0, may hold values from 1 to 2048, 4096 in all
- plan: int32 [128], P('dp'), parts along dimension 0, may hold values from 0 to 31, each once
Outputs:
- grad_queries: float32 [16384, 4096], P(('dp', 'ctx')), parts along dimension 0
- grad_keys: float32 [16384, 512], P(('dp', 'ctx')), parts along dimension 0
- grad_values: float32 [16384, 512], P(('dp', 'ctx')), parts along dimension 0
The draws below stay inside these ranges and needn't reach their ends.
There are 4 independent parts, one for each index of `dp`. The reference program is written for one: setup_inputs(seed, part) draws one part's arguments, and reference() takes and returns one part's arrays. A program takes and returns all parts, laid end to end along the dimension named above; each array names one. Nothing has to cross between parts.
Inputs may be any that keep to these rules, and one draw needn't show every extreme that they name: The lengths sum to 4096 and the longest is exactly 2048. `plan`: each query block appears in exactly one slot.
All inputs are finite; a program needn't handle non-finite values.
Results may differ from the reference program's by a relative error of at most 0.024.
Values may be sent and summed in bfloat16 or wider, within the bound.
No kernel may reach another device: no remote copies, remote signals or barrier semaphores. Data moves between devices by JAX's collectives and lax.ppermute only.
A program may use at most 128 MiB of HBM per device.

```python
import math
import jax
import jax.numpy as jnp
import numpy as np
from jax import lax

QH = 32
KVH = 4
HD = 128
BLOCK = 128
BLOCKS_DEV = 1
SEQ = 4096
NBLK = 32
DOCS = 8
MAXDOC = 2048
N_CTX = 32


def draw_queries(key, part):
    key = jax.random.fold_in(key, 1)
    return jnp.clip(jax.random.normal(key, (SEQ, QH * HD), jnp.float32), -6.0, 6.0).astype(jnp.bfloat16)


def draw_keys(key, part):
    key = jax.random.fold_in(key, 2)
    return jnp.clip(jax.random.normal(key, (SEQ, KVH * HD), jnp.float32), -6.0, 6.0).astype(jnp.bfloat16)


def levels(rng, shape, split, smallest, top_value):
    loudness = 1.0
    for dim, parts in split:
        heights = jax.random.uniform(jax.random.fold_in(jax.random.fold_in(rng, 6), dim), (parts,), jnp.float32, smallest / len(split), top_value / len(split))
        loudness = loudness * jnp.repeat(jnp.exp(heights), shape[dim] // parts).reshape((-1,) + (1,) * (len(shape) - 1 - dim))
    return loudness


def length_profile(count, total, most, skew):
    loads = [(1 << 20) // math.isqrt(rank ** skew) + 1 for rank in range(2, count + 1)]
    spare, given = total - most - (count - 1), [1] * (count - 1)
    while spare > 0:
        free = [i for i in range(count - 1) if given[i] < most]
        whole, left = sum([loads[i] for i in free]), spare
        for i in free:
            more = min(most - given[i], max(1, left * loads[i] // whole), spare)
            given[i] = given[i] + more
            spare = spare - more
    return np.array([most] + given)


def uneven(own_key, number_of, total, limit, lean):
    if number_of == 2:
        one = jax.random.randint(own_key, (), max(1, total - limit), min(limit, total - 1) + 1)
        return jnp.stack([one, total - one])
    sizes = jnp.asarray(length_profile(number_of, total, limit, lean), jnp.int32)
    pairs = (number_of - 1) // 2
    donor, receiver = sizes[1:1 + 2 * pairs:2], sizes[2:2 + 2 * pairs:2]
    margin = jnp.minimum(donor - 1, limit - receiver)
    moved = jax.random.randint(jax.random.fold_in(own_key, 1), (pairs,), 0, 1 << 20) % (margin + 1)
    sizes = sizes.at[1:1 + 2 * pairs:2].set(donor - moved).at[2:2 + 2 * pairs:2].set(receiver + moved)
    return sizes[jax.random.permutation(jax.random.fold_in(own_key, 2), number_of)]


def bell_draw(rng, extent, scale, limit, cuts=(), held_as=jnp.bfloat16):
    result = jax.random.normal(rng, extent, jnp.float32) * scale
    if len(cuts) > 0:
        result = levels(rng, extent, cuts, -0.22, 0.18) * result
    return jnp.clip(result, min=-limit, max=limit).astype(held_as)


def setup_inputs(seed: int = 0, part: int = 0) -> dict:
    streams_of = jax.random.split(jax.random.key(seed), 7)
    part_splits = jax.random.split(jax.random.fold_in(streams_of[6], part), 7)
    queries = draw_queries(jax.random.fold_in(jax.random.fold_in(streams_of[6], part), 71), part)
    keys = draw_keys(jax.random.fold_in(jax.random.fold_in(streams_of[6], part), 71), part)
    values = bell_draw(part_splits[2], (SEQ, KVH * HD), 1.0, 6.0, ((0, 32),))
    grad_out = bell_draw(part_splits[3], (SEQ, QH * HD), 1.0, 6.0, ((0, 32),))
    lengths = uneven(part_splits[4], DOCS, SEQ, MAXDOC, 2).astype(jnp.int32)
    plan = jax.random.permutation(part_splits[5], NBLK).astype(jnp.int32)
    return {"queries": queries, "keys": keys, "values": values, "grad_out": grad_out, "lengths": lengths, "plan": plan}


def doc_index(positions, doc_ends):
    return lax.optimization_barrier(jnp.sum((positions[:, None] >= doc_ends[None, :]).astype(jnp.int32), axis=1))

def bf16_round(array):
    narrow = lax.optimization_barrier(array.astype(jnp.bfloat16))
    return narrow.astype(jnp.float32)

def reference(queries, keys, values, grad_out, lengths, plan):
    inv_root = 1.0 / math.sqrt(HD)
    group_size = QH // KVH
    window = MAXDOC + BLOCK
    key_width = KVH * HD
    doc_ends = jnp.cumsum(lengths).astype(jnp.int32)

    def block_step(sums_state, slot_index):
        grad_keys, grad_values = sums_state
        block_start = (plan[slot_index] * BLOCK).astype(jnp.int32)
        query_pos = block_start + jnp.arange(BLOCK, dtype=jnp.int32)
        key_start = jnp.clip(block_start + BLOCK - window, 0, SEQ - window).astype(jnp.int32)
        key_pos = key_start + jnp.arange(window, dtype=jnp.int32)
        row_start = (slot_index * BLOCK).astype(jnp.int32)
        query_rows = lax.dynamic_slice_in_dim(queries, row_start, BLOCK, 0).reshape(BLOCK, KVH, group_size, HD).astype(jnp.float32)
        grad_rows = lax.dynamic_slice_in_dim(grad_out, row_start, BLOCK, 0).reshape(BLOCK, KVH, group_size, HD).astype(jnp.float32)
        key_tile = lax.dynamic_slice_in_dim(keys, key_start, window, 0).reshape(window, KVH, HD).astype(jnp.float32)
        value_tile = lax.dynamic_slice_in_dim(values, key_start, window, 0).reshape(window, KVH, HD).astype(jnp.float32)
        allowed = (doc_index(query_pos, doc_ends)[:, None] == doc_index(key_pos, doc_ends)[None, :]) & (key_pos[None, :] <= query_pos[:, None])
        scores = jnp.einsum('qkgd,tkd->kgqt', query_rows, key_tile) * inv_root
        scores = jnp.where(allowed, scores, -jnp.inf)
        row_max = lax.optimization_barrier(jnp.max(scores, axis=-1))
        log_norm = row_max + jnp.log(lax.optimization_barrier(jnp.sum(jnp.exp(scores - row_max[..., None]), axis=-1)))
        probabilities = jnp.exp(scores - log_norm[..., None])
        grad_probs = jnp.einsum('qkgd,tkd->kgqt', grad_rows, value_tile)
        row_dot = lax.optimization_barrier(jnp.sum(probabilities * grad_probs, axis=-1))
        grad_scores = probabilities * (grad_probs - row_dot[..., None])
        narrow_probs = bf16_round(probabilities)
        narrow_scores = bf16_round(grad_scores)
        grad_query = jnp.einsum('kgqt,tkd->qkgd', narrow_scores, key_tile) * inv_root
        tile_keys = jnp.einsum('kgqt,qkgd->tkd', narrow_scores, query_rows).reshape(window, key_width) * inv_root
        tile_values = jnp.einsum('kgqt,qkgd->tkd', narrow_probs, grad_rows).reshape(window, key_width)
        grad_keys = lax.dynamic_update_slice_in_dim(grad_keys, lax.dynamic_slice_in_dim(grad_keys, key_start, window, 0) + tile_keys, key_start, 0)
        grad_values = lax.dynamic_update_slice_in_dim(grad_values, lax.dynamic_slice_in_dim(grad_values, key_start, window, 0) + tile_values, key_start, 0)
        return ((grad_keys, grad_values), grad_query.reshape(BLOCK, QH * HD))
    zero_rows = jnp.zeros((SEQ, key_width), jnp.float32)

    def device_step(totals, device_number):
        slots = device_number * BLOCKS_DEV + jnp.arange(BLOCKS_DEV, dtype=jnp.int32)
        partials, grad_query = lax.scan(block_step, (zero_rows, zero_rows), slots)
        key_total = totals[0] + bf16_round(partials[0])
        value_total = totals[1] + bf16_round(partials[1])
        return ((key_total, value_total), grad_query)
    totals, grad_query = lax.scan(device_step, (zero_rows, zero_rows), jnp.arange(N_CTX, dtype=jnp.int32))
    return (grad_query.reshape(SEQ, QH * HD), totals[0], totals[1])
```

```python
import math

import jax
import jax.numpy as jnp
from jax import lax
from jax.experimental import pallas as pl
from jax.experimental.pallas import tpu as pltpu
from jax.sharding import PartitionSpec as P

HD = 128
BLOCK = 128
DOCS = 8
KVH = 4
GROUP = 8
NZ = 4
NY = 4
SEQ = 4096
NBLK = 32
WIDTH = GROUP * HD
TILE = 256
MAXTILES = 9
PAIR = 256
PAIRS = WIDTH // PAIR
NEG = -1e30
INV_ROOT = 1.0 / math.sqrt(HD)
EXP_SCALE = INV_ROOT / math.log(2.0)


def ring(dz, dy, dc):
    return [
        ((z * NY + y) * 2 + c, ((z + dz) % NZ * NY + (y + dy) % NY) * 2 + (c ^ dc))
        for z in range(NZ)
        for y in range(NY)
        for c in range(2)
    ]


def send(x, dz, dy, dc):
    return lax.ppermute(x, "ctx", ring(dz, dy, dc))


def attention_kernel(
    place, plan, lengths,
    qd0, qd1, qd2, qd3, ka0, ka1, ka2, ka3, kb0, kb1, kb2, kb3,
    dq0, dq1, dq2, dq3, keep, give,
    keys, values, dkeys, dvalues, scores, probs, qs, qst, gs, gst, dqt,
):
    z, y, c = place[0], place[1], place[2]
    own, other = (ka0, ka1, ka2, ka3), (kb0, kb1, kb2, kb3)
    for core_rel, arrays in enumerate((own, other)):
        for y_rel in range(NY):
            for z_rel in range(NZ):
                slot = ((z - z_rel + NZ) % NZ * NY + (y - y_rel + NY) % NY) * 2 + (c ^ core_rel)
                rows = pl.ds(pl.multiple_of(slot * BLOCK, BLOCK), BLOCK)
                keys[rows, :] = arrays[y_rel][z_rel, :, :HD]
                values[rows, :] = arrays[y_rel][z_rel, :, HD:]

    def clear(t, carry):
        rows = pl.ds(pl.multiple_of(t * TILE, TILE), TILE)
        dkeys[rows, :] = jnp.zeros((TILE, HD), jnp.float32)
        dvalues[rows, :] = jnp.zeros((TILE, HD), jnp.float32)
        return carry

    lax.fori_loop(0, SEQ // TILE, clear, 0)

    def block(d, carry):
        for i, qd in enumerate((qd0, qd1, qd2, qd3)):
            @pl.when(d == i)
            def _(qd=qd):
                for g in range(GROUP):
                    rows = slice(g * BLOCK, (g + 1) * BLOCK)
                    q = qd[:, g * HD:(g + 1) * HD]
                    o = qd[:, WIDTH + g * HD:WIDTH + (g + 1) * HD]
                    qs[rows, :] = q
                    gs[rows, :] = o
                    qst[:, rows] = q.T
                    gst[:, rows] = o.T

        first = plan[((z - d + NZ) % NZ * NY + y) * 2 + c] * BLOCK
        pos = first + lax.broadcasted_iota(jnp.int32, (1, BLOCK), 1)
        start = jnp.zeros((1, BLOCK), jnp.int32)
        low = jnp.int32(0)
        end = jnp.int32(0)
        for e in range(DOCS):
            end = end + lengths[e]
            start = jnp.where(end <= pos, end, start)
            low = jnp.where(end <= first, end, low)
        low_tile = low // TILE
        tiles = (first + BLOCK - 1) // TILE - low_tile + 1

        def stat(t, state):
            offset = (low_tile + t) * TILE
            rows = pl.ds(pl.multiple_of(offset, TILE), TILE)
            here = pl.ds(pl.multiple_of(t * TILE, TILE), TILE)
            key_pos = offset + lax.broadcasted_iota(jnp.int32, (TILE, BLOCK), 0)
            allowed = (key_pos >= start) & (key_pos <= pos)
            allowed = jnp.concatenate([allowed] * (PAIR // BLOCK), axis=1)
            k, v = keys[rows, :], values[rows, :]
            result = []
            for p in range(PAIRS):
                cols = slice(p * PAIR, (p + 1) * PAIR)
                top, total, dot = state[p]
                s = jnp.dot(k, qst[:, cols], preferred_element_type=jnp.float32)
                s = jnp.where(allowed, s, NEG)
                g = jnp.dot(v, gst[:, cols], preferred_element_type=jnp.float32)
                new_top = jnp.maximum(top, jnp.max(s, axis=0, keepdims=True))
                factor = jnp.exp2((top - new_top) * EXP_SCALE)
                e = jnp.exp2((s - new_top) * EXP_SCALE)
                scores[here, cols] = s
                probs[here, cols] = g
                result.append((
                    new_top,
                    total * factor + jnp.sum(e, axis=0, keepdims=True),
                    dot * factor + jnp.sum(e * g, axis=0, keepdims=True),
                ))
            return tuple(result)

        zero = jnp.zeros((1, PAIR), jnp.float32)
        state = lax.fori_loop(
            0, tiles, stat, ((jnp.full((1, PAIR), NEG, jnp.float32), zero, zero),) * PAIRS
        )
        norms = [
            (top, jnp.log2(total), dot / total) for top, total, dot in state
        ]
        dqt[...] = jnp.zeros((HD, WIDTH), jnp.float32)

        def grad(t, carry):
            rows = pl.ds(pl.multiple_of((low_tile + t) * TILE, TILE), TILE)
            here = pl.ds(pl.multiple_of(t * TILE, TILE), TILE)
            kt = keys[rows, :].T
            dk = dkeys[rows, :]
            dv = dvalues[rows, :]
            for p in range(PAIRS):
                cols = slice(p * PAIR, (p + 1) * PAIR)
                top, log_total, row_dot = norms[p]
                prob = jnp.exp2((scores[here, cols] - top) * EXP_SCALE - log_total)
                ds = prob * (probs[here, cols] - row_dot)
                prob = prob.astype(jnp.bfloat16)
                ds = ds.astype(jnp.bfloat16)
                dv = dv + jnp.dot(prob, gs[cols, :], preferred_element_type=jnp.float32)
                dk = dk + jnp.dot(ds, qs[cols, :], preferred_element_type=jnp.float32)
                dqt[:, cols] += jnp.dot(kt, ds, preferred_element_type=jnp.float32)
            dkeys[rows, :] = dk
            dvalues[rows, :] = dv
            return carry

        lax.fori_loop(0, tiles, grad, 0)
        for i, dq in enumerate((dq0, dq1, dq2, dq3)):
            @pl.when(d == i)
            def _(dq=dq):
                for g in range(GROUP):
                    cols = slice(g * HD, (g + 1) * HD)
                    dq[:, cols] = (dqt[:, cols].T * INV_ROOT).astype(dq.dtype)
        return carry

    lax.fori_loop(0, NZ, block, 0)

    for core_rel, out in enumerate((keep, give)):
        for y_rel in range(NY):
            for z_rel in range(NZ):
                slot = ((z + z_rel) % NZ * NY + (y + y_rel) % NY) * 2 + (c ^ core_rel)
                rows = pl.ds(pl.multiple_of(slot * BLOCK, BLOCK), BLOCK)
                out[y_rel, z_rel, :, :HD] = (dkeys[rows, :] * INV_ROOT).astype(out.dtype)
                out[y_rel, z_rel, :, HD:] = dvalues[rows, :].astype(out.dtype)


def attention(place, plan, lengths, blocks, own, other):
    smem = pl.BlockSpec(memory_space=pltpu.SMEM)
    vmem = pl.BlockSpec(memory_space=pltpu.VMEM)
    f32, bf16 = jnp.float32, jnp.bfloat16
    return pl.pallas_call(
        attention_kernel,
        out_shape=[jax.ShapeDtypeStruct((BLOCK, WIDTH), bf16)] * NZ
        + [jax.ShapeDtypeStruct((NY, NZ, BLOCK, 2 * HD), bf16)] * 2,
        in_specs=[smem] * 3 + [vmem] * 12,
        out_specs=[vmem] * 6,
        scratch_shapes=[
            pltpu.VMEM((SEQ, HD), bf16),
            pltpu.VMEM((SEQ, HD), bf16),
            pltpu.VMEM((SEQ, HD), f32),
            pltpu.VMEM((SEQ, HD), f32),
            pltpu.VMEM((MAXTILES * TILE, WIDTH), f32),
            pltpu.VMEM((MAXTILES * TILE, WIDTH), f32),
            pltpu.VMEM((WIDTH, HD), bf16),
            pltpu.VMEM((HD, WIDTH), bf16),
            pltpu.VMEM((WIDTH, HD), bf16),
            pltpu.VMEM((HD, WIDTH), bf16),
            pltpu.VMEM((HD, WIDTH), f32),
        ],
        compiler_params=pltpu.CompilerParams(vmem_limit_bytes=48 * 1024 * 1024),
        name="attention_grads",
    )(place, plan, lengths, *blocks, *own, *other)


def shards(queries, keys, values, grad_out, lengths, plan):
    me = lax.axis_index("ctx").astype(jnp.int32)
    z, y, c = me // (2 * NY), me // 2 % NY, me % 2
    place = jnp.stack([z, y, c])

    def head_of(d):
        return (z + d) % NZ

    def kv_part(d):
        at = head_of(d) * HD
        return jnp.concatenate(
            [lax.dynamic_slice_in_dim(keys, at, HD, 1), lax.dynamic_slice_in_dim(values, at, HD, 1)],
            axis=1,
        )

    def qd_part(d):
        at = head_of(d) * WIDTH
        return jnp.concatenate(
            [
                lax.dynamic_slice_in_dim(queries, at, WIDTH, 1),
                lax.dynamic_slice_in_dim(grad_out, at, WIDTH, 1),
            ],
            axis=1,
        )

    with jax.named_scope("spread_keys"):
        row = jnp.stack([kv_part(0)] + [send(kv_part(d), d, 0, 0) for d in (1, 2, 3)])
        own = [row] + [send(row, 0, d, 0) for d in (1, 2, 3)]
        other = [send(part, 0, 0, 1) for part in own]
    with jax.named_scope("spread_queries"):
        blocks = [qd_part(0)] + [send(qd_part(d), d, 0, 0) for d in (1, 2, 3)]

    with jax.named_scope("attention"):
        *dqs, keep, give = attention(place, plan, lengths, blocks, own, other)

    with jax.named_scope("return_queries"):
        parts = [dqs[0]] + [send(dqs[d], -d, 0, 0) for d in (1, 2, 3)]
        twice = jnp.concatenate(parts + parts[:-1], axis=1)
        grad_query = lax.dynamic_slice_in_dim(
            twice, (NZ - z) % NZ * WIDTH, NZ * WIDTH, 1
        ).astype(jnp.float32)

    with jax.named_scope("return_keys"):
        both = keep.astype(jnp.float32) + send(give, 0, 0, 1).astype(jnp.float32)
        both = both.astype(jnp.bfloat16)
        total = both[0].astype(jnp.float32)
        for part in [send(both[d], 0, d, 0) for d in (1, 2, 3)]:
            total = total + part.astype(jnp.float32)
        total = total.astype(jnp.bfloat16)
        heads = [total[0]] + [send(total[d], d, 0, 0) for d in (1, 2, 3)]
        heads = heads[::-1]
        twice = jnp.stack(heads + heads[:-1], axis=1)
        ordered = lax.dynamic_slice_in_dim(twice, NZ - 1 - z, NZ, 1).astype(jnp.float32)
        grad_keys = ordered[:, :, :HD].reshape(BLOCK, KVH * HD)
        grad_values = ordered[:, :, HD:].reshape(BLOCK, KVH * HD)
    return (grad_query, grad_keys, grad_values)


def solution(mesh):
    rows = P(("dp", "ctx"), None)
    return jax.shard_map(
        shards,
        mesh=mesh,
        in_specs=(rows, rows, rows, rows, P("dp"), P("dp")),
        out_specs=(rows, rows, rows),
        check_vma=False,
    )
```

```python
import functools
import math

import jax
import jax.numpy as jnp
from jax import lax
from jax.experimental import pallas as pl
from jax.experimental.pallas import tpu as pltpu
from jax.sharding import PartitionSpec as P

HD = 128
BLOCK = 128
DOCS = 8
KVH = 4
GROUP = 8
NZ = 4
NY = 4
SEQ = 4096
NBLK = 32
WIDTH = GROUP * HD
TILE = 256
MAXTILES = 9
PAIR = 256
PAIRS = WIDTH // PAIR
NEG = -1e30
INV_ROOT = 1.0 / math.sqrt(HD)
EXP_SCALE = INV_ROOT / math.log(2.0)


SMEM = pl.BlockSpec(memory_space=pltpu.SMEM)
VMEM = pl.BlockSpec(memory_space=pltpu.VMEM)
VMEM_BYTES = 40 * 1024 * 1024
BLOCK_FLOPS = 5 * 2 * WIDTH * 1024 * HD


def cost(flops, nbytes):
    return pl.CostEstimate(flops=flops, bytes_accessed=nbytes, transcendentals=0)


def ring(dz, dy, dc):
    return [
        ((z * NY + y) * 2 + c, ((z + dz) % NZ * NY + (y + dy) % NY) * 2 + (c ^ dc))
        for z in range(NZ)
        for y in range(NY)
        for c in range(2)
    ]


def send(x, dz, dy, dc):
    return lax.ppermute(x, "ctx", ring(dz, dy, dc))


def at_head(place, d, width):
    return pl.ds(pl.multiple_of((place[0] + d + NZ) % NZ * width, width), width)


def split_kernel(width, place, left, right, *outs):
    for d, out in enumerate(outs):
        out[:, :width] = left[:, at_head(place, d, width)]
        out[:, width:] = right[:, at_head(place, d, width)]


def split_heads(place, left, right):
    width = left.shape[1] // KVH
    return pl.pallas_call(
        functools.partial(split_kernel, width),
        out_shape=[jax.ShapeDtypeStruct((BLOCK, 2 * width), left.dtype)] * NZ,
        in_specs=[SMEM, VMEM, VMEM],
        out_specs=[VMEM] * NZ,
        cost_estimate=cost(0, 4 * left.size * 2),
        name="split_heads",
    )(place, left, right)


def join_queries_kernel(place, *refs):
    *parts, out = refs
    for d, part in enumerate(parts):
        out[:, at_head(place, d, WIDTH)] = part[...].astype(out.dtype)


def join_queries(place, parts):
    return pl.pallas_call(
        join_queries_kernel,
        out_shape=jax.ShapeDtypeStruct((BLOCK, KVH * WIDTH), jnp.float32),
        in_specs=[SMEM] + [VMEM] * NZ,
        out_specs=VMEM,
        cost_estimate=cost(0, BLOCK * KVH * WIDTH * 6),
        name="join_queries",
    )(place, *parts)


def join_keys_kernel(place, *refs):
    *parts, dk, dv = refs
    for d, part in enumerate(parts):
        dk[:, at_head(place, -d, HD)] = part[:, :HD].astype(dk.dtype)
        dv[:, at_head(place, -d, HD)] = part[:, HD:].astype(dv.dtype)


def join_keys(place, parts):
    return pl.pallas_call(
        join_keys_kernel,
        out_shape=[jax.ShapeDtypeStruct((BLOCK, KVH * HD), jnp.float32)] * 2,
        in_specs=[SMEM] + [VMEM] * NZ,
        out_specs=[VMEM] * 2,
        cost_estimate=cost(0, BLOCK * KVH * HD * 12),
        name="join_keys",
    )(place, *parts)


def slots(place, sign):
    z, y, c = place[0], place[1], place[2]
    for core_rel in range(2):
        for y_rel in range(NY):
            for z_rel in range(NZ):
                slot = (
                    (z + sign * z_rel + NZ) % NZ * NY + (y + sign * y_rel + NY) % NY
                ) * 2 + (c ^ core_rel)
                yield core_rel, y_rel, z_rel, pl.ds(pl.multiple_of(slot * BLOCK, BLOCK), BLOCK)


def attend(
    place, plan, lengths, distances, qds, dqs,
    keys, values, dkeys, dvalues, scores, probs, qs, qst, gs, gst, dqt,
):
    z, y, c = place[0], place[1], place[2]

    def block(i, carry):
        d = jnp.int32(distances[0])
        for k, qd in enumerate(qds):
            d = jnp.where(i == k, distances[k], d)

            @pl.when(i == k)
            def _(qd=qd):
                for g in range(GROUP):
                    rows = slice(g * BLOCK, (g + 1) * BLOCK)
                    q = qd[:, g * HD:(g + 1) * HD]
                    o = qd[:, WIDTH + g * HD:WIDTH + (g + 1) * HD]
                    qs[rows, :] = q
                    gs[rows, :] = o
                    qst[:, rows] = q.T
                    gst[:, rows] = o.T

        first = plan[((z - d + NZ) % NZ * NY + y) * 2 + c] * BLOCK
        pos = first + lax.broadcasted_iota(jnp.int32, (1, BLOCK), 1)
        start = jnp.zeros((1, BLOCK), jnp.int32)
        low = jnp.int32(0)
        end = jnp.int32(0)
        for e in range(DOCS):
            end = end + lengths[e]
            start = jnp.where(end <= pos, end, start)
            low = jnp.where(end <= first, end, low)
        low_tile = low // TILE
        tiles = (first + BLOCK - 1) // TILE - low_tile + 1

        def stat(t, state):
            offset = (low_tile + t) * TILE
            rows = pl.ds(pl.multiple_of(offset, TILE), TILE)
            here = pl.ds(pl.multiple_of(t * TILE, TILE), TILE)
            key_pos = offset + lax.broadcasted_iota(jnp.int32, (TILE, BLOCK), 0)
            allowed = (key_pos >= start) & (key_pos <= pos)
            allowed = jnp.concatenate([allowed] * (PAIR // BLOCK), axis=1)
            k, v = keys[rows, :], values[rows, :]
            result = []
            for p in range(PAIRS):
                cols = slice(p * PAIR, (p + 1) * PAIR)
                top, total, dot = state[p]
                s = jnp.dot(k, qst[:, cols], preferred_element_type=jnp.float32)
                s = jnp.where(allowed, s * EXP_SCALE, NEG)
                g = jnp.dot(v, gst[:, cols], preferred_element_type=jnp.float32)
                new_top = jnp.maximum(top, jnp.max(s, axis=0, keepdims=True))
                factor = jnp.exp2(top - new_top)
                e = jnp.exp2(s - new_top)
                scores[here, cols] = s
                probs[here, cols] = g
                result.append((
                    new_top,
                    total * factor + jnp.sum(e, axis=0, keepdims=True),
                    dot * factor + jnp.sum(e * g, axis=0, keepdims=True),
                ))
            return tuple(result)

        zero = jnp.zeros((1, PAIR), jnp.float32)
        state = lax.fori_loop(
            0, tiles, stat, ((jnp.full((1, PAIR), NEG, jnp.float32), zero, zero),) * PAIRS
        )
        norms = [(top + jnp.log2(total), dot / total) for top, total, dot in state]
        dqt[...] = jnp.zeros((HD, WIDTH), jnp.float32)

        def grad(t, carry):
            rows = pl.ds(pl.multiple_of((low_tile + t) * TILE, TILE), TILE)
            here = pl.ds(pl.multiple_of(t * TILE, TILE), TILE)
            kt = keys[rows, :].T
            dk = dkeys[rows, :]
            dv = dvalues[rows, :]
            for p in range(PAIRS):
                cols = slice(p * PAIR, (p + 1) * PAIR)
                log_norm, row_dot = norms[p]
                prob = jnp.exp2(scores[here, cols] - log_norm)
                ds = prob * (probs[here, cols] - row_dot)
                prob = prob.astype(jnp.bfloat16)
                ds = ds.astype(jnp.bfloat16)
                dv = dv + jnp.dot(prob, gs[cols, :], preferred_element_type=jnp.float32)
                dk = dk + jnp.dot(ds, qs[cols, :], preferred_element_type=jnp.float32)
                dqt[:, cols] += jnp.dot(kt, ds, preferred_element_type=jnp.float32)
            dkeys[rows, :] = dk
            dvalues[rows, :] = dv
            return carry

        lax.fori_loop(0, tiles, grad, 0)
        for k, dq in enumerate(dqs):
            @pl.when(i == k)
            def _(dq=dq):
                for g in range(GROUP):
                    cols = slice(g * HD, (g + 1) * HD)
                    dq[:, cols] = (dqt[:, cols].T * INV_ROOT).astype(dq.dtype)
        return carry

    lax.fori_loop(0, len(distances), block, 0)


def first_kernel(distances, place, plan, lengths, *refs):
    n = len(distances)
    qds, refs = refs[:n], refs[n:]
    sources, refs = (refs[:NY], refs[NY:2 * NY]), refs[2 * NY:]
    dqs, refs = refs[:n], refs[n:]
    keys, values, dkeys, dvalues = refs[:4]
    for core_rel, y_rel, z_rel, rows in slots(place, -1):
        keys[rows, :] = sources[core_rel][y_rel][z_rel, :, :HD]
        values[rows, :] = sources[core_rel][y_rel][z_rel, :, HD:]

    def clear(t, carry):
        rows = pl.ds(pl.multiple_of(t * TILE, TILE), TILE)
        dkeys[rows, :] = jnp.zeros((TILE, HD), jnp.float32)
        dvalues[rows, :] = jnp.zeros((TILE, HD), jnp.float32)
        return carry

    lax.fori_loop(0, SEQ // TILE, clear, 0)
    attend(place, plan, lengths, distances, qds, dqs, *refs)


def last_kernel(distances, place, plan, lengths, *refs):
    n = len(distances)
    qds, refs = refs[:n], refs[n:]
    (keys, values, dkeys_in, dvalues_in), refs = refs[:4], refs[4:]
    dqs, (keep, give, dkeys, dvalues), refs = refs[:n], refs[n:n + 4], refs[n + 4:]

    def load(t, carry):
        rows = pl.ds(pl.multiple_of(t * TILE, TILE), TILE)
        dkeys[rows, :] = dkeys_in[rows, :]
        dvalues[rows, :] = dvalues_in[rows, :]
        return carry

    lax.fori_loop(0, SEQ // TILE, load, 0)
    attend(place, plan, lengths, distances, qds, dqs, keys, values, dkeys, dvalues, *refs)
    for core_rel, y_rel, z_rel, rows in slots(place, 1):
        out = (keep, give)[core_rel]
        out[y_rel, z_rel, :, :HD] = (dkeys[rows, :] * INV_ROOT).astype(out.dtype)
        out[y_rel, z_rel, :, HD:] = dvalues[rows, :].astype(out.dtype)


def work_arrays():
    return [
        pltpu.VMEM((MAXTILES * TILE, WIDTH), jnp.float32),
        pltpu.VMEM((MAXTILES * TILE, WIDTH), jnp.float32),
        pltpu.VMEM((WIDTH, HD), jnp.bfloat16),
        pltpu.VMEM((HD, WIDTH), jnp.bfloat16),
        pltpu.VMEM((WIDTH, HD), jnp.bfloat16),
        pltpu.VMEM((HD, WIDTH), jnp.bfloat16),
        pltpu.VMEM((HD, WIDTH), jnp.float32),
    ]


def attend_first(place, plan, lengths, distances, qds, own, other):
    n = len(distances)
    *dqs, keys, values, dkeys, dvalues = pl.pallas_call(
        functools.partial(first_kernel, distances),
        out_shape=[jax.ShapeDtypeStruct((BLOCK, WIDTH), jnp.bfloat16)] * n
        + [jax.ShapeDtypeStruct((SEQ, HD), jnp.bfloat16)] * 2
        + [jax.ShapeDtypeStruct((SEQ, HD), jnp.float32)] * 2,
        in_specs=[SMEM] * 3 + [VMEM] * (n + 2 * NY),
        out_specs=[VMEM] * (n + 4),
        scratch_shapes=work_arrays(),
        compiler_params=pltpu.CompilerParams(vmem_limit_bytes=VMEM_BYTES),
        cost_estimate=cost(n * BLOCK_FLOPS, 8 * 2**20),
        name="attention_first",
    )(place, plan, lengths, *qds, *own, *other)
    return dqs, (keys, values, dkeys, dvalues)


def attend_last(place, plan, lengths, distances, qds, state):
    n = len(distances)
    return pl.pallas_call(
        functools.partial(last_kernel, distances),
        out_shape=[jax.ShapeDtypeStruct((BLOCK, WIDTH), jnp.bfloat16)] * n
        + [jax.ShapeDtypeStruct((NY, NZ, BLOCK, 2 * HD), jnp.bfloat16)] * 2,
        in_specs=[SMEM] * 3 + [VMEM] * (n + 4),
        out_specs=[VMEM] * (n + 2),
        scratch_shapes=[pltpu.VMEM((SEQ, HD), jnp.float32)] * 2 + work_arrays(),
        compiler_params=pltpu.CompilerParams(vmem_limit_bytes=VMEM_BYTES),
        cost_estimate=cost(n * BLOCK_FLOPS, 8 * 2**20),
        name="attention_last",
    )(place, plan, lengths, *qds, *state)


def shards(queries, keys, values, grad_out, lengths, plan):
    me = lax.axis_index("ctx").astype(jnp.int32)
    place = jnp.stack([me // (2 * NY), me // 2 % NY, me % 2])

    with jax.named_scope("spread_keys"):
        kv = split_heads(place, keys, values)
        row = jnp.stack([kv[0]] + [send(kv[d], d, 0, 0) for d in (1, 2, 3)])
        own = [row] + [send(row, 0, d, 0) for d in (1, 2, 3)]
        other = [send(part, 0, 0, 1) for part in own]
    with jax.named_scope("spread_queries"):
        qd = split_heads(place, queries, grad_out)
        near = [send(qd[d], d, 0, 0) for d in (1, 3)]
        late, near = lax.optimization_barrier((qd[2], near))
        far = send(late, 2, 0, 0)

    with jax.named_scope("attention"):
        (dq0, dq1, dq3), state = attend_first(
            place, plan, lengths, (0, 1, 3), (qd[0], *near), own, other
        )
        dq2, keep, give = attend_last(place, plan, lengths, (2,), (far,), state)

    with jax.named_scope("return_queries"):
        back1, back3 = send(dq1, -1, 0, 0), send(dq3, -3, 0, 0)
        give, back1, back3 = lax.optimization_barrier((give, back1, back3))
        back2 = send(dq2, -2, 0, 0)
        grad_query = join_queries(place, (dq0, back1, back2, back3))

    with jax.named_scope("return_keys"):
        both = keep.astype(jnp.float32) + send(give, 0, 0, 1).astype(jnp.float32)
        both = both.astype(jnp.bfloat16)
        total = both[0].astype(jnp.float32)
        for part in [send(both[d], 0, d, 0) for d in (1, 2, 3)]:
            total = total + part.astype(jnp.float32)
        total = total.astype(jnp.bfloat16)
        grad_keys, grad_values = join_keys(
            place, [total[0]] + [send(total[d], d, 0, 0) for d in (1, 2, 3)]
        )
    return (grad_query, grad_keys, grad_values)


def solution(mesh):
    rows = P(("dp", "ctx"), None)
    return jax.shard_map(
        shards,
        mesh=mesh,
        in_specs=(rows, rows, rows, rows, P("dp"), P("dp")),
        out_specs=(rows, rows, rows),
        check_vma=False,
    )
```

```python
import functools
import math

import jax
import jax.numpy as jnp
from jax import lax
from jax.experimental import pallas as pl
from jax.experimental.pallas import tpu as pltpu
from jax.sharding import PartitionSpec as P

HD = 128
BLOCK = 128
DOCS = 8
KVH = 4
GROUP = 8
NZ = 4
NY = 4
SEQ = 4096
NBLK = 32
WIDTH = GROUP * HD
TILE = 256
MAXTILES = 9
SIZES = (2, 1)
PAIR = 256
PAIRS = WIDTH // PAIR
NEG = -1e30
INV_ROOT = 1.0 / math.sqrt(HD)
EXP_SCALE = INV_ROOT / math.log(2.0)


SMEM = pl.BlockSpec(memory_space=pltpu.SMEM)
VMEM = pl.BlockSpec(memory_space=pltpu.VMEM)
VMEM_BYTES = 40 * 1024 * 1024
BLOCK_FLOPS = 5 * 2 * WIDTH * 1024 * HD


def cost(flops, nbytes):
    return pl.CostEstimate(flops=flops, bytes_accessed=nbytes, transcendentals=0)


def ring(dz, dy, dc):
    return [
        ((z * NY + y) * 2 + c, ((z + dz) % NZ * NY + (y + dy) % NY) * 2 + (c ^ dc))
        for z in range(NZ)
        for y in range(NY)
        for c in range(2)
    ]


def send(x, dz, dy, dc):
    return lax.ppermute(x, "ctx", ring(dz, dy, dc))


def at_head(place, d, width):
    return pl.ds(pl.multiple_of((place[0] + d + NZ) % NZ * width, width), width)


def here():
    me = lax.axis_index("ctx")
    return lax.shift_right_logical(me, 3), lax.shift_right_logical(me, 1) & 3, me & 1


def split_kernel(width, left, right, *outs):
    place = here()
    for d, out in enumerate(outs):
        out[:, :width] = left[:, at_head(place, d, width)]
        out[:, width:] = right[:, at_head(place, d, width)]


def split_heads(left, right):
    width = left.shape[1] // KVH
    return pl.pallas_call(
        functools.partial(split_kernel, width),
        out_shape=[jax.ShapeDtypeStruct((BLOCK, 2 * width), left.dtype)] * NZ,
        in_specs=[VMEM, VMEM],
        out_specs=[VMEM] * NZ,
        compiler_params=pltpu.CompilerParams(vmem_limit_bytes=12 * 2**20),
        cost_estimate=cost(0, 4 * left.size * 2),
        name="split_heads",
    )(left, right)


def join_queries_kernel(*refs):
    place = here()
    *parts, out = refs
    for d, part in enumerate(parts):
        out[:, at_head(place, d, WIDTH)] = part[...].astype(out.dtype)


def join_queries(parts):
    return pl.pallas_call(
        join_queries_kernel,
        out_shape=jax.ShapeDtypeStruct((BLOCK, KVH * WIDTH), jnp.float32),
        in_specs=[VMEM] * NZ,
        out_specs=VMEM,
        compiler_params=pltpu.CompilerParams(vmem_limit_bytes=12 * 2**20),
        cost_estimate=cost(0, BLOCK * KVH * WIDTH * 6),
        name="join_queries",
    )(*parts)


def join_keys_kernel(*refs):
    place = here()
    *parts, dk, dv = refs
    for d, part in enumerate(parts):
        dk[:, at_head(place, -d, HD)] = part[:, :HD].astype(dk.dtype)
        dv[:, at_head(place, -d, HD)] = part[:, HD:].astype(dv.dtype)


def join_keys(parts):
    return pl.pallas_call(
        join_keys_kernel,
        out_shape=[jax.ShapeDtypeStruct((BLOCK, KVH * HD), jnp.float32)] * 2,
        in_specs=[VMEM] * NZ,
        out_specs=[VMEM] * 2,
        compiler_params=pltpu.CompilerParams(vmem_limit_bytes=12 * 2**20),
        cost_estimate=cost(0, BLOCK * KVH * HD * 12),
        name="join_keys",
    )(*parts)


def slots(place, sign):
    z, y, c = place[0], place[1], place[2]
    for core_rel in range(2):
        for y_rel in range(NY):
            for z_rel in range(NZ):
                slot = (
                    (z + sign * z_rel + NZ) % NZ * NY + (y + sign * y_rel + NY) % NY
                ) * 2 + (c ^ core_rel)
                yield core_rel, y_rel, z_rel, pl.ds(pl.multiple_of(slot * BLOCK, BLOCK), BLOCK)


def attend(
    place, plan, lengths, distances, qds, dqs,
    keys, values, dkeys, dvalues, scores, probs, qs, qst, gs, gst, dqt,
):
    z, y, c = place[0], place[1], place[2]

    def block(i, carry):
        d = jnp.int32(distances[0])
        for k, qd in enumerate(qds):
            d = jnp.where(i == k, distances[k], d)

            @pl.when(i == k)
            def _(qd=qd):
                for g in range(GROUP):
                    rows = slice(g * BLOCK, (g + 1) * BLOCK)
                    q = qd[:, g * HD:(g + 1) * HD]
                    o = qd[:, WIDTH + g * HD:WIDTH + (g + 1) * HD]
                    qs[rows, :] = q
                    gs[rows, :] = o
                    qst[:, rows] = q.T
                    gst[:, rows] = o.T

        first = plan[((z - d + NZ) % NZ * NY + y) * 2 + c] * BLOCK
        pos = first + lax.broadcasted_iota(jnp.int32, (1, BLOCK), 1)
        start = jnp.zeros((1, BLOCK), jnp.int32)
        low = jnp.int32(0)
        end = jnp.int32(0)
        for e in range(DOCS):
            end = end + lengths[e]
            start = jnp.where(end <= pos, end, start)
            low = jnp.where(end <= first, end, low)
        tiles = (first + BLOCK - low // BLOCK * BLOCK + TILE - 1) // TILE
        base = jnp.maximum(first + BLOCK - tiles * TILE, 0)

        def sweep(body, state):
            done = jnp.int32(0)
            for size in SIZES:
                count = (tiles - done) // size
                state = lax.fori_loop(
                    0,
                    count,
                    lambda t, state, done=done, size=size: body(
                        (done + t * size) * TILE, size * TILE, state
                    ),
                    state,
                )
                done = done + count * size
            return state

        def stat(offset, size, state):
            offset = pl.multiple_of(offset, TILE)
            rows = pl.ds(pl.multiple_of(base + offset, BLOCK), size)
            key_pos = base + offset + lax.broadcasted_iota(jnp.int32, (size, BLOCK), 0)
            allowed = (key_pos >= start) & (key_pos <= pos)
            allowed = jnp.concatenate([allowed] * (PAIR // BLOCK), axis=1)
            k, v = keys[rows, :], values[rows, :]
            result = []

            def fold(x, op):
                x = x.reshape(-1, 8, PAIR)
                out = x[0]
                for i in range(1, x.shape[0]):
                    out = op(out, x[i])
                return out

            def dots(p):
                cols = slice(p * PAIR, (p + 1) * PAIR)
                high = None
                for r in range(0, size, TILE):
                    at = pl.ds(offset + r, TILE)
                    s = jnp.dot(k[r:r + TILE], qst[:, cols], preferred_element_type=jnp.float32)
                    s = jnp.where(allowed[r:r + TILE], s * EXP_SCALE, NEG)
                    scores[at, cols] = s
                    here_high = fold(s, jnp.maximum)
                    high = here_high if high is None else jnp.maximum(high, here_high)
                    probs[at, cols] = jnp.dot(v[r:r + TILE], gst[:, cols], preferred_element_type=jnp.float32)
                return high

            def sums(p, high):
                cols = slice(p * PAIR, (p + 1) * PAIR)
                top, total, dot = state[p]
                new_top = jnp.maximum(top, jnp.max(high, axis=0, keepdims=True))
                factor = jnp.exp2(top - new_top)
                add, mul = jnp.zeros((8, PAIR), jnp.float32), jnp.zeros((8, PAIR), jnp.float32)
                for r in range(0, size, TILE):
                    at = pl.ds(offset + r, TILE)
                    e = jnp.exp2(scores[at, cols] - new_top)
                    add = add + fold(e, jnp.add)
                    mul = mul + fold(e * probs[at, cols], jnp.add)
                result.append((
                    new_top,
                    total * factor + jnp.sum(add, axis=0, keepdims=True),
                    dot * factor + jnp.sum(mul, axis=0, keepdims=True),
                ))

            ahead = [dots(p) for p in range(1)]
            for p in range(PAIRS):
                if p + 1 < PAIRS:
                    ahead.append(dots(p + 1))
                sums(p, ahead[p])
            return tuple(result)

        zero = jnp.zeros((1, PAIR), jnp.float32)
        state = sweep(stat, ((jnp.full((1, PAIR), NEG, jnp.float32), zero, zero),) * PAIRS)
        norms = [(top + jnp.log2(total), dot / total) for top, total, dot in state]
        dqt[...] = jnp.zeros((HD, WIDTH), jnp.float32)

        def grad(offset, size, carry):
            offset = pl.multiple_of(offset, TILE)
            rows = pl.ds(pl.multiple_of(base + offset, BLOCK), size)
            at = pl.ds(offset, size)
            kt = keys[rows, :].T
            dk = dkeys[rows, :]
            dv = dvalues[rows, :]
            for p in range(PAIRS):
                cols = slice(p * PAIR, (p + 1) * PAIR)
                log_norm, row_dot = norms[p]
                prob = jnp.exp2(scores[at, cols] - log_norm)
                ds = prob * (probs[at, cols] - row_dot)
                prob = prob.astype(jnp.bfloat16)
                ds = ds.astype(jnp.bfloat16)
                dv = dv + jnp.dot(prob, gs[cols, :], preferred_element_type=jnp.float32)
                dk = dk + jnp.dot(ds, qs[cols, :], preferred_element_type=jnp.float32)
                dqt[:, cols] += jnp.dot(kt, ds, preferred_element_type=jnp.float32)
            dkeys[rows, :] = dk
            dvalues[rows, :] = dv
            return carry

        sweep(grad, 0)
        for k, dq in enumerate(dqs):
            @pl.when(i == k)
            def _(dq=dq):
                for g in range(GROUP):
                    cols = slice(g * HD, (g + 1) * HD)
                    dq[:, cols] = (dqt[:, cols].T * INV_ROOT).astype(dq.dtype)
        return carry

    lax.fori_loop(0, len(distances), block, 0)


def first_kernel(distances, plan, lengths, *refs):
    place = here()
    n = len(distances)
    qds, refs = refs[:n], refs[n:]
    sources, refs = (refs[:NY], refs[NY:2 * NY]), refs[2 * NY:]
    dqs, refs = refs[:n], refs[n:]
    keys, values, dkeys, dvalues = refs[:4]
    for core_rel, y_rel, z_rel, rows in slots(place, -1):
        keys[rows, :] = sources[core_rel][y_rel][z_rel, :, :HD]
        values[rows, :] = sources[core_rel][y_rel][z_rel, :, HD:]

    def clear(t, carry):
        rows = pl.ds(pl.multiple_of(t * TILE, TILE), TILE)
        dkeys[rows, :] = jnp.zeros((TILE, HD), jnp.float32)
        dvalues[rows, :] = jnp.zeros((TILE, HD), jnp.float32)
        return carry

    lax.fori_loop(0, SEQ // TILE, clear, 0)
    attend(place, plan, lengths, distances, qds, dqs, *refs)


def last_kernel(distances, plan, lengths, *refs):
    place = here()
    n = len(distances)
    qds, refs = refs[:n], refs[n:]
    (keys, values, dkeys_in, dvalues_in), refs = refs[:4], refs[4:]
    dqs, (keep, give, dkeys, dvalues), refs = refs[:n], refs[n:n + 4], refs[n + 4:]

    def load(t, carry):
        rows = pl.ds(pl.multiple_of(t * TILE, TILE), TILE)
        dkeys[rows, :] = dkeys_in[rows, :]
        dvalues[rows, :] = dvalues_in[rows, :]
        return carry

    lax.fori_loop(0, SEQ // TILE, load, 0)
    attend(place, plan, lengths, distances, qds, dqs, keys, values, dkeys, dvalues, *refs)
    for core_rel, y_rel, z_rel, rows in slots(place, 1):
        out = (keep, give)[core_rel]
        out[y_rel, z_rel, :, :HD] = (dkeys[rows, :] * INV_ROOT).astype(out.dtype)
        out[y_rel, z_rel, :, HD:] = dvalues[rows, :].astype(out.dtype)


def work_arrays():
    return [
        pltpu.VMEM((MAXTILES * TILE, WIDTH), jnp.float32),
        pltpu.VMEM((MAXTILES * TILE, WIDTH), jnp.float32),
        pltpu.VMEM((WIDTH, HD), jnp.bfloat16),
        pltpu.VMEM((HD, WIDTH), jnp.bfloat16),
        pltpu.VMEM((WIDTH, HD), jnp.bfloat16),
        pltpu.VMEM((HD, WIDTH), jnp.bfloat16),
        pltpu.VMEM((HD, WIDTH), jnp.float32),
    ]


def attend_first(plan, lengths, distances, qds, own, other):
    n = len(distances)
    *dqs, keys, values, dkeys, dvalues = pl.pallas_call(
        functools.partial(first_kernel, distances),
        out_shape=[jax.ShapeDtypeStruct((BLOCK, WIDTH), jnp.bfloat16)] * n
        + [jax.ShapeDtypeStruct((SEQ, HD), jnp.bfloat16)] * 2
        + [jax.ShapeDtypeStruct((SEQ, HD), jnp.float32)] * 2,
        in_specs=[SMEM] * 2 + [VMEM] * (n + 2 * NY),
        out_specs=[VMEM] * (n + 4),
        scratch_shapes=work_arrays(),
        compiler_params=pltpu.CompilerParams(vmem_limit_bytes=VMEM_BYTES),
        cost_estimate=cost(n * BLOCK_FLOPS, 8 * 2**20),
        name="attention_first",
    )(plan, lengths, *qds, *own, *other)
    return dqs, (keys, values, dkeys, dvalues)


def attend_last(plan, lengths, distances, qds, state):
    n = len(distances)
    return pl.pallas_call(
        functools.partial(last_kernel, distances),
        out_shape=[jax.ShapeDtypeStruct((BLOCK, WIDTH), jnp.bfloat16)] * n
        + [jax.ShapeDtypeStruct((NY, NZ, BLOCK, 2 * HD), jnp.bfloat16)] * 2,
        in_specs=[SMEM] * 2 + [VMEM] * (n + 4),
        out_specs=[VMEM] * (n + 2),
        scratch_shapes=[pltpu.VMEM((SEQ, HD), jnp.float32)] * 2 + work_arrays(),
        compiler_params=pltpu.CompilerParams(vmem_limit_bytes=VMEM_BYTES),
        cost_estimate=cost(n * BLOCK_FLOPS, 8 * 2**20),
        name="attention_last",
    )(plan, lengths, *qds, *state)


def shards(queries, keys, values, grad_out, lengths, plan):
    with jax.named_scope("spread_keys"):
        kv = split_heads(keys, values)
        row = [kv[0]] + [send(kv[d], d, 0, 0) for d in (1, 2, 3)]
        qd = split_heads(queries, grad_out)
        row, qd = lax.optimization_barrier((row, qd))
        row = jnp.stack(row)
        own = [row] + [send(row, 0, d, 0) for d in (1, 2, 3)]
        other = [send(part, 0, 0, 1) for part in own]
    with jax.named_scope("spread_queries"):
        near = [send(qd[d], d, 0, 0) for d in (1, 3)]
        late, near = lax.optimization_barrier((qd[2], near))
        far = send(late, 2, 0, 0)

    with jax.named_scope("attention"):
        (dq0, dq1, dq3), state = attend_first(
            plan, lengths, (0, 1, 3), (qd[0], *near), own, other
        )
        dq2, keep, give = attend_last(plan, lengths, (2,), (far,), state)

    with jax.named_scope("return_queries"):
        back1, back3 = send(dq1, -1, 0, 0), send(dq3, -3, 0, 0)
        give, back1, back3 = lax.optimization_barrier((give, back1, back3))
        back2 = send(dq2, -2, 0, 0)
        grad_query = join_queries((dq0, back1, back2, back3))

    with jax.named_scope("return_keys"):
        both = keep.astype(jnp.float32) + send(give, 0, 0, 1).astype(jnp.float32)
        both = both.astype(jnp.bfloat16)
        total = both[0].astype(jnp.float32)
        for part in [send(both[d], 0, d, 0) for d in (1, 2, 3)]:
            total = total + part.astype(jnp.float32)
        total = total.astype(jnp.bfloat16)
        grad_keys, grad_values = join_keys(
            [total[0]] + [send(total[d], d, 0, 0) for d in (1, 2, 3)]
        )
    return (grad_query, grad_keys, grad_values)


def solution(mesh):
    rows = P(("dp", "ctx"), None)
    return jax.shard_map(
        shards,
        mesh=mesh,
        in_specs=(rows, rows, rows, rows, P("dp"), P("dp")),
        out_specs=(rows, rows, rows),
        check_vma=False,
    )
```

```python
import functools
import math

import jax
import jax.numpy as jnp
from jax import lax
from jax.experimental import pallas as pl
from jax.experimental.pallas import tpu as pltpu
from jax.sharding import PartitionSpec as P

HD = 128
BLOCK = 128
DOCS = 8
KVH = 4
GROUP = 8
NZ = 4
NY = 4
SEQ = 4096
NBLK = 32
WIDTH = GROUP * HD
TILE = 256
MAXTILES = 9
SIZES = (2, 1)
PAIR = 256
PAIRS = WIDTH // PAIR
NEG = -1e30
INV_ROOT = 1.0 / math.sqrt(HD)
EXP_SCALE = INV_ROOT / math.log(2.0)


SMEM = pl.BlockSpec(memory_space=pltpu.SMEM)
VMEM = pl.BlockSpec(memory_space=pltpu.VMEM)
HBM = pl.BlockSpec(memory_space=pltpu.HBM)
SMALL_VMEM_BYTES = 12 * 1024 * 1024
PACK_VMEM_BYTES = 56 * 1024 * 1024
VMEM_BYTES = 40 * 1024 * 1024
BLOCK_FLOPS = 5 * 2 * WIDTH * 1024 * HD


def cost(flops, nbytes):
    return pl.CostEstimate(flops=flops, bytes_accessed=nbytes, transcendentals=0)


def ring(dz, dy, dc):
    return [
        ((z * NY + y) * 2 + c, ((z + dz) % NZ * NY + (y + dy) % NY) * 2 + (c ^ dc))
        for z in range(NZ)
        for y in range(NY)
        for c in range(2)
    ]


SAME_CORE = [[chip * 2 + core for chip in range(NZ * NY)] for core in range(2)]


def exchange(x):
    return lax.all_to_all(
        x, "ctx", split_axis=0, concat_axis=0, axis_index_groups=SAME_CORE, tiled=True
    )


def send(x, dz, dy, dc):
    return lax.ppermute(x, "ctx", ring(dz, dy, dc))


def at_head(place, d, width):
    return pl.ds(pl.multiple_of((place[0] + d + NZ) % NZ * width, width), width)


def here():
    me = lax.axis_index("ctx")
    return lax.shift_right_logical(me, 3), lax.shift_right_logical(me, 1) & 3, me & 1


def pack_kernel(width, left, right, *refs):
    outs, sems = refs[:NZ], refs[NZ]
    place = here()
    copies = []
    for d, out in enumerate(outs):
        for half, source in enumerate((left, right)):
            copies.append(pltpu.make_async_copy(
                source.at[:, at_head(place, d, width)],
                out.at[:, half * width:(half + 1) * width],
                sems.at[len(copies)],
            ))
            copies[-1].start()
    for copy in copies:
        copy.wait()


def pack(left, right):
    width = left.shape[1] // KVH
    return pl.pallas_call(
        functools.partial(pack_kernel, width),
        out_shape=[jax.ShapeDtypeStruct((BLOCK, 2 * width), left.dtype)] * NZ,
        in_specs=[HBM] * 2,
        out_specs=[VMEM] * NZ,
        scratch_shapes=[pltpu.SemaphoreType.DMA((2 * NZ,))],
        compiler_params=pltpu.CompilerParams(vmem_limit_bytes=PACK_VMEM_BYTES),
        cost_estimate=cost(0, 4 * left.size * 2),
        name="pack",
    )(left, right)


def put_heads(place, parts, out, wide, sems):
    copies = []
    for i, (d, part) in enumerate(parts):
        wide[i] = part[...].astype(wide.dtype)
        copies.append(
            pltpu.make_async_copy(wide.at[i], out.at[:, at_head(place, d, WIDTH)], sems.at[i])
        )
        copies[-1].start()
    return copies


def join_near_kernel(dq0, dq1, dq3, out, wide, sems):
    for copy in put_heads(here(), ((0, dq0), (1, dq1), (3, dq3)), out, wide, sems):
        copy.wait()


def join_near(dq0, dq1, dq3):
    return pl.pallas_call(
        join_near_kernel,
        out_shape=jax.ShapeDtypeStruct((BLOCK, KVH * WIDTH), jnp.float32),
        in_specs=[VMEM] * 3,
        out_specs=HBM,
        scratch_shapes=[
            pltpu.VMEM((3, BLOCK, WIDTH), jnp.float32),
            pltpu.SemaphoreType.DMA((3,)),
        ],
        compiler_params=pltpu.CompilerParams(vmem_limit_bytes=SMALL_VMEM_BYTES),
        cost_estimate=cost(0, BLOCK * KVH * WIDTH * 6),
        name="join_near",
    )(dq0, dq1, dq3)


def finish_kernel(partials, dq2, grad_in, out, dk, dv, wide, sems):
    copies = put_heads(here(), ((2, dq2),), out, wide, sems)
    for h in range(KVH):
        total = partials[h * NY].astype(jnp.float32)
        for y in range(1, NY):
            total = total + partials[h * NY + y].astype(jnp.float32)
        dk[:, h * HD:(h + 1) * HD] = total[:, :HD]
        dv[:, h * HD:(h + 1) * HD] = total[:, HD:]
    for copy in copies:
        copy.wait()


def finish(partials, dq2, grad_query):
    return pl.pallas_call(
        finish_kernel,
        out_shape=[jax.ShapeDtypeStruct((BLOCK, KVH * WIDTH), jnp.float32)]
        + [jax.ShapeDtypeStruct((BLOCK, KVH * HD), jnp.float32)] * 2,
        in_specs=[VMEM, VMEM, HBM],
        out_specs=[HBM, VMEM, VMEM],
        input_output_aliases={2: 0},
        scratch_shapes=[
            pltpu.VMEM((1, BLOCK, WIDTH), jnp.float32),
            pltpu.SemaphoreType.DMA((1,)),
        ],
        compiler_params=pltpu.CompilerParams(vmem_limit_bytes=SMALL_VMEM_BYTES),
        cost_estimate=cost(0, 4 * 2**20),
        name="finish",
    )(partials, dq2, grad_query)


def slots(place):
    for core_rel in range(2):
        for chip in range(NZ * NY):
            slot = chip * 2 + (place[2] ^ core_rel)
            yield core_rel, chip, pl.ds(pl.multiple_of(slot * BLOCK, BLOCK), BLOCK)


def attend(
    place, plan, lengths, distances, qds, dqs,
    keys, values, dkeys, dvalues, scores, probs, qs, qst, gs, gst, dqt,
):
    z, y, c = place[0], place[1], place[2]

    def block(i, carry):
        d = jnp.int32(distances[0])
        for k, qd in enumerate(qds):
            d = jnp.where(i == k, distances[k], d)

            @pl.when(i == k)
            def _(qd=qd):
                for g in range(GROUP):
                    rows = slice(g * BLOCK, (g + 1) * BLOCK)
                    q = qd[:, g * HD:(g + 1) * HD]
                    o = qd[:, WIDTH + g * HD:WIDTH + (g + 1) * HD]
                    qs[rows, :] = q
                    gs[rows, :] = o
                    qst[:, rows] = q.T
                    gst[:, rows] = o.T

        first = plan[((z - d + NZ) % NZ * NY + y) * 2 + c] * BLOCK
        pos = first + lax.broadcasted_iota(jnp.int32, (1, BLOCK), 1)
        start = jnp.zeros((1, BLOCK), jnp.int32)
        low = jnp.int32(0)
        end = jnp.int32(0)
        for e in range(DOCS):
            end = end + lengths[e]
            start = jnp.where(end <= pos, end, start)
            low = jnp.where(end <= first, end, low)
        tiles = (first + BLOCK - low // BLOCK * BLOCK + TILE - 1) // TILE
        base = jnp.maximum(first + BLOCK - tiles * TILE, 0)

        def sweep(body, state):
            done = jnp.int32(0)
            for size in SIZES:
                count = (tiles - done) // size
                state = lax.fori_loop(
                    0,
                    count,
                    lambda t, state, done=done, size=size: body(
                        (done + t * size) * TILE, size * TILE, state
                    ),
                    state,
                )
                done = done + count * size
            return state

        def stat(offset, size, state):
            offset = pl.multiple_of(offset, TILE)
            rows = pl.ds(pl.multiple_of(base + offset, BLOCK), size)
            key_pos = base + offset + lax.broadcasted_iota(jnp.int32, (size, BLOCK), 0)
            allowed = (key_pos >= start) & (key_pos <= pos)
            allowed = jnp.concatenate([allowed] * (PAIR // BLOCK), axis=1)
            k, v = keys[rows, :], values[rows, :]
            result = []

            def fold(x, op):
                x = x.reshape(-1, 8, PAIR)
                out = x[0]
                for i in range(1, x.shape[0]):
                    out = op(out, x[i])
                return out

            def dots(p):
                cols = slice(p * PAIR, (p + 1) * PAIR)
                high = None
                for r in range(0, size, TILE):
                    at = pl.ds(offset + r, TILE)
                    s = jnp.dot(k[r:r + TILE], qst[:, cols], preferred_element_type=jnp.float32)
                    s = jnp.where(allowed[r:r + TILE], s * EXP_SCALE, NEG)
                    scores[at, cols] = s
                    here_high = fold(s, jnp.maximum)
                    high = here_high if high is None else jnp.maximum(high, here_high)
                    probs[at, cols] = jnp.dot(v[r:r + TILE], gst[:, cols], preferred_element_type=jnp.float32)
                return high

            def sums(p, high):
                cols = slice(p * PAIR, (p + 1) * PAIR)
                top, total, dot = state[p]
                new_top = jnp.maximum(top, jnp.max(high, axis=0, keepdims=True))
                factor = jnp.exp2(top - new_top)
                add, mul = jnp.zeros((8, PAIR), jnp.float32), jnp.zeros((8, PAIR), jnp.float32)
                for r in range(0, size, TILE):
                    at = pl.ds(offset + r, TILE)
                    e = jnp.exp2(scores[at, cols] - new_top)
                    add = add + fold(e, jnp.add)
                    mul = mul + fold(e * probs[at, cols], jnp.add)
                result.append((
                    new_top,
                    total * factor + jnp.sum(add, axis=0, keepdims=True),
                    dot * factor + jnp.sum(mul, axis=0, keepdims=True),
                ))

            ahead = [dots(p) for p in range(1)]
            for p in range(PAIRS):
                if p + 1 < PAIRS:
                    ahead.append(dots(p + 1))
                sums(p, ahead[p])
            return tuple(result)

        zero = jnp.zeros((1, PAIR), jnp.float32)
        state = sweep(stat, ((jnp.full((1, PAIR), NEG, jnp.float32), zero, zero),) * PAIRS)
        norms = [(top + jnp.log2(total), dot / total) for top, total, dot in state]
        dqt[...] = jnp.zeros((HD, WIDTH), jnp.float32)

        def grad(offset, size, carry):
            offset = pl.multiple_of(offset, TILE)
            rows = pl.ds(pl.multiple_of(base + offset, BLOCK), size)
            at = pl.ds(offset, size)
            kt = keys[rows, :].T
            dk = dkeys[rows, :]
            dv = dvalues[rows, :]
            for p in range(PAIRS):
                cols = slice(p * PAIR, (p + 1) * PAIR)
                log_norm, row_dot = norms[p]
                prob = jnp.exp2(scores[at, cols] - log_norm)
                ds = prob * (probs[at, cols] - row_dot)
                prob = prob.astype(jnp.bfloat16)
                ds = ds.astype(jnp.bfloat16)
                dv = dv + jnp.dot(prob, gs[cols, :], preferred_element_type=jnp.float32)
                dk = dk + jnp.dot(ds, qs[cols, :], preferred_element_type=jnp.float32)
                dqt[:, cols] += jnp.dot(kt, ds, preferred_element_type=jnp.float32)
            dkeys[rows, :] = dk
            dvalues[rows, :] = dv
            return carry

        sweep(grad, 0)
        for k, dq in enumerate(dqs):
            @pl.when(i == k)
            def _(dq=dq):
                for g in range(GROUP):
                    cols = slice(g * HD, (g + 1) * HD)
                    dq[:, cols] = (dqt[:, cols].T * INV_ROOT).astype(dq.dtype)
        return carry

    lax.fori_loop(0, len(distances), block, 0)


def first_kernel(distances, plan, lengths, *refs):
    place = here()
    n = len(distances)
    qds, refs = refs[:n], refs[n:]
    sources, refs = (refs[:NY], refs[NY:2 * NY]), refs[2 * NY:]
    dqs, refs = refs[:n], refs[n:]
    keys, values, dkeys, dvalues = refs[:4]
    z, y, c = place
    for core_rel in range(2):
        for y_rel in range(NY):
            for z_rel in range(NZ):
                chip = ((z - z_rel) & (NZ - 1)) * NY + ((y - y_rel) & (NY - 1))
                slot = chip * 2 + (c ^ core_rel)
                rows = pl.ds(pl.multiple_of(slot * BLOCK, BLOCK), BLOCK)
                keys[rows, :] = sources[core_rel][y_rel][z_rel, :, :HD]
                values[rows, :] = sources[core_rel][y_rel][z_rel, :, HD:]

    def clear(t, carry):
        rows = pl.ds(pl.multiple_of(t * TILE, TILE), TILE)
        dkeys[rows, :] = jnp.zeros((TILE, HD), jnp.float32)
        dvalues[rows, :] = jnp.zeros((TILE, HD), jnp.float32)
        return carry

    lax.fori_loop(0, SEQ // TILE, clear, 0)
    attend(place, plan, lengths, distances, qds, dqs, *refs)


def last_kernel(distances, plan, lengths, *refs):
    place = here()
    n = len(distances)
    qds, refs = refs[:n], refs[n:]
    (keys, values, dkeys_in, dvalues_in), refs = refs[:4], refs[4:]
    dqs, (keep, give, dkeys, dvalues), refs = refs[:n], refs[n:n + 4], refs[n + 4:]

    def load(t, carry):
        rows = pl.ds(pl.multiple_of(t * TILE, TILE), TILE)
        dkeys[rows, :] = dkeys_in[rows, :]
        dvalues[rows, :] = dvalues_in[rows, :]
        return carry

    lax.fori_loop(0, SEQ // TILE, load, 0)
    attend(place, plan, lengths, distances, qds, dqs, keys, values, dkeys, dvalues, *refs)
    for core_rel, chip, rows in slots(place):
        out = (keep, give)[core_rel]
        out[chip, :, :HD] = (dkeys[rows, :] * INV_ROOT).astype(out.dtype)
        out[chip, :, HD:] = dvalues[rows, :].astype(out.dtype)


def work_arrays():
    return [
        pltpu.VMEM((MAXTILES * TILE, WIDTH), jnp.float32),
        pltpu.VMEM((MAXTILES * TILE, WIDTH), jnp.float32),
        pltpu.VMEM((WIDTH, HD), jnp.bfloat16),
        pltpu.VMEM((HD, WIDTH), jnp.bfloat16),
        pltpu.VMEM((WIDTH, HD), jnp.bfloat16),
        pltpu.VMEM((HD, WIDTH), jnp.bfloat16),
        pltpu.VMEM((HD, WIDTH), jnp.float32),
    ]


def attend_first(plan, lengths, distances, qds, own, other):
    n = len(distances)
    *dqs, keys, values, dkeys, dvalues = pl.pallas_call(
        functools.partial(first_kernel, distances),
        out_shape=[jax.ShapeDtypeStruct((BLOCK, WIDTH), jnp.bfloat16)] * n
        + [jax.ShapeDtypeStruct((SEQ, HD), jnp.bfloat16)] * 2
        + [jax.ShapeDtypeStruct((SEQ, HD), jnp.float32)] * 2,
        in_specs=[SMEM] * 2 + [VMEM] * (n + 2 * NY),
        out_specs=[VMEM] * (n + 4),
        scratch_shapes=work_arrays(),
        compiler_params=pltpu.CompilerParams(vmem_limit_bytes=VMEM_BYTES),
        cost_estimate=cost(n * BLOCK_FLOPS, 8 * 2**20),
        name="attention_first",
    )(plan, lengths, *qds, *own, *other)
    return dqs, (keys, values, dkeys, dvalues)


def attend_last(plan, lengths, distances, qds, state):
    n = len(distances)
    return pl.pallas_call(
        functools.partial(last_kernel, distances),
        out_shape=[jax.ShapeDtypeStruct((BLOCK, WIDTH), jnp.bfloat16)] * n
        + [jax.ShapeDtypeStruct((NZ * NY, BLOCK, 2 * HD), jnp.bfloat16)] * 2,
        in_specs=[SMEM] * 2 + [VMEM] * (n + 4),
        out_specs=[VMEM] * (n + 2),
        scratch_shapes=[pltpu.VMEM((SEQ, HD), jnp.float32)] * 2 + work_arrays(),
        compiler_params=pltpu.CompilerParams(vmem_limit_bytes=VMEM_BYTES),
        cost_estimate=cost(n * BLOCK_FLOPS, 8 * 2**20),
        name="attention_last",
    )(plan, lengths, *qds, *state)


def shards(queries, keys, values, grad_out, lengths, plan):
    with jax.named_scope("spread_keys"):
        kv = pack(keys, values)
        row = [kv[0]] + [send(kv[d], d, 0, 0) for d in (1, 2, 3)]
        qd = pack(queries, grad_out)
        row, qd = lax.optimization_barrier((row, qd))
        row = jnp.stack(row)
        own = [row] + [send(row, 0, d, 0) for d in (1, 2, 3)]
        other = [send(part, 0, 0, 1) for part in own]
    with jax.named_scope("spread_queries"):
        near = [send(qd[d], d, 0, 0) for d in (1, 3)]
        late, near = lax.optimization_barrier((qd[2], near))
        far = send(late, 2, 0, 0)

    with jax.named_scope("attention"):
        (dq0, dq1, dq3), state = attend_first(
            plan, lengths, (0, 1, 3), (qd[0], *near), own, other
        )
        dq2, keep, give = attend_last(plan, lengths, (2,), (far,), state)

    with jax.named_scope("return_queries"):
        back1, back3 = send(dq1, -1, 0, 0), send(dq3, -3, 0, 0)
        give, back1, back3 = lax.optimization_barrier((give, back1, back3))
        grad_query = join_near(dq0, back1, back3)
        back2 = send(dq2, -2, 0, 0)

    with jax.named_scope("return_keys"):
        both = keep.astype(jnp.float32) + send(give, 0, 0, 1).astype(jnp.float32)
        both, grad_query = lax.optimization_barrier((both.astype(jnp.bfloat16), grad_query))
        partials = exchange(both)
        return tuple(finish(partials, back2, grad_query))


def solution(mesh):
    rows = P(("dp", "ctx"), None)
    return jax.shard_map(
        shards,
        mesh=mesh,
        in_specs=(rows, rows, rows, rows, P("dp"), P("dp")),
        out_specs=(rows, rows, rows),
        check_vma=False,
    )
```

```python
import functools
import math

import jax
import jax.numpy as jnp
from jax import lax
from jax.experimental import pallas as pl
from jax.experimental.pallas import tpu as pltpu
from jax.sharding import PartitionSpec as P

HD = 128
BLOCK = 128
DOCS = 8
KVH = 4
GROUP = 8
NZ = 4
NY = 4
SEQ = 4096
NBLK = 32
WIDTH = GROUP * HD
TILE = 256
MAXTILES = 9
SIZES = (2, 1)
PAIR = 256
PAIRS = WIDTH // PAIR
NEG = -1e30
INV_ROOT = 1.0 / math.sqrt(HD)
EXP_SCALE = INV_ROOT / math.log(2.0)


SMEM = pl.BlockSpec(memory_space=pltpu.SMEM)
VMEM = pl.BlockSpec(memory_space=pltpu.VMEM)
HBM = pl.BlockSpec(memory_space=pltpu.HBM)
SMALL_VMEM_BYTES = 12 * 1024 * 1024
PACK_VMEM_BYTES = 56 * 1024 * 1024
VMEM_BYTES = 40 * 1024 * 1024
BLOCK_FLOPS = 5 * 2 * WIDTH * 1024 * HD


def cost(flops, nbytes):
    return pl.CostEstimate(flops=flops, bytes_accessed=nbytes, transcendentals=0)


def ring(dz, dy, dc):
    return [
        ((z * NY + y) * 2 + c, ((z + dz) % NZ * NY + (y + dy) % NY) * 2 + (c ^ dc))
        for z in range(NZ)
        for y in range(NY)
        for c in range(2)
    ]


def send(x, dz, dy, dc):
    return lax.ppermute(x, "ctx", ring(dz, dy, dc))


def at_head(place, d, width):
    return pl.ds(pl.multiple_of((place[0] + d + NZ) % NZ * width, width), width)


def here():
    me = lax.axis_index("ctx")
    return lax.shift_right_logical(me, 3), lax.shift_right_logical(me, 1) & 3, me & 1


def pack_kernel(width, left, right, *refs):
    outs, sems = refs[:NZ], refs[NZ]
    place = here()
    copies = []
    for d, out in enumerate(outs):
        for half, source in enumerate((left, right)):
            copies.append(pltpu.make_async_copy(
                source.at[:, at_head(place, d, width)],
                out.at[:, half * width:(half + 1) * width],
                sems.at[len(copies)],
            ))
            copies[-1].start()
    for copy in copies:
        copy.wait()


def pack(left, right, vmem_bytes):
    width = left.shape[1] // KVH
    return pl.pallas_call(
        functools.partial(pack_kernel, width),
        out_shape=[jax.ShapeDtypeStruct((BLOCK, 2 * width), left.dtype)] * NZ,
        in_specs=[HBM] * 2,
        out_specs=[VMEM] * NZ,
        scratch_shapes=[pltpu.SemaphoreType.DMA((2 * NZ,))],
        compiler_params=pltpu.CompilerParams(vmem_limit_bytes=vmem_bytes),
        cost_estimate=cost(0, 4 * left.size * 2),
        name="pack",
    )(left, right)


def put_heads(place, parts, out, wide, sems):
    copies = []
    for i, (d, part) in enumerate(parts):
        wide[i] = part[...].astype(wide.dtype)
        copies.append(
            pltpu.make_async_copy(wide.at[i], out.at[:, at_head(place, d, WIDTH)], sems.at[i])
        )
        copies[-1].start()
    return copies


def join_early_kernel(dq0, dq1, dq2, out, wide, sems):
    for copy in put_heads(here(), ((0, dq0), (1, dq1), (2, dq2)), out, wide, sems):
        copy.wait()


def join_early(dq0, dq1, dq2):
    return pl.pallas_call(
        join_early_kernel,
        out_shape=jax.ShapeDtypeStruct((BLOCK, KVH * WIDTH), jnp.float32),
        in_specs=[VMEM] * 3,
        out_specs=HBM,
        scratch_shapes=[
            pltpu.VMEM((3, BLOCK, WIDTH), jnp.float32),
            pltpu.SemaphoreType.DMA((3,)),
        ],
        compiler_params=pltpu.CompilerParams(vmem_limit_bytes=SMALL_VMEM_BYTES),
        cost_estimate=cost(0, BLOCK * KVH * WIDTH * 6),
        name="join_early",
    )(dq0, dq1, dq2)


def finish_kernel(part0, part1, part2, part3, dq3, grad_in, out, dk, dv, wide, sems):
    place = here()
    copies = put_heads(place, ((3, dq3),), out, wide, sems)
    for d, part in enumerate((part0, part1, part2, part3)):
        dk[:, at_head(place, -d, HD)] = part[:, :HD].astype(dk.dtype)
        dv[:, at_head(place, -d, HD)] = part[:, HD:].astype(dv.dtype)
    for copy in copies:
        copy.wait()


def finish(parts, dq3, grad_query):
    return pl.pallas_call(
        finish_kernel,
        out_shape=[jax.ShapeDtypeStruct((BLOCK, KVH * WIDTH), jnp.float32)]
        + [jax.ShapeDtypeStruct((BLOCK, KVH * HD), jnp.float32)] * 2,
        in_specs=[VMEM] * (NZ + 1) + [HBM],
        out_specs=[HBM, VMEM, VMEM],
        input_output_aliases={NZ + 1: 0},
        scratch_shapes=[
            pltpu.VMEM((1, BLOCK, WIDTH), jnp.float32),
            pltpu.SemaphoreType.DMA((1,)),
        ],
        compiler_params=pltpu.CompilerParams(vmem_limit_bytes=SMALL_VMEM_BYTES),
        cost_estimate=cost(0, 4 * 2**20),
        name="finish",
    )(*parts, dq3, grad_query)


def slots(place, sign):
    z, y, c = place
    for core_rel in range(2):
        for y_rel in range(NY):
            for z_rel in range(NZ):
                chip = ((z + sign * z_rel) & (NZ - 1)) * NY + ((y + sign * y_rel) & (NY - 1))
                slot = chip * 2 + (c ^ core_rel)
                yield core_rel, y_rel, z_rel, pl.ds(pl.multiple_of(slot * BLOCK, BLOCK), BLOCK)


def attend(
    place, plan, lengths, distances, qds, dqs,
    keys, values, dkeys, dvalues, scores, probs, qs, qst, gs, gst, dqt,
):
    z, y, c = place[0], place[1], place[2]

    def block(i, carry):
        d = jnp.int32(distances[0])
        for k, qd in enumerate(qds):
            d = jnp.where(i == k, distances[k], d)

            @pl.when(i == k)
            def _(qd=qd):
                for g in range(GROUP):
                    rows = slice(g * BLOCK, (g + 1) * BLOCK)
                    q = qd[:, g * HD:(g + 1) * HD]
                    o = qd[:, WIDTH + g * HD:WIDTH + (g + 1) * HD]
                    qs[rows, :] = q
                    gs[rows, :] = o
                    qst[:, rows] = q.T
                    gst[:, rows] = o.T

        first = plan[((z - d + NZ) % NZ * NY + y) * 2 + c] * BLOCK
        pos = first + lax.broadcasted_iota(jnp.int32, (1, BLOCK), 1)
        start = jnp.zeros((1, BLOCK), jnp.int32)
        low = jnp.int32(0)
        end = jnp.int32(0)
        for e in range(DOCS):
            end = end + lengths[e]
            start = jnp.where(end <= pos, end, start)
            low = jnp.where(end <= first, end, low)
        tiles = (first + BLOCK - low // BLOCK * BLOCK + TILE - 1) // TILE
        base = jnp.maximum(first + BLOCK - tiles * TILE, 0)

        def sweep(body, state):
            done = jnp.int32(0)
            for size in SIZES:
                count = (tiles - done) // size
                state = lax.fori_loop(
                    0,
                    count,
                    lambda t, state, done=done, size=size: body(
                        (done + t * size) * TILE, size * TILE, state
                    ),
                    state,
                )
                done = done + count * size
            return state

        def stat(offset, size, state):
            offset = pl.multiple_of(offset, TILE)
            rows = pl.ds(pl.multiple_of(base + offset, BLOCK), size)
            key_pos = base + offset + lax.broadcasted_iota(jnp.int32, (size, BLOCK), 0)
            allowed = (key_pos >= start) & (key_pos <= pos)
            allowed = jnp.concatenate([allowed] * (PAIR // BLOCK), axis=1)
            k, v = keys[rows, :], values[rows, :]
            result = []

            def fold(x, op):
                x = x.reshape(-1, 8, PAIR)
                out = x[0]
                for i in range(1, x.shape[0]):
                    out = op(out, x[i])
                return out

            def dots(p):
                cols = slice(p * PAIR, (p + 1) * PAIR)
                high = None
                for r in range(0, size, TILE):
                    at = pl.ds(offset + r, TILE)
                    s = jnp.dot(k[r:r + TILE], qst[:, cols], preferred_element_type=jnp.float32)
                    s = jnp.where(allowed[r:r + TILE], s * EXP_SCALE, NEG)
                    scores[at, cols] = s
                    here_high = fold(s, jnp.maximum)
                    high = here_high if high is None else jnp.maximum(high, here_high)
                    probs[at, cols] = jnp.dot(v[r:r + TILE], gst[:, cols], preferred_element_type=jnp.float32)
                return high

            def sums(p, high):
                cols = slice(p * PAIR, (p + 1) * PAIR)
                top, total, dot = state[p]
                new_top = jnp.maximum(top, jnp.max(high, axis=0, keepdims=True))
                factor = jnp.exp2(top - new_top)
                add, mul = jnp.zeros((8, PAIR), jnp.float32), jnp.zeros((8, PAIR), jnp.float32)
                for r in range(0, size, TILE):
                    at = pl.ds(offset + r, TILE)
                    e = jnp.exp2(scores[at, cols] - new_top)
                    add = add + fold(e, jnp.add)
                    mul = mul + fold(e * probs[at, cols], jnp.add)
                result.append((
                    new_top,
                    total * factor + jnp.sum(add, axis=0, keepdims=True),
                    dot * factor + jnp.sum(mul, axis=0, keepdims=True),
                ))

            ahead = [dots(p) for p in range(1)]
            for p in range(PAIRS):
                if p + 1 < PAIRS:
                    ahead.append(dots(p + 1))
                sums(p, ahead[p])
            return tuple(result)

        zero = jnp.zeros((1, PAIR), jnp.float32)
        state = sweep(stat, ((jnp.full((1, PAIR), NEG, jnp.float32), zero, zero),) * PAIRS)
        norms = [(top + jnp.log2(total), dot / total) for top, total, dot in state]
        dqt[...] = jnp.zeros((HD, WIDTH), jnp.float32)

        def grad(offset, size, carry):
            offset = pl.multiple_of(offset, TILE)
            rows = pl.ds(pl.multiple_of(base + offset, BLOCK), size)
            at = pl.ds(offset, size)
            kt = keys[rows, :].T
            dk = dkeys[rows, :]
            dv = dvalues[rows, :]
            for p in range(PAIRS):
                cols = slice(p * PAIR, (p + 1) * PAIR)
                log_norm, row_dot = norms[p]
                prob = jnp.exp2(scores[at, cols] - log_norm)
                ds = prob * (probs[at, cols] - row_dot)
                prob = prob.astype(jnp.bfloat16)
                ds = ds.astype(jnp.bfloat16)
                dv = dv + jnp.dot(prob, gs[cols, :], preferred_element_type=jnp.float32)
                dk = dk + jnp.dot(ds, qs[cols, :], preferred_element_type=jnp.float32)
                dqt[:, cols] += jnp.dot(kt, ds, preferred_element_type=jnp.float32)
            dkeys[rows, :] = dk
            dvalues[rows, :] = dv
            return carry

        sweep(grad, 0)
        for k, dq in enumerate(dqs):
            @pl.when(i == k)
            def _(dq=dq):
                for g in range(GROUP):
                    cols = slice(g * HD, (g + 1) * HD)
                    dq[:, cols] = (dqt[:, cols].T * INV_ROOT).astype(dq.dtype)
        return carry

    lax.fori_loop(0, len(distances), block, 0)


def first_kernel(distances, plan, lengths, *refs):
    place = here()
    n = len(distances)
    qds, refs = refs[:n], refs[n:]
    sources, refs = (refs[:NY], refs[NY:2 * NY]), refs[2 * NY:]
    dqs, refs = refs[:n], refs[n:]
    keys, values, dkeys, dvalues = refs[:4]
    for core_rel, y_rel, z_rel, rows in slots(place, -1):
        keys[rows, :] = sources[core_rel][y_rel][z_rel, :, :HD]
        values[rows, :] = sources[core_rel][y_rel][z_rel, :, HD:]

    def clear(t, carry):
        rows = pl.ds(pl.multiple_of(t * TILE, TILE), TILE)
        dkeys[rows, :] = jnp.zeros((TILE, HD), jnp.float32)
        dvalues[rows, :] = jnp.zeros((TILE, HD), jnp.float32)
        return carry

    lax.fori_loop(0, SEQ // TILE, clear, 0)
    attend(place, plan, lengths, distances, qds, dqs, *refs)


def last_kernel(distances, plan, lengths, *refs):
    place = here()
    n = len(distances)
    qds, refs = refs[:n], refs[n:]
    (keys, values, dkeys_in, dvalues_in), refs = refs[:4], refs[4:]
    dqs, (keep, give, dkeys, dvalues), refs = refs[:n], refs[n:n + 4], refs[n + 4:]

    def load(t, carry):
        rows = pl.ds(pl.multiple_of(t * TILE, TILE), TILE)
        dkeys[rows, :] = dkeys_in[rows, :]
        dvalues[rows, :] = dvalues_in[rows, :]
        return carry

    lax.fori_loop(0, SEQ // TILE, load, 0)
    attend(place, plan, lengths, distances, qds, dqs, keys, values, dkeys, dvalues, *refs)
    for core_rel, y_rel, z_rel, rows in slots(place, 1):
        out = (keep, give)[core_rel]
        out[y_rel, z_rel, :, :HD] = (dkeys[rows, :] * INV_ROOT).astype(out.dtype)
        out[y_rel, z_rel, :, HD:] = dvalues[rows, :].astype(out.dtype)


def work_arrays():
    return [
        pltpu.VMEM((MAXTILES * TILE, WIDTH), jnp.float32),
        pltpu.VMEM((MAXTILES * TILE, WIDTH), jnp.float32),
        pltpu.VMEM((WIDTH, HD), jnp.bfloat16),
        pltpu.VMEM((HD, WIDTH), jnp.bfloat16),
        pltpu.VMEM((WIDTH, HD), jnp.bfloat16),
        pltpu.VMEM((HD, WIDTH), jnp.bfloat16),
        pltpu.VMEM((HD, WIDTH), jnp.float32),
    ]


def attend_first(plan, lengths, distances, qds, own, other):
    n = len(distances)
    *dqs, keys, values, dkeys, dvalues = pl.pallas_call(
        functools.partial(first_kernel, distances),
        out_shape=[jax.ShapeDtypeStruct((BLOCK, WIDTH), jnp.bfloat16)] * n
        + [jax.ShapeDtypeStruct((SEQ, HD), jnp.bfloat16)] * 2
        + [jax.ShapeDtypeStruct((SEQ, HD), jnp.float32)] * 2,
        in_specs=[SMEM] * 2 + [VMEM] * (n + 2 * NY),
        out_specs=[VMEM] * (n + 4),
        scratch_shapes=work_arrays(),
        compiler_params=pltpu.CompilerParams(vmem_limit_bytes=VMEM_BYTES),
        cost_estimate=cost(n * BLOCK_FLOPS, 8 * 2**20),
        name="attention_first",
    )(plan, lengths, *qds, *own, *other)
    return dqs, (keys, values, dkeys, dvalues)


def attend_last(plan, lengths, distances, qds, state):
    n = len(distances)
    return pl.pallas_call(
        functools.partial(last_kernel, distances),
        out_shape=[jax.ShapeDtypeStruct((BLOCK, WIDTH), jnp.bfloat16)] * n
        + [jax.ShapeDtypeStruct((NY, NZ, BLOCK, 2 * HD), jnp.bfloat16)] * 2,
        in_specs=[SMEM] * 2 + [VMEM] * (n + 4),
        out_specs=[VMEM] * (n + 2),
        scratch_shapes=[pltpu.VMEM((SEQ, HD), jnp.float32)] * 2 + work_arrays(),
        compiler_params=pltpu.CompilerParams(vmem_limit_bytes=VMEM_BYTES),
        cost_estimate=cost(n * BLOCK_FLOPS, 8 * 2**20),
        name="attention_last",
    )(plan, lengths, *qds, *state)


def shards(queries, keys, values, grad_out, lengths, plan):
    with jax.named_scope("spread_keys"):
        kv = pack(keys, values, PACK_VMEM_BYTES)
        row = [kv[0]] + [send(kv[d], d, 0, 0) for d in (1, 2, 3)]
        qd = pack(queries, grad_out, SMALL_VMEM_BYTES)
        row, qd = lax.optimization_barrier((row, qd))
        row = jnp.stack(row)
        own = [row] + [send(row, 0, d, 0) for d in (1, 2, 3)]
        other = [send(part, 0, 0, 1) for part in own]
    with jax.named_scope("spread_queries"):
        near = [send(qd[d], d, 0, 0) for d in (1, 3)]
        late, near = lax.optimization_barrier((qd[2], near))
        far = send(late, 2, 0, 0)

    with jax.named_scope("attention"):
        (dq0, dq1, dq3), state = attend_first(
            plan, lengths, (0, 1, 3), (qd[0], *near), own, other
        )
        dq2, keep, give = attend_last(plan, lengths, (2,), (far,), state)

    with jax.named_scope("return_keys"):
        both = keep.astype(jnp.float32) + send(give, 0, 0, 1).astype(jnp.float32)
        both = both.astype(jnp.bfloat16)
        back1, back2 = send(dq1, -1, 0, 0), send(dq2, -2, 0, 0)
        grad_query = join_early(dq0, back1, back2)
        parts = [send(both[d], 0, d, 0) for d in (1, 2, 3)]
        parts, dq3, grad_query = lax.optimization_barrier((parts, dq3, grad_query))
        back3 = send(dq3, -3, 0, 0)
        total = both[0].astype(jnp.float32)
        for part in parts:
            total = total + part.astype(jnp.float32)
        total = total.astype(jnp.bfloat16)
        heads = [total[0]] + [send(total[d], d, 0, 0) for d in (1, 2, 3)]
        return tuple(finish(heads, back3, grad_query))


def solution(mesh):
    rows = P(("dp", "ctx"), None)
    return jax.shard_map(
        shards,
        mesh=mesh,
        in_specs=(rows, rows, rows, rows, P("dp"), P("dp")),
        out_specs=(rows, rows, rows),
        check_vma=False,
    )
```

```python
import functools
import math

import jax
import jax.numpy as jnp
from jax import lax
from jax.experimental import pallas as pl
from jax.experimental.pallas import tpu as pltpu
from jax.sharding import PartitionSpec as P

HD = 128
BLOCK = 128
DOCS = 8
KVH = 4
GROUP = 8
NZ = 4
NY = 4
SEQ = 4096
NBLK = 32
WIDTH = GROUP * HD
TILE = 256
MAXTILES = 9
SIZES = (2, 1)
PAIR = 256
PAIRS = WIDTH // PAIR
NEG = -1e30
SMALL_SUM = 1e-6
LARGE_SUM = 1e30
INV_ROOT = 1.0 / math.sqrt(HD)
EXP_SCALE = INV_ROOT / math.log(2.0)


SMEM = pl.BlockSpec(memory_space=pltpu.SMEM)
VMEM = pl.BlockSpec(memory_space=pltpu.VMEM)
HBM = pl.BlockSpec(memory_space=pltpu.HBM)
SMALL_VMEM_BYTES = 12 * 1024 * 1024
PACK_VMEM_BYTES = 56 * 1024 * 1024
VMEM_BYTES = 40 * 1024 * 1024
BLOCK_FLOPS = 5 * 2 * WIDTH * 1024 * HD


def cost(flops, nbytes):
    return pl.CostEstimate(flops=flops, bytes_accessed=nbytes, transcendentals=0)


def ring(dz, dy, dc):
    return [
        ((z * NY + y) * 2 + c, ((z + dz) % NZ * NY + (y + dy) % NY) * 2 + (c ^ dc))
        for z in range(NZ)
        for y in range(NY)
        for c in range(2)
    ]


def send(x, dz, dy, dc):
    return lax.ppermute(x, "ctx", ring(dz, dy, dc))


def at_head(place, d, width):
    return pl.ds(pl.multiple_of((place[0] + d + NZ) % NZ * width, width), width)


def here():
    me = lax.axis_index("ctx")
    return lax.shift_right_logical(me, 3), lax.shift_right_logical(me, 1) & 3, me & 1


def pack_kernel(width, left, right, *refs):
    outs, sems = refs[:NZ], refs[NZ]
    place = here()
    copies = []
    for d, out in enumerate(outs):
        for half, source in enumerate((left, right)):
            copies.append(pltpu.make_async_copy(
                source.at[:, at_head(place, d, width)],
                out.at[:, half * width:(half + 1) * width],
                sems.at[len(copies)],
            ))
            copies[-1].start()
    for copy in copies:
        copy.wait()


def pack(left, right, space):
    width = left.shape[1] // KVH
    return pl.pallas_call(
        functools.partial(pack_kernel, width),
        out_shape=[jax.ShapeDtypeStruct((BLOCK, 2 * width), left.dtype)] * NZ,
        in_specs=[HBM] * 2,
        out_specs=[space] * NZ,
        scratch_shapes=[pltpu.SemaphoreType.DMA((2 * NZ,))],
        compiler_params=pltpu.CompilerParams(vmem_limit_bytes=PACK_VMEM_BYTES if space is HBM else SMALL_VMEM_BYTES),
        cost_estimate=cost(0, 4 * left.size * 2),
        name="pack",
    )(left, right)


def join_queries_kernel(dq0, dq1, dq2, dq3, out, wide, sems):
    place = here()
    copies = []
    for d, part in enumerate((dq0, dq1, dq2, dq3)):
        wide[d] = part[...].astype(wide.dtype)
        copies.append(
            pltpu.make_async_copy(wide.at[d], out.at[:, at_head(place, d, WIDTH)], sems.at[d])
        )
        copies[-1].start()
    for copy in copies:
        copy.wait()


def join_queries(parts):
    return pl.pallas_call(
        join_queries_kernel,
        out_shape=jax.ShapeDtypeStruct((BLOCK, KVH * WIDTH), jnp.float32),
        in_specs=[VMEM] * NZ,
        out_specs=HBM,
        scratch_shapes=[
            pltpu.VMEM((NZ, BLOCK, WIDTH), jnp.float32),
            pltpu.SemaphoreType.DMA((NZ,)),
        ],
        compiler_params=pltpu.CompilerParams(vmem_limit_bytes=SMALL_VMEM_BYTES),
        cost_estimate=cost(0, BLOCK * KVH * WIDTH * 6),
        name="join_queries",
    )(*parts)


def join_keys_kernel(part0, part1, part2, part3, dk, dv):
    place = here()
    for d, part in enumerate((part0, part1, part2, part3)):
        dk[:, at_head(place, -d, HD)] = part[:, :HD].astype(dk.dtype)
        dv[:, at_head(place, -d, HD)] = part[:, HD:].astype(dv.dtype)


def join_keys(parts):
    return pl.pallas_call(
        join_keys_kernel,
        out_shape=[jax.ShapeDtypeStruct((BLOCK, KVH * HD), jnp.float32)] * 2,
        in_specs=[VMEM] * NZ,
        out_specs=[VMEM] * 2,
        compiler_params=pltpu.CompilerParams(vmem_limit_bytes=SMALL_VMEM_BYTES),
        cost_estimate=cost(0, BLOCK * KVH * HD * 12),
        name="join_keys",
    )(*parts)


def slots(place, sign):
    z, y, c = place
    for core_rel in range(2):
        for y_rel in range(NY):
            for z_rel in range(NZ):
                chip = ((z + sign * z_rel) & (NZ - 1)) * NY + ((y + sign * y_rel) & (NY - 1))
                slot = chip * 2 + (c ^ core_rel)
                yield core_rel, y_rel, z_rel, pl.ds(pl.multiple_of(slot * BLOCK, BLOCK), BLOCK)


def attend(
    place, plan, lengths, distances, qds, dqs,
    keys, values, dkeys, dvalues, scores, probs, qs, qst, gs, gst, dqt, norms,
):
    z, y, c = place[0], place[1], place[2]

    def block(i, carry):
        d = jnp.int32(distances[0])
        for k, qd in enumerate(qds):
            d = jnp.where(i == k, distances[k], d)

            @pl.when(i == k)
            def _(qd=qd):
                for g in range(GROUP):
                    rows = slice(g * BLOCK, (g + 1) * BLOCK)
                    q = qd[:, g * HD:(g + 1) * HD]
                    o = qd[:, WIDTH + g * HD:WIDTH + (g + 1) * HD]
                    qs[rows, :] = q
                    gs[rows, :] = o
                    qst[:, rows] = q.T
                    gst[:, rows] = o.T

        first = plan[((z - d + NZ) % NZ * NY + y) * 2 + c] * BLOCK
        pos = first + lax.broadcasted_iota(jnp.int32, (1, BLOCK), 1)
        start = jnp.zeros((1, BLOCK), jnp.int32)
        low = jnp.int32(0)
        end = jnp.int32(0)
        for e in range(DOCS):
            end = end + lengths[e]
            start = jnp.where(end <= pos, end, start)
            low = jnp.where(end <= first, end, low)
        tiles = (first + BLOCK - low // BLOCK * BLOCK + TILE - 1) // TILE
        base = jnp.maximum(first + BLOCK - tiles * TILE, 0)

        def sweep(body, state):
            done = jnp.int32(0)
            for size in SIZES:
                count = (tiles - done) // size
                state = lax.fori_loop(
                    0,
                    count,
                    lambda t, state, done=done, size=size: body(
                        (done + t * size) * TILE, size * TILE, state
                    ),
                    state,
                )
                done = done + count * size
            return state

        def mask(offset, size):
            key_pos = base + offset + lax.broadcasted_iota(jnp.int32, (size, BLOCK), 0)
            allowed = (key_pos >= start) & (key_pos <= pos)
            return jnp.concatenate([allowed] * (PAIR // BLOCK), axis=1)

        def stat(offset, size, state):
            offset = pl.multiple_of(offset, TILE)
            rows = pl.ds(pl.multiple_of(base + offset, BLOCK), size)
            at = pl.ds(offset, size)
            allowed = mask(offset, size)
            k, v = keys[rows, :], values[rows, :]
            result = []
            for p in range(PAIRS):
                cols = slice(p * PAIR, (p + 1) * PAIR)
                total, dot = state[p]
                s = jnp.dot(k, qst[:, cols], preferred_element_type=jnp.float32)
                e = jnp.exp2(jnp.where(allowed, s * EXP_SCALE, NEG))
                scores[at, cols] = e
                g = jnp.dot(v, gst[:, cols], preferred_element_type=jnp.float32)
                probs[at, cols] = g
                result.append((
                    total + jnp.sum(e, axis=0, keepdims=True),
                    dot + jnp.sum(e * g, axis=0, keepdims=True),
                ))
            return tuple(result)

        zero = jnp.zeros((1, PAIR), jnp.float32)
        state = sweep(stat, ((zero, zero),) * PAIRS)
        far_off = jnp.zeros((1, PAIR), jnp.float32)
        for p, (total, dot) in enumerate(state):
            cols = slice(p * PAIR, (p + 1) * PAIR)
            norms[0:1, cols] = 1.0 / total
            norms[1:2, cols] = dot / total
            fine = (total > SMALL_SUM) & (total < LARGE_SUM) & (jnp.abs(dot) < LARGE_SUM)
            far_off = jnp.where(fine, far_off, 1.0)

        @pl.when(jnp.max(far_off) > 0.0)
        def _():
            def stat_shifted(t, state):
                offset = pl.multiple_of(t * TILE, TILE)
                rows = pl.ds(pl.multiple_of(base + offset, BLOCK), TILE)
                at = pl.ds(offset, TILE)
                allowed = mask(offset, TILE)
                k = keys[rows, :]
                result = []
                for p in range(PAIRS):
                    cols = slice(p * PAIR, (p + 1) * PAIR)
                    top, total, dot = state[p]
                    s = jnp.dot(k, qst[:, cols], preferred_element_type=jnp.float32)
                    s = jnp.where(allowed, s * EXP_SCALE, NEG)
                    scores[at, cols] = s
                    new_top = jnp.maximum(top, jnp.max(s, axis=0, keepdims=True))
                    factor = jnp.exp2(top - new_top)
                    e = jnp.exp2(s - new_top)
                    result.append((
                        new_top,
                        total * factor + jnp.sum(e, axis=0, keepdims=True),
                        dot * factor + jnp.sum(e * probs[at, cols], axis=0, keepdims=True),
                    ))
                return tuple(result)

            lowest = jnp.full((1, PAIR), NEG, jnp.float32)
            state = lax.fori_loop(0, tiles, stat_shifted, ((lowest, zero, zero),) * PAIRS)
            for p, (top, total, dot) in enumerate(state):
                cols = slice(p * PAIR, (p + 1) * PAIR)
                norms[0:1, cols] = jnp.ones((1, PAIR), jnp.float32)
                norms[1:2, cols] = dot / total
                norms[2:3, cols] = top + jnp.log2(total)

            def normalise(t, carry):
                at = pl.ds(pl.multiple_of(t * TILE, TILE), TILE)
                for p in range(PAIRS):
                    cols = slice(p * PAIR, (p + 1) * PAIR)
                    scores[at, cols] = jnp.exp2(scores[at, cols] - norms[2:3, cols])
                return carry

            lax.fori_loop(0, tiles, normalise, 0)

        dqt[...] = jnp.zeros((HD, WIDTH), jnp.float32)

        def grad(offset, size, carry):
            offset = pl.multiple_of(offset, TILE)
            rows = pl.ds(pl.multiple_of(base + offset, BLOCK), size)
            at = pl.ds(offset, size)
            kt = keys[rows, :].T
            dk = dkeys[rows, :]
            dv = dvalues[rows, :]
            for p in range(PAIRS):
                cols = slice(p * PAIR, (p + 1) * PAIR)
                prob = scores[at, cols] * norms[0:1, cols]
                ds = prob * (probs[at, cols] - norms[1:2, cols])
                prob = prob.astype(jnp.bfloat16)
                ds = ds.astype(jnp.bfloat16)
                dv = dv + jnp.dot(prob, gs[cols, :], preferred_element_type=jnp.float32)
                dk = dk + jnp.dot(ds, qs[cols, :], preferred_element_type=jnp.float32)
                dqt[:, cols] += jnp.dot(kt, ds, preferred_element_type=jnp.float32)
            dkeys[rows, :] = dk
            dvalues[rows, :] = dv
            return carry

        sweep(grad, 0)
        for k, dq in enumerate(dqs):
            @pl.when(i == k)
            def _(dq=dq):
                for g in range(GROUP):
                    cols = slice(g * HD, (g + 1) * HD)
                    dq[:, cols] = (dqt[:, cols].T * INV_ROOT).astype(dq.dtype)
        return carry

    lax.fori_loop(0, len(distances), block, 0)


def first_kernel(distances, plan, lengths, *refs):
    place = here()
    n = len(distances)
    qds, refs = refs[:n], refs[n:]
    sources, refs = (refs[:NY], refs[NY:2 * NY]), refs[2 * NY:]
    dqs, refs = refs[:n], refs[n:]
    keys, values, dkeys, dvalues = refs[:4]
    for core_rel, y_rel, z_rel, rows in slots(place, -1):
        keys[rows, :] = sources[core_rel][y_rel][z_rel, :, :HD]
        values[rows, :] = sources[core_rel][y_rel][z_rel, :, HD:]

    def clear(t, carry):
        rows = pl.ds(pl.multiple_of(t * TILE, TILE), TILE)
        dkeys[rows, :] = jnp.zeros((TILE, HD), jnp.float32)
        dvalues[rows, :] = jnp.zeros((TILE, HD), jnp.float32)
        return carry

    lax.fori_loop(0, SEQ // TILE, clear, 0)
    attend(place, plan, lengths, distances, qds, dqs, *refs)


def last_kernel(distances, plan, lengths, *refs):
    place = here()
    n = len(distances)
    qds, refs = refs[:n], refs[n:]
    (keys, values, dkeys_in, dvalues_in), refs = refs[:4], refs[4:]
    dqs, (keep, give, dkeys, dvalues), refs = refs[:n], refs[n:n + 4], refs[n + 4:]

    def load(t, carry):
        rows = pl.ds(pl.multiple_of(t * TILE, TILE), TILE)
        dkeys[rows, :] = dkeys_in[rows, :]
        dvalues[rows, :] = dvalues_in[rows, :]
        return carry

    lax.fori_loop(0, SEQ // TILE, load, 0)
    attend(place, plan, lengths, distances, qds, dqs, keys, values, dkeys, dvalues, *refs)
    for core_rel, y_rel, z_rel, rows in slots(place, 1):
        out = (keep, give)[core_rel]
        out[y_rel, z_rel, :, :HD] = (dkeys[rows, :] * INV_ROOT).astype(out.dtype)
        out[y_rel, z_rel, :, HD:] = dvalues[rows, :].astype(out.dtype)


def work_arrays():
    return [
        pltpu.VMEM((MAXTILES * TILE, WIDTH), jnp.float32),
        pltpu.VMEM((MAXTILES * TILE, WIDTH), jnp.float32),
        pltpu.VMEM((WIDTH, HD), jnp.bfloat16),
        pltpu.VMEM((HD, WIDTH), jnp.bfloat16),
        pltpu.VMEM((WIDTH, HD), jnp.bfloat16),
        pltpu.VMEM((HD, WIDTH), jnp.bfloat16),
        pltpu.VMEM((HD, WIDTH), jnp.float32),
        pltpu.VMEM((8, WIDTH), jnp.float32),
    ]


def attend_first(plan, lengths, distances, qds, own, other):
    n = len(distances)
    *dqs, keys, values, dkeys, dvalues = pl.pallas_call(
        functools.partial(first_kernel, distances),
        out_shape=[jax.ShapeDtypeStruct((BLOCK, WIDTH), jnp.bfloat16)] * n
        + [jax.ShapeDtypeStruct((SEQ, HD), jnp.bfloat16)] * 2
        + [jax.ShapeDtypeStruct((SEQ, HD), jnp.float32)] * 2,
        in_specs=[SMEM] * 2 + [VMEM] * (n + 2 * NY),
        out_specs=[VMEM] * (n + 4),
        scratch_shapes=work_arrays(),
        compiler_params=pltpu.CompilerParams(vmem_limit_bytes=VMEM_BYTES),
        cost_estimate=cost(n * BLOCK_FLOPS, 8 * 2**20),
        name="attention_first",
    )(plan, lengths, *qds, *own, *other)
    return dqs, (keys, values, dkeys, dvalues)


def attend_last(plan, lengths, distances, qds, state):
    n = len(distances)
    return pl.pallas_call(
        functools.partial(last_kernel, distances),
        out_shape=[jax.ShapeDtypeStruct((BLOCK, WIDTH), jnp.bfloat16)] * n
        + [jax.ShapeDtypeStruct((NY, NZ, BLOCK, 2 * HD), jnp.bfloat16)] * 2,
        in_specs=[SMEM] * 2 + [VMEM] * (n + 4),
        out_specs=[VMEM] * (n + 2),
        scratch_shapes=[pltpu.VMEM((SEQ, HD), jnp.float32)] * 2 + work_arrays(),
        compiler_params=pltpu.CompilerParams(vmem_limit_bytes=VMEM_BYTES),
        cost_estimate=cost(n * BLOCK_FLOPS, 8 * 2**20),
        name="attention_last",
    )(plan, lengths, *qds, *state)


def shards(queries, keys, values, grad_out, lengths, plan):
    with jax.named_scope("spread_keys"):
        kv = pack(keys, values, HBM)
        row = [kv[0]] + [send(kv[d], d, 0, 0) for d in (1, 2, 3)]
        qd = pack(queries, grad_out, VMEM)
        row, qd = lax.optimization_barrier((row, qd))
        row = jnp.stack(row)
        own = [row] + [send(row, 0, d, 0) for d in (1, 2, 3)]
        other = [send(part, 0, 0, 1) for part in own]
    with jax.named_scope("spread_queries"):
        near = [send(qd[d], d, 0, 0) for d in (1, 3)]
        late, near = lax.optimization_barrier((qd[2], near))
        far = send(late, 2, 0, 0)

    with jax.named_scope("attention"):
        (dq0, dq1, dq3), state = attend_first(
            plan, lengths, (0, 1, 3), (qd[0], *near), own, other
        )
        dq2, keep, give = attend_last(plan, lengths, (2,), (far,), state)

    with jax.named_scope("return_keys"):
        both = keep.astype(jnp.float32) + send(give, 0, 0, 1).astype(jnp.float32)
        both = both.astype(jnp.bfloat16)
        back1, back2 = send(dq1, -1, 0, 0), send(dq2, -2, 0, 0)
        parts = [send(both[d], 0, d, 0) for d in (1, 2, 3)]
        dq3, parts[0] = lax.optimization_barrier((dq3, parts[0]))
        back3 = send(dq3, -3, 0, 0)
        total = both[0].astype(jnp.float32)
        for part in parts:
            total = total + part.astype(jnp.float32)
        total, back1, back2 = lax.optimization_barrier((total.astype(jnp.bfloat16), back1, back2))
        heads = [total[0]] + [send(total[d], d, 0, 0) for d in (1, 2, 3)]
        grad_query = join_queries((dq0, back1, back2, back3))
        heads, grad_query = lax.optimization_barrier((heads, grad_query))
        return (grad_query, *join_keys(heads))


def solution(mesh):
    rows = P(("dp", "ctx"), None)
    return jax.shard_map(
        shards,
        mesh=mesh,
        in_specs=(rows, rows, rows, rows, P("dp"), P("dp")),
        out_specs=(rows, rows, rows),
        check_vma=False,
    )
```

```python
import functools
import math

import jax
import jax.numpy as jnp
from jax import lax
from jax.experimental import pallas as pl
from jax.experimental.pallas import tpu as pltpu
from jax.sharding import PartitionSpec as P

HD = 128
BLOCK = 128
DOCS = 8
KVH = 4
GROUP = 8
NZ = 4
NY = 4
SEQ = 4096
NBLK = 32
WIDTH = GROUP * HD
TILE = 256
MAXTILES = 9
SIZES = (2, 1)
PAIR = 256
PAIRS = WIDTH // PAIR
NEG = -1e30
SMALL_SUM = 1e-6
LARGE_SUM = 1e30
INV_ROOT = 1.0 / math.sqrt(HD)
EXP_SCALE = INV_ROOT / math.log(2.0)


SMEM = pl.BlockSpec(memory_space=pltpu.SMEM)
VMEM = pl.BlockSpec(memory_space=pltpu.VMEM)
HBM = pl.BlockSpec(memory_space=pltpu.HBM)
SMALL_VMEM_BYTES = 12 * 1024 * 1024
VMEM_BYTES = 40 * 1024 * 1024
BLOCK_FLOPS = 5 * 2 * WIDTH * 1024 * HD


def cost(flops, nbytes):
    return pl.CostEstimate(flops=flops, bytes_accessed=nbytes, transcendentals=0)


def ring(dz, dy, dc):
    return [
        ((z * NY + y) * 2 + c, ((z + dz) % NZ * NY + (y + dy) % NY) * 2 + (c ^ dc))
        for z in range(NZ)
        for y in range(NY)
        for c in range(2)
    ]


def send(x, dz, dy, dc):
    return lax.ppermute(x, "ctx", ring(dz, dy, dc))


def at_head(place, d, width):
    return pl.ds(pl.multiple_of((place[0] + d + NZ) % NZ * width, width), width)


def here():
    me = lax.axis_index("ctx")
    return lax.shift_right_logical(me, 3), lax.shift_right_logical(me, 1) & 3, me & 1


def pack_kernel(width, left, right, *refs):
    outs, sems = refs[:NZ], refs[NZ]
    place = here()
    copies = []
    for d, out in enumerate(outs):
        for half, source in enumerate((left, right)):
            copies.append(pltpu.make_async_copy(
                source.at[:, at_head(place, d, width)],
                out.at[:, half * width:(half + 1) * width],
                sems.at[len(copies)],
            ))
            copies[-1].start()
    for copy in copies:
        copy.wait()


def pack(left, right):
    width = left.shape[1] // KVH
    return pl.pallas_call(
        functools.partial(pack_kernel, width),
        out_shape=[jax.ShapeDtypeStruct((BLOCK, 2 * width), left.dtype)] * NZ,
        in_specs=[HBM] * 2,
        out_specs=[VMEM] * NZ,
        scratch_shapes=[pltpu.SemaphoreType.DMA((2 * NZ,))],
        compiler_params=pltpu.CompilerParams(vmem_limit_bytes=SMALL_VMEM_BYTES),
        cost_estimate=cost(0, 4 * left.size * 2),
        name="pack",
    )(left, right)


def join_queries_kernel(dq0, dq1, dq2, dq3, out, wide, sems):
    place = here()
    copies = []
    for d, part in enumerate((dq0, dq1, dq2, dq3)):
        wide[d] = part[...].astype(wide.dtype)
        copies.append(
            pltpu.make_async_copy(wide.at[d], out.at[:, at_head(place, d, WIDTH)], sems.at[d])
        )
        copies[-1].start()
    for copy in copies:
        copy.wait()


def join_queries(parts):
    return pl.pallas_call(
        join_queries_kernel,
        out_shape=jax.ShapeDtypeStruct((BLOCK, KVH * WIDTH), jnp.float32),
        in_specs=[VMEM] * NZ,
        out_specs=HBM,
        scratch_shapes=[
            pltpu.VMEM((NZ, BLOCK, WIDTH), jnp.float32),
            pltpu.SemaphoreType.DMA((NZ,)),
        ],
        compiler_params=pltpu.CompilerParams(vmem_limit_bytes=SMALL_VMEM_BYTES),
        cost_estimate=cost(0, BLOCK * KVH * WIDTH * 6),
        name="join_queries",
    )(*parts)


def join_keys_kernel(part0, part1, part2, part3, dk, dv):
    place = here()
    for d, part in enumerate((part0, part1, part2, part3)):
        dk[:, at_head(place, -d, HD)] = part[:, :HD].astype(dk.dtype)
        dv[:, at_head(place, -d, HD)] = part[:, HD:].astype(dv.dtype)


def join_keys(parts):
    return pl.pallas_call(
        join_keys_kernel,
        out_shape=[jax.ShapeDtypeStruct((BLOCK, KVH * HD), jnp.float32)] * 2,
        in_specs=[VMEM] * NZ,
        out_specs=[VMEM] * 2,
        compiler_params=pltpu.CompilerParams(vmem_limit_bytes=SMALL_VMEM_BYTES),
        cost_estimate=cost(0, BLOCK * KVH * HD * 12),
        name="join_keys",
    )(*parts)


def slots(place, sign):
    z, y, c = place
    for core_rel in range(2):
        for y_rel in range(NY):
            for z_rel in range(NZ):
                chip = ((z + sign * z_rel) & (NZ - 1)) * NY + ((y + sign * y_rel) & (NY - 1))
                slot = chip * 2 + (c ^ core_rel)
                yield core_rel, y_rel, z_rel, pl.ds(pl.multiple_of(slot * BLOCK, BLOCK), BLOCK)


def attend(
    place, plan, lengths, distances, qds, dqs,
    keys, values, dkeys, dvalues, scores, probs, qs, qst, gs, gst, dqt, norms,
):
    z, y, c = place[0], place[1], place[2]

    def block(i, carry):
        d = jnp.int32(distances[0])
        for k, qd in enumerate(qds):
            d = jnp.where(i == k, distances[k], d)

            @pl.when(i == k)
            def _(qd=qd):
                for g in range(GROUP):
                    rows = slice(g * BLOCK, (g + 1) * BLOCK)
                    q = qd[:, g * HD:(g + 1) * HD]
                    o = qd[:, WIDTH + g * HD:WIDTH + (g + 1) * HD]
                    qs[rows, :] = q
                    gs[rows, :] = o
                    qst[:, rows] = q.T
                    gst[:, rows] = o.T

        first = plan[((z - d + NZ) % NZ * NY + y) * 2 + c] * BLOCK
        pos = first + lax.broadcasted_iota(jnp.int32, (1, BLOCK), 1)
        start = jnp.zeros((1, BLOCK), jnp.int32)
        low = jnp.int32(0)
        end = jnp.int32(0)
        for e in range(DOCS):
            end = end + lengths[e]
            start = jnp.where(end <= pos, end, start)
            low = jnp.where(end <= first, end, low)
        tiles = (first + BLOCK - low // BLOCK * BLOCK + TILE - 1) // TILE
        base = jnp.maximum(first + BLOCK - tiles * TILE, 0)

        def sweep(body, state):
            done = jnp.int32(0)
            for size in SIZES:
                count = (tiles - done) // size
                state = lax.fori_loop(
                    0,
                    count,
                    lambda t, state, done=done, size=size: body(
                        (done + t * size) * TILE, size * TILE, state
                    ),
                    state,
                )
                done = done + count * size
            return state

        def mask(offset, size):
            key_pos = base + offset + lax.broadcasted_iota(jnp.int32, (size, BLOCK), 0)
            allowed = (key_pos >= start) & (key_pos <= pos)
            return jnp.concatenate([allowed] * (PAIR // BLOCK), axis=1)

        def stat(offset, size, state):
            offset = pl.multiple_of(offset, TILE)
            rows = pl.ds(pl.multiple_of(base + offset, BLOCK), size)
            at = pl.ds(offset, size)
            allowed = mask(offset, size)
            k, v = keys[rows, :], values[rows, :]
            result = []
            for p in range(PAIRS):
                cols = slice(p * PAIR, (p + 1) * PAIR)
                total, dot = state[p]
                s = jnp.dot(k, qst[:, cols], preferred_element_type=jnp.float32)
                e = jnp.exp2(jnp.where(allowed, s * EXP_SCALE, NEG))
                scores[at, cols] = e
                g = jnp.dot(v, gst[:, cols], preferred_element_type=jnp.float32)
                probs[at, cols] = g
                result.append((
                    total + jnp.sum(e, axis=0, keepdims=True),
                    dot + jnp.sum(e * g, axis=0, keepdims=True),
                ))
            return tuple(result)

        zero = jnp.zeros((1, PAIR), jnp.float32)
        state = sweep(stat, ((zero, zero),) * PAIRS)
        far_off = jnp.zeros((1, PAIR), jnp.float32)
        for p, (total, dot) in enumerate(state):
            cols = slice(p * PAIR, (p + 1) * PAIR)
            norms[0:1, cols] = 1.0 / total
            norms[1:2, cols] = dot / total
            fine = (total > SMALL_SUM) & (total < LARGE_SUM) & (jnp.abs(dot) < LARGE_SUM)
            far_off = jnp.where(fine, far_off, 1.0)

        @pl.when(jnp.max(far_off) > 0.0)
        def _():
            def stat_shifted(t, state):
                offset = pl.multiple_of(t * TILE, TILE)
                rows = pl.ds(pl.multiple_of(base + offset, BLOCK), TILE)
                at = pl.ds(offset, TILE)
                allowed = mask(offset, TILE)
                k = keys[rows, :]
                result = []
                for p in range(PAIRS):
                    cols = slice(p * PAIR, (p + 1) * PAIR)
                    top, total, dot = state[p]
                    s = jnp.dot(k, qst[:, cols], preferred_element_type=jnp.float32)
                    s = jnp.where(allowed, s * EXP_SCALE, NEG)
                    scores[at, cols] = s
                    new_top = jnp.maximum(top, jnp.max(s, axis=0, keepdims=True))
                    factor = jnp.exp2(top - new_top)
                    e = jnp.exp2(s - new_top)
                    result.append((
                        new_top,
                        total * factor + jnp.sum(e, axis=0, keepdims=True),
                        dot * factor + jnp.sum(e * probs[at, cols], axis=0, keepdims=True),
                    ))
                return tuple(result)

            lowest = jnp.full((1, PAIR), NEG, jnp.float32)
            state = lax.fori_loop(0, tiles, stat_shifted, ((lowest, zero, zero),) * PAIRS)
            for p, (top, total, dot) in enumerate(state):
                cols = slice(p * PAIR, (p + 1) * PAIR)
                norms[0:1, cols] = jnp.ones((1, PAIR), jnp.float32)
                norms[1:2, cols] = dot / total
                norms[2:3, cols] = top + jnp.log2(total)

            def normalise(t, carry):
                at = pl.ds(pl.multiple_of(t * TILE, TILE), TILE)
                for p in range(PAIRS):
                    cols = slice(p * PAIR, (p + 1) * PAIR)
                    scores[at, cols] = jnp.exp2(scores[at, cols] - norms[2:3, cols])
                return carry

            lax.fori_loop(0, tiles, normalise, 0)

        dqt[...] = jnp.zeros((HD, WIDTH), jnp.float32)

        def grad(offset, size, carry):
            offset = pl.multiple_of(offset, TILE)
            rows = pl.ds(pl.multiple_of(base + offset, BLOCK), size)
            at = pl.ds(offset, size)
            kt = keys[rows, :].T
            dk = dkeys[rows, :]
            dv = dvalues[rows, :]
            for p in range(PAIRS):
                cols = slice(p * PAIR, (p + 1) * PAIR)
                prob = scores[at, cols] * norms[0:1, cols]
                ds = prob * (probs[at, cols] - norms[1:2, cols])
                prob = prob.astype(jnp.bfloat16)
                ds = ds.astype(jnp.bfloat16)
                dv = dv + jnp.dot(prob, gs[cols, :], preferred_element_type=jnp.float32)
                dk = dk + jnp.dot(ds, qs[cols, :], preferred_element_type=jnp.float32)
                dqt[:, cols] += jnp.dot(kt, ds, preferred_element_type=jnp.float32)
            dkeys[rows, :] = dk
            dvalues[rows, :] = dv
            return carry

        sweep(grad, 0)
        for k, dq in enumerate(dqs):
            @pl.when(i == k)
            def _(dq=dq):
                for g in range(GROUP):
                    cols = slice(g * HD, (g + 1) * HD)
                    dq[:, cols] = (dqt[:, cols].T * INV_ROOT).astype(dq.dtype)
        return carry

    lax.fori_loop(0, len(distances), block, 0)


def first_kernel(distances, plan, lengths, *refs):
    place = here()
    n = len(distances)
    qds, refs = refs[:n], refs[n:]
    sources, refs = (refs[:NY], refs[NY:2 * NY]), refs[2 * NY:]
    dqs, refs = refs[:n], refs[n:]
    keys, values, dkeys, dvalues = refs[:4]
    for core_rel, y_rel, z_rel, rows in slots(place, -1):
        keys[rows, :] = sources[core_rel][y_rel][z_rel, :, :HD]
        values[rows, :] = sources[core_rel][y_rel][z_rel, :, HD:]

    def clear(t, carry):
        rows = pl.ds(pl.multiple_of(t * TILE, TILE), TILE)
        dkeys[rows, :] = jnp.zeros((TILE, HD), jnp.float32)
        dvalues[rows, :] = jnp.zeros((TILE, HD), jnp.float32)
        return carry

    lax.fori_loop(0, SEQ // TILE, clear, 0)
    attend(place, plan, lengths, distances, qds, dqs, *refs)


def last_kernel(distances, plan, lengths, *refs):
    place = here()
    n = len(distances)
    qds, refs = refs[:n], refs[n:]
    (keys, values, dkeys_in, dvalues_in), refs = refs[:4], refs[4:]
    dqs, (keep, give, dkeys, dvalues), refs = refs[:n], refs[n:n + 4], refs[n + 4:]

    def load(t, carry):
        rows = pl.ds(pl.multiple_of(t * TILE, TILE), TILE)
        dkeys[rows, :] = dkeys_in[rows, :]
        dvalues[rows, :] = dvalues_in[rows, :]
        return carry

    lax.fori_loop(0, SEQ // TILE, load, 0)
    attend(place, plan, lengths, distances, qds, dqs, keys, values, dkeys, dvalues, *refs)
    for core_rel, y_rel, z_rel, rows in slots(place, 1):
        out = (keep, give)[core_rel]
        out[y_rel, z_rel, :, :HD] = (dkeys[rows, :] * INV_ROOT).astype(out.dtype)
        out[y_rel, z_rel, :, HD:] = dvalues[rows, :].astype(out.dtype)


def work_arrays():
    return [
        pltpu.VMEM((MAXTILES * TILE, WIDTH), jnp.float32),
        pltpu.VMEM((MAXTILES * TILE, WIDTH), jnp.float32),
        pltpu.VMEM((WIDTH, HD), jnp.bfloat16),
        pltpu.VMEM((HD, WIDTH), jnp.bfloat16),
        pltpu.VMEM((WIDTH, HD), jnp.bfloat16),
        pltpu.VMEM((HD, WIDTH), jnp.bfloat16),
        pltpu.VMEM((HD, WIDTH), jnp.float32),
        pltpu.VMEM((8, WIDTH), jnp.float32),
    ]


def attend_first(plan, lengths, distances, qds, own, other):
    n = len(distances)
    *dqs, keys, values, dkeys, dvalues = pl.pallas_call(
        functools.partial(first_kernel, distances),
        out_shape=[jax.ShapeDtypeStruct((BLOCK, WIDTH), jnp.bfloat16)] * n
        + [jax.ShapeDtypeStruct((SEQ, HD), jnp.bfloat16)] * 2
        + [jax.ShapeDtypeStruct((SEQ, HD), jnp.float32)] * 2,
        in_specs=[SMEM] * 2 + [VMEM] * (n + 2 * NY),
        out_specs=[VMEM] * (n + 4),
        scratch_shapes=work_arrays(),
        compiler_params=pltpu.CompilerParams(vmem_limit_bytes=VMEM_BYTES),
        cost_estimate=cost(n * BLOCK_FLOPS, 8 * 2**20),
        name="attention_first",
    )(plan, lengths, *qds, *own, *other)
    return dqs, (keys, values, dkeys, dvalues)


def attend_last(plan, lengths, distances, qds, state):
    n = len(distances)
    return pl.pallas_call(
        functools.partial(last_kernel, distances),
        out_shape=[jax.ShapeDtypeStruct((BLOCK, WIDTH), jnp.bfloat16)] * n
        + [jax.ShapeDtypeStruct((NY, NZ, BLOCK, 2 * HD), jnp.bfloat16)] * 2,
        in_specs=[SMEM] * 2 + [VMEM] * (n + 4),
        out_specs=[VMEM] * (n + 2),
        scratch_shapes=[pltpu.VMEM((SEQ, HD), jnp.float32)] * 2 + work_arrays(),
        compiler_params=pltpu.CompilerParams(vmem_limit_bytes=VMEM_BYTES),
        cost_estimate=cost(n * BLOCK_FLOPS, 8 * 2**20),
        name="attention_last",
    )(plan, lengths, *qds, *state)


def shards(queries, keys, values, grad_out, lengths, plan):
    z = lax.shift_right_logical(lax.axis_index("ctx").astype(jnp.int32), 3)

    def kv_part(d):
        at = ((z + d) & (NZ - 1)) * HD
        return jnp.concatenate(
            [lax.dynamic_slice_in_dim(keys, at, HD, 1), lax.dynamic_slice_in_dim(values, at, HD, 1)],
            axis=1,
        )

    with jax.named_scope("spread_keys"):
        row = [kv_part(0)] + [send(kv_part(d), d, 0, 0) for d in (1, 2, 3)]
        qd = pack(queries, grad_out)
        row, qd = lax.optimization_barrier((row, qd))
        row = jnp.stack(row)
        own = [row] + [send(row, 0, d, 0) for d in (1, 2, 3)]
        other = [send(part, 0, 0, 1) for part in own]
    with jax.named_scope("spread_queries"):
        near = [send(qd[d], d, 0, 0) for d in (1, 3)]
        late, near = lax.optimization_barrier((qd[2], near))
        far = send(late, 2, 0, 0)

    with jax.named_scope("attention"):
        (dq0, dq1, dq3), state = attend_first(
            plan, lengths, (0, 1, 3), (qd[0], *near), own, other
        )
        dq2, keep, give = attend_last(plan, lengths, (2,), (far,), state)

    with jax.named_scope("return_keys"):
        both = keep.astype(jnp.float32) + send(give, 0, 0, 1).astype(jnp.float32)
        both = both.astype(jnp.bfloat16)
        back1, back2 = send(dq1, -1, 0, 0), send(dq2, -2, 0, 0)
        parts = [send(both[d], 0, d, 0) for d in (1, 2, 3)]
        dq3, parts[0] = lax.optimization_barrier((dq3, parts[0]))
        back3 = send(dq3, -3, 0, 0)
        total = both[0].astype(jnp.float32)
        for part in parts:
            total = total + part.astype(jnp.float32)
        total, back1, back2 = lax.optimization_barrier((total.astype(jnp.bfloat16), back1, back2))
        heads = [total[0]] + [send(total[d], d, 0, 0) for d in (1, 2, 3)]
        grad_query = join_queries((dq0, back1, back2, back3))
        heads, grad_query = lax.optimization_barrier((heads, grad_query))
        return (grad_query, *join_keys(heads))


def solution(mesh):
    rows = P(("dp", "ctx"), None)
    return jax.shard_map(
        shards,
        mesh=mesh,
        in_specs=(rows, rows, rows, rows, P("dp"), P("dp")),
        out_specs=(rows, rows, rows),
        check_vma=False,
    )
```

```python
import functools
import math

import jax
import jax.numpy as jnp
from jax import lax
from jax.experimental import pallas as pl
from jax.experimental.pallas import tpu as pltpu
from jax.sharding import PartitionSpec as P

HD = 128
BLOCK = 128
DOCS = 8
KVH = 4
GROUP = 8
NZ = 4
NY = 4
SEQ = 4096
NBLK = 32
WIDTH = GROUP * HD
TILE = 256
MAXTILES = 9
SIZES = (4, 1)
PAIR = 256
PAIRS = WIDTH // PAIR
NEG = -1e30
SMALL_SUM = 1e-6
LARGE_SUM = 1e30
INV_ROOT = 1.0 / math.sqrt(HD)
EXP_SCALE = INV_ROOT / math.log(2.0)


SMEM = pl.BlockSpec(memory_space=pltpu.SMEM)
VMEM = pl.BlockSpec(memory_space=pltpu.VMEM)
HBM = pl.BlockSpec(memory_space=pltpu.HBM)
SMALL_VMEM_BYTES = 12 * 1024 * 1024
VMEM_BYTES = 40 * 1024 * 1024
BLOCK_FLOPS = 5 * 2 * WIDTH * 1024 * HD


def cost(flops, nbytes):
    return pl.CostEstimate(flops=flops, bytes_accessed=nbytes, transcendentals=0)


def ring(dz, dy, dc):
    return [
        ((z * NY + y) * 2 + c, ((z + dz) % NZ * NY + (y + dy) % NY) * 2 + (c ^ dc))
        for z in range(NZ)
        for y in range(NY)
        for c in range(2)
    ]


def send(x, dz, dy, dc):
    return lax.ppermute(x, "ctx", ring(dz, dy, dc))


def at_head(place, d, width):
    return pl.ds(pl.multiple_of((place[0] + d + NZ) % NZ * width, width), width)


def here():
    me = lax.axis_index("ctx")
    return lax.shift_right_logical(me, 3), lax.shift_right_logical(me, 1) & 3, me & 1


def pack_kernel(width, left, right, *refs):
    outs, sems = refs[:NZ], refs[NZ]
    place = here()
    copies = []
    for d, out in enumerate(outs):
        for half, source in enumerate((left, right)):
            copies.append(pltpu.make_async_copy(
                source.at[:, at_head(place, d, width)],
                out.at[:, half * width:(half + 1) * width],
                sems.at[len(copies)],
            ))
            copies[-1].start()
    for copy in copies:
        copy.wait()


def pack(left, right):
    width = left.shape[1] // KVH
    return pl.pallas_call(
        functools.partial(pack_kernel, width),
        out_shape=[jax.ShapeDtypeStruct((BLOCK, 2 * width), left.dtype)] * NZ,
        in_specs=[HBM] * 2,
        out_specs=[VMEM] * NZ,
        scratch_shapes=[pltpu.SemaphoreType.DMA((2 * NZ,))],
        compiler_params=pltpu.CompilerParams(vmem_limit_bytes=SMALL_VMEM_BYTES),
        cost_estimate=cost(0, 4 * left.size * 2),
        name="pack",
    )(left, right)


def join_queries_kernel(dq0, dq1, dq2, dq3, out, wide, sems):
    place = here()
    copies = []
    for d, part in enumerate((dq0, dq1, dq2, dq3)):
        wide[d] = part[...].astype(wide.dtype)
        copies.append(
            pltpu.make_async_copy(wide.at[d], out.at[:, at_head(place, d, WIDTH)], sems.at[d])
        )
        copies[-1].start()
    for copy in copies:
        copy.wait()


def join_queries(parts):
    return pl.pallas_call(
        join_queries_kernel,
        out_shape=jax.ShapeDtypeStruct((BLOCK, KVH * WIDTH), jnp.float32),
        in_specs=[VMEM] * NZ,
        out_specs=HBM,
        scratch_shapes=[
            pltpu.VMEM((NZ, BLOCK, WIDTH), jnp.float32),
            pltpu.SemaphoreType.DMA((NZ,)),
        ],
        compiler_params=pltpu.CompilerParams(vmem_limit_bytes=SMALL_VMEM_BYTES),
        cost_estimate=cost(0, BLOCK * KVH * WIDTH * 6),
        name="join_queries",
    )(*parts)


def join_keys_kernel(part0, part1, part2, part3, dk, dv):
    place = here()
    for d, part in enumerate((part0, part1, part2, part3)):
        dk[:, at_head(place, -d, HD)] = part[:, :HD].astype(dk.dtype)
        dv[:, at_head(place, -d, HD)] = part[:, HD:].astype(dv.dtype)


def join_keys(parts):
    return pl.pallas_call(
        join_keys_kernel,
        out_shape=[jax.ShapeDtypeStruct((BLOCK, KVH * HD), jnp.float32)] * 2,
        in_specs=[VMEM] * NZ,
        out_specs=[VMEM] * 2,
        compiler_params=pltpu.CompilerParams(vmem_limit_bytes=SMALL_VMEM_BYTES),
        cost_estimate=cost(0, BLOCK * KVH * HD * 12),
        name="join_keys",
    )(*parts)


def slots(place, sign):
    z, y, c = place
    for core_rel in range(2):
        for y_rel in range(NY):
            for z_rel in range(NZ):
                chip = ((z + sign * z_rel) & (NZ - 1)) * NY + ((y + sign * y_rel) & (NY - 1))
                slot = chip * 2 + (c ^ core_rel)
                yield core_rel, y_rel, z_rel, pl.ds(pl.multiple_of(slot * BLOCK, BLOCK), BLOCK)


def attend(
    place, plan, lengths, distances, qds, dqs,
    keys, values, dkeys, dvalues, scores, probs, qs, qst, gs, gst, dqt, norms,
):
    z, y, c = place[0], place[1], place[2]

    def block(i, carry):
        d = jnp.int32(distances[0])
        for k, qd in enumerate(qds):
            d = jnp.where(i == k, distances[k], d)

            @pl.when(i == k)
            def _(qd=qd):
                for g in range(GROUP):
                    rows = slice(g * BLOCK, (g + 1) * BLOCK)
                    q = qd[:, g * HD:(g + 1) * HD]
                    o = qd[:, WIDTH + g * HD:WIDTH + (g + 1) * HD]
                    qs[rows, :] = q
                    gs[rows, :] = o
                    qst[:, rows] = q.T
                    gst[:, rows] = o.T

        first = plan[((z - d + NZ) % NZ * NY + y) * 2 + c] * BLOCK
        pos = first + lax.broadcasted_iota(jnp.int32, (1, BLOCK), 1)
        start = jnp.zeros((1, BLOCK), jnp.int32)
        low = jnp.int32(0)
        end = jnp.int32(0)
        for e in range(DOCS):
            end = end + lengths[e]
            start = jnp.where(end <= pos, end, start)
            low = jnp.where(end <= first, end, low)
        tiles = (first + BLOCK - low // BLOCK * BLOCK + TILE - 1) // TILE
        base = jnp.maximum(first + BLOCK - tiles * TILE, 0)

        def sweep(body, state):
            done = jnp.int32(0)
            for size in SIZES:
                count = (tiles - done) // size
                state = lax.fori_loop(
                    0,
                    count,
                    lambda t, state, done=done, size=size: body(
                        (done + t * size) * TILE, size * TILE, state
                    ),
                    state,
                )
                done = done + count * size
            return state

        def mask(offset, size):
            key_pos = base + offset + lax.broadcasted_iota(jnp.int32, (size, BLOCK), 0)
            allowed = (key_pos >= start) & (key_pos <= pos)
            return jnp.concatenate([allowed] * (PAIR // BLOCK), axis=1)

        def stat(offset, size, state):
            offset = pl.multiple_of(offset, TILE)
            rows = pl.ds(pl.multiple_of(base + offset, BLOCK), size)
            at = pl.ds(offset, size)
            allowed = mask(offset, size)
            k, v = keys[rows, :], values[rows, :]
            result = []
            for p in range(PAIRS):
                cols = slice(p * PAIR, (p + 1) * PAIR)
                total, dot = state[p]
                s = jnp.dot(k, qst[:, cols], preferred_element_type=jnp.float32)
                e = jnp.exp2(jnp.where(allowed, s * EXP_SCALE, NEG))
                scores[at, cols] = e
                g = jnp.dot(v, gst[:, cols], preferred_element_type=jnp.float32)
                probs[at, cols] = g
                result.append((
                    total + jnp.sum(e, axis=0, keepdims=True),
                    dot + jnp.sum(e * g, axis=0, keepdims=True),
                ))
            return tuple(result)

        zero = jnp.zeros((1, PAIR), jnp.float32)
        state = sweep(stat, ((zero, zero),) * PAIRS)
        far_off = jnp.zeros((1, PAIR), jnp.float32)
        for p, (total, dot) in enumerate(state):
            cols = slice(p * PAIR, (p + 1) * PAIR)
            norms[0:1, cols] = 1.0 / total
            norms[1:2, cols] = dot / total
            fine = (total > SMALL_SUM) & (total < LARGE_SUM) & (jnp.abs(dot) < LARGE_SUM)
            far_off = jnp.where(fine, far_off, 1.0)

        @pl.when(jnp.max(far_off) > 0.0)
        def _():
            def stat_shifted(t, state):
                offset = pl.multiple_of(t * TILE, TILE)
                rows = pl.ds(pl.multiple_of(base + offset, BLOCK), TILE)
                at = pl.ds(offset, TILE)
                allowed = mask(offset, TILE)
                k = keys[rows, :]
                result = []
                for p in range(PAIRS):
                    cols = slice(p * PAIR, (p + 1) * PAIR)
                    top, total, dot = state[p]
                    s = jnp.dot(k, qst[:, cols], preferred_element_type=jnp.float32)
                    s = jnp.where(allowed, s * EXP_SCALE, NEG)
                    scores[at, cols] = s
                    new_top = jnp.maximum(top, jnp.max(s, axis=0, keepdims=True))
                    factor = jnp.exp2(top - new_top)
                    e = jnp.exp2(s - new_top)
                    result.append((
                        new_top,
                        total * factor + jnp.sum(e, axis=0, keepdims=True),
                        dot * factor + jnp.sum(e * probs[at, cols], axis=0, keepdims=True),
                    ))
                return tuple(result)

            lowest = jnp.full((1, PAIR), NEG, jnp.float32)
            state = lax.fori_loop(0, tiles, stat_shifted, ((lowest, zero, zero),) * PAIRS)
            for p, (top, total, dot) in enumerate(state):
                cols = slice(p * PAIR, (p + 1) * PAIR)
                norms[0:1, cols] = jnp.ones((1, PAIR), jnp.float32)
                norms[1:2, cols] = dot / total
                norms[2:3, cols] = top + jnp.log2(total)

            def normalise(t, carry):
                at = pl.ds(pl.multiple_of(t * TILE, TILE), TILE)
                for p in range(PAIRS):
                    cols = slice(p * PAIR, (p + 1) * PAIR)
                    scores[at, cols] = jnp.exp2(scores[at, cols] - norms[2:3, cols])
                return carry

            lax.fori_loop(0, tiles, normalise, 0)

        dqt[...] = jnp.zeros((HD, WIDTH), jnp.float32)

        def grad(offset, size, carry):
            offset = pl.multiple_of(offset, TILE)
            rows = pl.ds(pl.multiple_of(base + offset, BLOCK), size)
            at = pl.ds(offset, size)
            kt = keys[rows, :].T
            dk = dkeys[rows, :]
            dv = dvalues[rows, :]
            for p in range(PAIRS):
                cols = slice(p * PAIR, (p + 1) * PAIR)
                prob = scores[at, cols] * norms[0:1, cols]
                ds = prob * (probs[at, cols] - norms[1:2, cols])
                prob = prob.astype(jnp.bfloat16)
                ds = ds.astype(jnp.bfloat16)
                dv = dv + jnp.dot(prob, gs[cols, :], preferred_element_type=jnp.float32)
                dk = dk + jnp.dot(ds, qs[cols, :], preferred_element_type=jnp.float32)
                dqt[:, cols] += jnp.dot(kt, ds, preferred_element_type=jnp.float32)
            dkeys[rows, :] = dk
            dvalues[rows, :] = dv
            return carry

        sweep(grad, 0)
        for k, dq in enumerate(dqs):
            @pl.when(i == k)
            def _(dq=dq):
                for g in range(GROUP):
                    cols = slice(g * HD, (g + 1) * HD)
                    dq[:, cols] = (dqt[:, cols].T * INV_ROOT).astype(dq.dtype)
        return carry

    lax.fori_loop(0, len(distances), block, 0)


def first_kernel(distances, plan, lengths, *refs):
    place = here()
    n = len(distances)
    qds, refs = refs[:n], refs[n:]
    sources, refs = (refs[:NY], refs[NY:2 * NY]), refs[2 * NY:]
    dqs, refs = refs[:n], refs[n:]
    keys, values, dkeys, dvalues = refs[:4]
    for core_rel, y_rel, z_rel, rows in slots(place, -1):
        keys[rows, :] = sources[core_rel][y_rel][z_rel, :, :HD]
        values[rows, :] = sources[core_rel][y_rel][z_rel, :, HD:]

    def clear(t, carry):
        rows = pl.ds(pl.multiple_of(t * TILE, TILE), TILE)
        dkeys[rows, :] = jnp.zeros((TILE, HD), jnp.float32)
        dvalues[rows, :] = jnp.zeros((TILE, HD), jnp.float32)
        return carry

    lax.fori_loop(0, SEQ // TILE, clear, 0)
    attend(place, plan, lengths, distances, qds, dqs, *refs)


def last_kernel(distances, plan, lengths, *refs):
    place = here()
    n = len(distances)
    qds, refs = refs[:n], refs[n:]
    (keys, values, dkeys_in, dvalues_in), refs = refs[:4], refs[4:]
    dqs, (keep, give, dkeys, dvalues), refs = refs[:n], refs[n:n + 4], refs[n + 4:]

    def load(t, carry):
        rows = pl.ds(pl.multiple_of(t * TILE, TILE), TILE)
        dkeys[rows, :] = dkeys_in[rows, :]
        dvalues[rows, :] = dvalues_in[rows, :]
        return carry

    lax.fori_loop(0, SEQ // TILE, load, 0)
    attend(place, plan, lengths, distances, qds, dqs, keys, values, dkeys, dvalues, *refs)
    for core_rel, y_rel, z_rel, rows in slots(place, 1):
        out = (keep, give)[core_rel]
        out[y_rel, z_rel, :, :HD] = (dkeys[rows, :] * INV_ROOT).astype(out.dtype)
        out[y_rel, z_rel, :, HD:] = dvalues[rows, :].astype(out.dtype)


def work_arrays():
    return [
        pltpu.VMEM((MAXTILES * TILE, WIDTH), jnp.float32),
        pltpu.VMEM((MAXTILES * TILE, WIDTH), jnp.float32),
        pltpu.VMEM((WIDTH, HD), jnp.bfloat16),
        pltpu.VMEM((HD, WIDTH), jnp.bfloat16),
        pltpu.VMEM((WIDTH, HD), jnp.bfloat16),
        pltpu.VMEM((HD, WIDTH), jnp.bfloat16),
        pltpu.VMEM((HD, WIDTH), jnp.float32),
        pltpu.VMEM((8, WIDTH), jnp.float32),
    ]


def attend_first(plan, lengths, distances, qds, own, other):
    n = len(distances)
    *dqs, keys, values, dkeys, dvalues = pl.pallas_call(
        functools.partial(first_kernel, distances),
        out_shape=[jax.ShapeDtypeStruct((BLOCK, WIDTH), jnp.bfloat16)] * n
        + [jax.ShapeDtypeStruct((SEQ, HD), jnp.bfloat16)] * 2
        + [jax.ShapeDtypeStruct((SEQ, HD), jnp.float32)] * 2,
        in_specs=[SMEM] * 2 + [VMEM] * (n + 2 * NY),
        out_specs=[VMEM] * (n + 4),
        scratch_shapes=work_arrays(),
        compiler_params=pltpu.CompilerParams(vmem_limit_bytes=VMEM_BYTES),
        cost_estimate=cost(n * BLOCK_FLOPS, 8 * 2**20),
        name="attention_first",
    )(plan, lengths, *qds, *own, *other)
    return dqs, (keys, values, dkeys, dvalues)


def attend_last(plan, lengths, distances, qds, state):
    n = len(distances)
    return pl.pallas_call(
        functools.partial(last_kernel, distances),
        out_shape=[jax.ShapeDtypeStruct((BLOCK, WIDTH), jnp.bfloat16)] * n
        + [jax.ShapeDtypeStruct((NY, NZ, BLOCK, 2 * HD), jnp.bfloat16)] * 2,
        in_specs=[SMEM] * 2 + [VMEM] * (n + 4),
        out_specs=[VMEM] * (n + 2),
        scratch_shapes=[pltpu.VMEM((SEQ, HD), jnp.float32)] * 2 + work_arrays(),
        compiler_params=pltpu.CompilerParams(vmem_limit_bytes=VMEM_BYTES),
        cost_estimate=cost(n * BLOCK_FLOPS, 8 * 2**20),
        name="attention_last",
    )(plan, lengths, *qds, *state)


def shards(queries, keys, values, grad_out, lengths, plan):
    z = lax.shift_right_logical(lax.axis_index("ctx").astype(jnp.int32), 3)

    def kv_part(d):
        at = ((z + d) & (NZ - 1)) * HD
        return jnp.concatenate(
            [lax.dynamic_slice_in_dim(keys, at, HD, 1), lax.dynamic_slice_in_dim(values, at, HD, 1)],
            axis=1,
        )

    with jax.named_scope("spread_keys"):
        row = [kv_part(0)] + [send(kv_part(d), d, 0, 0) for d in (1, 2, 3)]
        qd = pack(queries, grad_out)
        row, qd = lax.optimization_barrier((row, qd))
        row = jnp.stack(row)
        own = [row] + [send(row, 0, d, 0) for d in (1, 2, 3)]
        other = [send(part, 0, 0, 1) for part in own]
    with jax.named_scope("spread_queries"):
        near = [send(qd[d], d, 0, 0) for d in (1, 3)]
        late, near = lax.optimization_barrier((qd[2], near))
        far = send(late, 2, 0, 0)

    with jax.named_scope("attention"):
        (dq0, dq1, dq3), state = attend_first(
            plan, lengths, (0, 1, 3), (qd[0], *near), own, other
        )
        dq2, keep, give = attend_last(plan, lengths, (2,), (far,), state)

    with jax.named_scope("return_keys"):
        both = keep.astype(jnp.float32) + send(give, 0, 0, 1).astype(jnp.float32)
        both = both.astype(jnp.bfloat16)
        back1, back3 = send(dq1, -1, 0, 0), send(dq3, -3, 0, 0)
        parts = [send(both[d], 0, d, 0) for d in (1, 2, 3)]
        dq2, parts[0] = lax.optimization_barrier((dq2, parts[0]))
        back2 = send(dq2, -2, 0, 0)
        total = both[0].astype(jnp.float32)
        for part in parts:
            total = total + part.astype(jnp.float32)
        total, back1, back3 = lax.optimization_barrier((total.astype(jnp.bfloat16), back1, back3))
        heads = [total[0]] + [send(total[d], d, 0, 0) for d in (1, 2, 3)]
        grad_query = join_queries((dq0, back1, back2, back3))
        heads, grad_query = lax.optimization_barrier((heads, grad_query))
        return (grad_query, *join_keys(heads))


def solution(mesh):
    rows = P(("dp", "ctx"), None)
    return jax.shard_map(
        shards,
        mesh=mesh,
        in_specs=(rows, rows, rows, rows, P("dp"), P("dp")),
        out_specs=(rows, rows, rows),
        check_vma=False,
    )
```

```python
import functools
import math

import jax
import jax.numpy as jnp
from jax import lax
from jax.experimental import pallas as pl
from jax.experimental.pallas import tpu as pltpu
from jax.sharding import PartitionSpec as P

HD = 128
BLOCK = 128
DOCS = 8
KVH = 4
GROUP = 8
NZ = 4
NY = 4
SEQ = 4096
NBLK = 32
WIDTH = GROUP * HD
TILE = 256
MAXTILES = 9
SIZES = (4, 1)
PAIR = 256
PAIRS = WIDTH // PAIR
NEG = -1e30
SMALL_SUM = 1e-6
LARGE_SUM = 1e30
INV_ROOT = 1.0 / math.sqrt(HD)
EXP_SCALE = INV_ROOT / math.log(2.0)


SMEM = pl.BlockSpec(memory_space=pltpu.SMEM)
VMEM = pl.BlockSpec(memory_space=pltpu.VMEM)
HBM = pl.BlockSpec(memory_space=pltpu.HBM)
SMALL_VMEM_BYTES = 12 * 1024 * 1024
VMEM_BYTES = 40 * 1024 * 1024
BLOCK_FLOPS = 5 * 2 * WIDTH * 1024 * HD


def cost(flops, nbytes):
    return pl.CostEstimate(flops=flops, bytes_accessed=nbytes, transcendentals=0)


def ring(dz, dy, dc):
    return [
        ((z * NY + y) * 2 + c, ((z + dz) % NZ * NY + (y + dy) % NY) * 2 + (c ^ dc))
        for z in range(NZ)
        for y in range(NY)
        for c in range(2)
    ]


def send(x, dz, dy, dc):
    return lax.ppermute(x, "ctx", ring(dz, dy, dc))


def at_head(place, d, width):
    return pl.ds(pl.multiple_of((place[0] + d + NZ) % NZ * width, width), width)


def here():
    me = lax.axis_index("ctx")
    return lax.shift_right_logical(me, 3), lax.shift_right_logical(me, 1) & 3, me & 1


def pack_kernel(width, left, right, *refs):
    outs, sems = refs[:NZ], refs[NZ]
    place = here()
    copies = []
    for d, out in enumerate(outs):
        for half, source in enumerate((left, right)):
            copies.append(pltpu.make_async_copy(
                source.at[:, at_head(place, d, width)],
                out.at[:, half * width:(half + 1) * width],
                sems.at[len(copies)],
            ))
            copies[-1].start()
    for copy in copies:
        copy.wait()


def pack(left, right):
    width = left.shape[1] // KVH
    return pl.pallas_call(
        functools.partial(pack_kernel, width),
        out_shape=[jax.ShapeDtypeStruct((BLOCK, 2 * width), left.dtype)] * NZ,
        in_specs=[HBM] * 2,
        out_specs=[VMEM] * NZ,
        scratch_shapes=[pltpu.SemaphoreType.DMA((2 * NZ,))],
        compiler_params=pltpu.CompilerParams(vmem_limit_bytes=SMALL_VMEM_BYTES),
        cost_estimate=cost(0, 4 * left.size * 2),
        name="pack",
    )(left, right)


def join_queries_kernel(dq0, dq1, dq2, dq3, out, wide, sems):
    place = here()
    copies = []
    for d, part in enumerate((dq0, dq1, dq2, dq3)):
        wide[d] = part[...].astype(wide.dtype)
        copies.append(
            pltpu.make_async_copy(wide.at[d], out.at[:, at_head(place, d, WIDTH)], sems.at[d])
        )
        copies[-1].start()
    for copy in copies:
        copy.wait()


def join_queries(parts):
    return pl.pallas_call(
        join_queries_kernel,
        out_shape=jax.ShapeDtypeStruct((BLOCK, KVH * WIDTH), jnp.float32),
        in_specs=[VMEM] * NZ,
        out_specs=HBM,
        scratch_shapes=[
            pltpu.VMEM((NZ, BLOCK, WIDTH), jnp.float32),
            pltpu.SemaphoreType.DMA((NZ,)),
        ],
        compiler_params=pltpu.CompilerParams(vmem_limit_bytes=SMALL_VMEM_BYTES),
        cost_estimate=cost(0, BLOCK * KVH * WIDTH * 6),
        name="join_queries",
    )(*parts)


def join_keys_kernel(part0, part1, part2, part3, dk, dv):
    place = here()
    for d, part in enumerate((part0, part1, part2, part3)):
        dk[:, at_head(place, -d, HD)] = part[:, :HD].astype(dk.dtype)
        dv[:, at_head(place, -d, HD)] = part[:, HD:].astype(dv.dtype)


def join_keys(parts):
    return pl.pallas_call(
        join_keys_kernel,
        out_shape=[jax.ShapeDtypeStruct((BLOCK, KVH * HD), jnp.float32)] * 2,
        in_specs=[VMEM] * NZ,
        out_specs=[VMEM] * 2,
        compiler_params=pltpu.CompilerParams(vmem_limit_bytes=SMALL_VMEM_BYTES),
        cost_estimate=cost(0, BLOCK * KVH * HD * 12),
        name="join_keys",
    )(*parts)


def slots(place, sign):
    z, y, c = place
    for core_rel in range(2):
        for y_rel in range(NY):
            for z_rel in range(NZ):
                chip = ((z + sign * z_rel) & (NZ - 1)) * NY + ((y + sign * y_rel) & (NY - 1))
                slot = chip * 2 + (c ^ core_rel)
                yield core_rel, y_rel, z_rel, pl.ds(pl.multiple_of(slot * BLOCK, BLOCK), BLOCK)


def attend(
    place, plan, lengths, distances, qds, dqs,
    keys, values, dkeys, dvalues, scores, probs, qs, qst, gs, gst, dqt, norms,
):
    z, y, c = place[0], place[1], place[2]

    def block(i, carry):
        d = jnp.int32(distances[0])
        for k, qd in enumerate(qds):
            d = jnp.where(i == k, distances[k], d)

            @pl.when(i == k)
            def _(qd=qd):
                for g in range(GROUP):
                    rows = slice(g * BLOCK, (g + 1) * BLOCK)
                    q = qd[:, g * HD:(g + 1) * HD]
                    o = qd[:, WIDTH + g * HD:WIDTH + (g + 1) * HD]
                    qs[rows, :] = q
                    gs[rows, :] = o
                    qst[:, rows] = q.T
                    gst[:, rows] = o.T

        first = plan[((z - d + NZ) % NZ * NY + y) * 2 + c] * BLOCK
        pos = first + lax.broadcasted_iota(jnp.int32, (1, BLOCK), 1)
        start = jnp.zeros((1, BLOCK), jnp.int32)
        low = jnp.int32(0)
        end = jnp.int32(0)
        for e in range(DOCS):
            end = end + lengths[e]
            start = jnp.where(end <= pos, end, start)
            low = jnp.where(end <= first, end, low)
        tiles = (first + BLOCK - low // BLOCK * BLOCK + TILE - 1) // TILE
        base = jnp.maximum(first + BLOCK - tiles * TILE, 0)

        def sweep(body, state):
            done = jnp.int32(0)
            for size in SIZES:
                count = (tiles - done) // size
                state = lax.fori_loop(
                    0,
                    count,
                    lambda t, state, done=done, size=size: body(
                        (done + t * size) * TILE, size * TILE, state
                    ),
                    state,
                )
                done = done + count * size
            return state

        def mask(offset, size):
            key_pos = base + offset + lax.broadcasted_iota(jnp.int32, (size, BLOCK), 0)
            allowed = (key_pos >= start) & (key_pos <= pos)
            return jnp.concatenate([allowed] * (PAIR // BLOCK), axis=1)

        def stat(offset, size, state):
            offset = pl.multiple_of(offset, TILE)
            rows = pl.ds(pl.multiple_of(base + offset, BLOCK), size)
            at = pl.ds(offset, size)
            allowed = mask(offset, size)
            k, v = keys[rows, :], values[rows, :]
            result = []
            for p in range(PAIRS):
                cols = slice(p * PAIR, (p + 1) * PAIR)
                total, dot = state[p]
                s = jnp.dot(k, qst[:, cols], preferred_element_type=jnp.float32)
                e = jnp.exp2(jnp.where(allowed, s * EXP_SCALE, NEG))
                scores[at, cols] = e
                g = jnp.dot(v, gst[:, cols], preferred_element_type=jnp.float32)
                probs[at, cols] = g
                result.append((
                    total + jnp.sum(e, axis=0, keepdims=True),
                    dot + jnp.sum(e * g, axis=0, keepdims=True),
                ))
            return tuple(result)

        zero = jnp.zeros((1, PAIR), jnp.float32)
        state = sweep(stat, ((zero, zero),) * PAIRS)
        far_off = jnp.zeros((1, PAIR), jnp.float32)
        for p, (total, dot) in enumerate(state):
            cols = slice(p * PAIR, (p + 1) * PAIR)
            norms[0:1, cols] = 1.0 / total
            norms[1:2, cols] = dot / total
            fine = (total > SMALL_SUM) & (total < LARGE_SUM) & (jnp.abs(dot) < LARGE_SUM)
            far_off = jnp.where(fine, far_off, 1.0)

        @pl.when(jnp.max(far_off) > 0.0)
        def _():
            def stat_shifted(t, state):
                offset = pl.multiple_of(t * TILE, TILE)
                rows = pl.ds(pl.multiple_of(base + offset, BLOCK), TILE)
                at = pl.ds(offset, TILE)
                allowed = mask(offset, TILE)
                k = keys[rows, :]
                result = []
                for p in range(PAIRS):
                    cols = slice(p * PAIR, (p + 1) * PAIR)
                    top, total, dot = state[p]
                    s = jnp.dot(k, qst[:, cols], preferred_element_type=jnp.float32)
                    s = jnp.where(allowed, s * EXP_SCALE, NEG)
                    scores[at, cols] = s
                    new_top = jnp.maximum(top, jnp.max(s, axis=0, keepdims=True))
                    factor = jnp.exp2(top - new_top)
                    e = jnp.exp2(s - new_top)
                    result.append((
                        new_top,
                        total * factor + jnp.sum(e, axis=0, keepdims=True),
                        dot * factor + jnp.sum(e * probs[at, cols], axis=0, keepdims=True),
                    ))
                return tuple(result)

            lowest = jnp.full((1, PAIR), NEG, jnp.float32)
            state = lax.fori_loop(0, tiles, stat_shifted, ((lowest, zero, zero),) * PAIRS)
            for p, (top, total, dot) in enumerate(state):
                cols = slice(p * PAIR, (p + 1) * PAIR)
                norms[0:1, cols] = jnp.ones((1, PAIR), jnp.float32)
                norms[1:2, cols] = dot / total
                norms[2:3, cols] = top + jnp.log2(total)

            def normalise(t, carry):
                at = pl.ds(pl.multiple_of(t * TILE, TILE), TILE)
                for p in range(PAIRS):
                    cols = slice(p * PAIR, (p + 1) * PAIR)
                    scores[at, cols] = jnp.exp2(scores[at, cols] - norms[2:3, cols])
                return carry

            lax.fori_loop(0, tiles, normalise, 0)

        dqt[...] = jnp.zeros((HD, WIDTH), jnp.float32)

        def grad(offset, size, carry):
            offset = pl.multiple_of(offset, TILE)
            rows = pl.ds(pl.multiple_of(base + offset, BLOCK), size)
            at = pl.ds(offset, size)
            kt = keys[rows, :].T
            dk = dkeys[rows, :]
            dv = dvalues[rows, :]
            for p in range(PAIRS):
                cols = slice(p * PAIR, (p + 1) * PAIR)
                prob = scores[at, cols] * norms[0:1, cols]
                ds = prob * (probs[at, cols] - norms[1:2, cols])
                prob = prob.astype(jnp.bfloat16)
                ds = ds.astype(jnp.bfloat16)
                dv = dv + jnp.dot(prob, gs[cols, :], preferred_element_type=jnp.float32)
                dk = dk + jnp.dot(ds, qs[cols, :], preferred_element_type=jnp.float32)
                dqt[:, cols] += jnp.dot(kt, ds, preferred_element_type=jnp.float32)
            dkeys[rows, :] = dk
            dvalues[rows, :] = dv
            return carry

        sweep(grad, 0)
        for k, dq in enumerate(dqs):
            @pl.when(i == k)
            def _(dq=dq):
                for g in range(GROUP):
                    cols = slice(g * HD, (g + 1) * HD)
                    dq[:, cols] = (dqt[:, cols].T * INV_ROOT).astype(dq.dtype)
        return carry

    lax.fori_loop(0, len(distances), block, 0)


def first_kernel(distances, plan, lengths, *refs):
    place = here()
    n = len(distances)
    qds, refs = refs[:n], refs[n:]
    sources, refs = (refs[:NY], refs[NY:2 * NY]), refs[2 * NY:]
    dqs, refs = refs[:n], refs[n:]
    keys, values, dkeys, dvalues = refs[:4]
    for core_rel, y_rel, z_rel, rows in slots(place, -1):
        keys[rows, :] = sources[core_rel][y_rel][z_rel, :, :HD]
        values[rows, :] = sources[core_rel][y_rel][z_rel, :, HD:]

    def clear(t, carry):
        rows = pl.ds(pl.multiple_of(t * TILE, TILE), TILE)
        dkeys[rows, :] = jnp.zeros((TILE, HD), jnp.float32)
        dvalues[rows, :] = jnp.zeros((TILE, HD), jnp.float32)
        return carry

    lax.fori_loop(0, SEQ // TILE, clear, 0)
    attend(place, plan, lengths, distances, qds, dqs, *refs)


def last_kernel(distances, plan, lengths, *refs):
    place = here()
    n = len(distances)
    qds, refs = refs[:n], refs[n:]
    (keys, values, dkeys_in, dvalues_in), refs = refs[:4], refs[4:]
    dqs, (keep, give, dkeys, dvalues), refs = refs[:n], refs[n:n + 4], refs[n + 4:]

    def load(t, carry):
        rows = pl.ds(pl.multiple_of(t * TILE, TILE), TILE)
        dkeys[rows, :] = dkeys_in[rows, :]
        dvalues[rows, :] = dvalues_in[rows, :]
        return carry

    lax.fori_loop(0, SEQ // TILE, load, 0)
    attend(place, plan, lengths, distances, qds, dqs, keys, values, dkeys, dvalues, *refs)
    for core_rel, y_rel, z_rel, rows in slots(place, 1):
        out = (keep, give)[core_rel]
        out[y_rel, z_rel, :, :HD] = (dkeys[rows, :] * INV_ROOT).astype(out.dtype)
        out[y_rel, z_rel, :, HD:] = dvalues[rows, :].astype(out.dtype)


def work_arrays():
    return [
        pltpu.VMEM((MAXTILES * TILE, WIDTH), jnp.float32),
        pltpu.VMEM((MAXTILES * TILE, WIDTH), jnp.float32),
        pltpu.VMEM((WIDTH, HD), jnp.bfloat16),
        pltpu.VMEM((HD, WIDTH), jnp.bfloat16),
        pltpu.VMEM((WIDTH, HD), jnp.bfloat16),
        pltpu.VMEM((HD, WIDTH), jnp.bfloat16),
        pltpu.VMEM((HD, WIDTH), jnp.float32),
        pltpu.VMEM((8, WIDTH), jnp.float32),
    ]


def attend_first(plan, lengths, distances, qds, own, other):
    n = len(distances)
    *dqs, keys, values, dkeys, dvalues = pl.pallas_call(
        functools.partial(first_kernel, distances),
        out_shape=[jax.ShapeDtypeStruct((BLOCK, WIDTH), jnp.bfloat16)] * n
        + [jax.ShapeDtypeStruct((SEQ, HD), jnp.bfloat16)] * 2
        + [jax.ShapeDtypeStruct((SEQ, HD), jnp.float32)] * 2,
        in_specs=[SMEM] * 2 + [VMEM] * (n + 2 * NY),
        out_specs=[VMEM] * (n + 4),
        scratch_shapes=work_arrays(),
        compiler_params=pltpu.CompilerParams(vmem_limit_bytes=VMEM_BYTES),
        cost_estimate=cost(0, 0),
        name="attention_first",
    )(plan, lengths, *qds, *own, *other)
    return dqs, (keys, values, dkeys, dvalues)


def attend_last(plan, lengths, distances, qds, state):
    n = len(distances)
    return pl.pallas_call(
        functools.partial(last_kernel, distances),
        out_shape=[jax.ShapeDtypeStruct((BLOCK, WIDTH), jnp.bfloat16)] * n
        + [jax.ShapeDtypeStruct((NY, NZ, BLOCK, 2 * HD), jnp.bfloat16)] * 2,
        in_specs=[SMEM] * 2 + [VMEM] * (n + 4),
        out_specs=[VMEM] * (n + 2),
        scratch_shapes=[pltpu.VMEM((SEQ, HD), jnp.float32)] * 2 + work_arrays(),
        compiler_params=pltpu.CompilerParams(vmem_limit_bytes=VMEM_BYTES),
        cost_estimate=cost(n * BLOCK_FLOPS, 8 * 2**20),
        name="attention_last",
    )(plan, lengths, *qds, *state)


def shards(queries, keys, values, grad_out, lengths, plan):
    z = lax.shift_right_logical(lax.axis_index("ctx").astype(jnp.int32), 3)

    def kv_part(d):
        at = ((z + d) & (NZ - 1)) * HD
        return jnp.concatenate(
            [lax.dynamic_slice_in_dim(keys, at, HD, 1), lax.dynamic_slice_in_dim(values, at, HD, 1)],
            axis=1,
        )

    with jax.named_scope("spread_keys"):
        row = [kv_part(0)] + [send(kv_part(d), d, 0, 0) for d in (1, 2, 3)]
        qd = pack(queries, grad_out)
        row, qd = lax.optimization_barrier((row, qd))
        row = jnp.stack(row)
        own = [row] + [send(row, 0, d, 0) for d in (1, 2, 3)]
    with jax.named_scope("spread_queries"):
        near = [send(qd[d], d, 0, 0) for d in (1, 3)]
        late, near = lax.optimization_barrier((qd[2], near))
        far = send(late, 2, 0, 0)
    with jax.named_scope("spread_keys"):
        own[1], near = lax.optimization_barrier((own[1], near))
        own[2], near = lax.optimization_barrier((own[2], near))
        own[3], near = lax.optimization_barrier((own[3], near))
        other = [send(part, 0, 0, 1) for part in own]

    with jax.named_scope("attention"):
        (dq0, dq1, dq3), state = attend_first(
            plan, lengths, (0, 1, 3), (qd[0], *near), own, other
        )
        dq2, keep, give = attend_last(plan, lengths, (2,), (far,), state)

    with jax.named_scope("return_keys"):
        both = keep.astype(jnp.float32) + send(give, 0, 0, 1).astype(jnp.float32)
        both = both.astype(jnp.bfloat16)
        back1, back3 = send(dq1, -1, 0, 0), send(dq3, -3, 0, 0)
        parts = [send(both[d], 0, d, 0) for d in (1, 2, 3)]
        dq2, parts[0] = lax.optimization_barrier((dq2, parts[0]))
        back2 = send(dq2, -2, 0, 0)
        total = both[0].astype(jnp.float32)
        for part in parts:
            total = total + part.astype(jnp.float32)
        total, back1, back3 = lax.optimization_barrier((total.astype(jnp.bfloat16), back1, back3))
        heads = [total[0]] + [send(total[d], d, 0, 0) for d in (1, 2, 3)]
        grad_query = join_queries((dq0, back1, back2, back3))
        heads, grad_query = lax.optimization_barrier((heads, grad_query))
        return (grad_query, *join_keys(heads))


def solution(mesh):
    rows = P(("dp", "ctx"), None)
    return jax.shard_map(
        shards,
        mesh=mesh,
        in_specs=(rows, rows, rows, rows, P("dp"), P("dp")),
        out_specs=(rows, rows, rows),
        check_vma=False,
    )
```

```python
import functools
import math

import jax
import jax.numpy as jnp
from jax import lax
from jax.experimental import pallas as pl
from jax.experimental.pallas import tpu as pltpu
from jax.sharding import PartitionSpec as P

HD = 128
BLOCK = 128
DOCS = 8
KVH = 4
GROUP = 8
NZ = 4
NY = 4
SEQ = 4096
NBLK = 32
WIDTH = GROUP * HD
TILE = 256
MAXTILES = 9
SIZES = (4, 1)
PAIR = 256
PAIRS = WIDTH // PAIR
NEG = -1e30
SMALL_SUM = 1e-6
LARGE_SUM = 1e30
INV_ROOT = 1.0 / math.sqrt(HD)
EXP_SCALE = INV_ROOT / math.log(2.0)


SMEM = pl.BlockSpec(memory_space=pltpu.SMEM)
VMEM = pl.BlockSpec(memory_space=pltpu.VMEM)
HBM = pl.BlockSpec(memory_space=pltpu.HBM)
SMALL_VMEM_BYTES = 12 * 1024 * 1024
VMEM_BYTES = 40 * 1024 * 1024
BLOCK_FLOPS = 5 * 2 * WIDTH * 1024 * HD


def cost(flops, nbytes):
    return pl.CostEstimate(flops=flops, bytes_accessed=nbytes, transcendentals=0)


def ring(dz, dy, dc):
    return [
        ((z * NY + y) * 2 + c, ((z + dz) % NZ * NY + (y + dy) % NY) * 2 + (c ^ dc))
        for z in range(NZ)
        for y in range(NY)
        for c in range(2)
    ]


def send(x, dz, dy, dc):
    return lax.ppermute(x, "ctx", ring(dz, dy, dc))


def at_head(place, d, width):
    return pl.ds(pl.multiple_of((place[0] + d + NZ) % NZ * width, width), width)


def here():
    me = lax.axis_index("ctx")
    return lax.shift_right_logical(me, 3), lax.shift_right_logical(me, 1) & 3, me & 1


def pack_kernel(width, left, right, *refs):
    outs, sems = refs[:NZ], refs[NZ]
    place = here()
    copies = []
    for d, out in enumerate(outs):
        for half, source in enumerate((left, right)):
            copies.append(pltpu.make_async_copy(
                source.at[:, at_head(place, d, width)],
                out.at[:, half * width:(half + 1) * width],
                sems.at[len(copies)],
            ))
            copies[-1].start()
    for copy in copies:
        copy.wait()


def pack(left, right):
    width = left.shape[1] // KVH
    return pl.pallas_call(
        functools.partial(pack_kernel, width),
        out_shape=[jax.ShapeDtypeStruct((BLOCK, 2 * width), left.dtype)] * NZ,
        in_specs=[HBM] * 2,
        out_specs=[VMEM] * NZ,
        scratch_shapes=[pltpu.SemaphoreType.DMA((2 * NZ,))],
        compiler_params=pltpu.CompilerParams(vmem_limit_bytes=SMALL_VMEM_BYTES),
        cost_estimate=cost(0, 4 * left.size * 2),
        name="pack",
    )(left, right)


def join_queries_kernel(dq0, dq1, dq2, dq3, out, wide, sems):
    place = here()
    copies = []
    for d, part in enumerate((dq0, dq1, dq2, dq3)):
        wide[d] = part[...].astype(wide.dtype)
        copies.append(
            pltpu.make_async_copy(wide.at[d], out.at[:, at_head(place, d, WIDTH)], sems.at[d])
        )
        copies[-1].start()
    for copy in copies:
        copy.wait()


def join_queries(parts):
    return pl.pallas_call(
        join_queries_kernel,
        out_shape=jax.ShapeDtypeStruct((BLOCK, KVH * WIDTH), jnp.float32),
        in_specs=[VMEM] * NZ,
        out_specs=HBM,
        scratch_shapes=[
            pltpu.VMEM((NZ, BLOCK, WIDTH), jnp.float32),
            pltpu.SemaphoreType.DMA((NZ,)),
        ],
        compiler_params=pltpu.CompilerParams(vmem_limit_bytes=SMALL_VMEM_BYTES),
        cost_estimate=cost(0, BLOCK * KVH * WIDTH * 6),
        name="join_queries",
    )(*parts)


def join_keys_kernel(part0, part1, part2, part3, dk, dv):
    place = here()
    for d, part in enumerate((part0, part1, part2, part3)):
        dk[:, at_head(place, -d, HD)] = part[:, :HD].astype(dk.dtype)
        dv[:, at_head(place, -d, HD)] = part[:, HD:].astype(dv.dtype)


def join_keys(parts):
    return pl.pallas_call(
        join_keys_kernel,
        out_shape=[jax.ShapeDtypeStruct((BLOCK, KVH * HD), jnp.float32)] * 2,
        in_specs=[VMEM] * NZ,
        out_specs=[VMEM] * 2,
        compiler_params=pltpu.CompilerParams(vmem_limit_bytes=SMALL_VMEM_BYTES),
        cost_estimate=cost(0, BLOCK * KVH * HD * 12),
        name="join_keys",
    )(*parts)


def slots(place, sign):
    z, y, c = place
    for core_rel in range(2):
        for y_rel in range(NY):
            for z_rel in range(NZ):
                chip = ((z + sign * z_rel) & (NZ - 1)) * NY + ((y + sign * y_rel) & (NY - 1))
                slot = chip * 2 + (c ^ core_rel)
                yield core_rel, y_rel, z_rel, pl.ds(pl.multiple_of(slot * BLOCK, BLOCK), BLOCK)


def attend(
    place, plan, lengths, distances, qds, dqs,
    keys, values, dkeys, dvalues, scores, probs, qs, qst, gs, gst, dqt, norms,
):
    z, y, c = place[0], place[1], place[2]

    def block(i, carry):
        d = jnp.int32(distances[0])
        for k, qd in enumerate(qds):
            d = jnp.where(i == k, distances[k], d)

            @pl.when(i == k)
            def _(qd=qd):
                for g in range(GROUP):
                    rows = slice(g * BLOCK, (g + 1) * BLOCK)
                    q = qd[:, g * HD:(g + 1) * HD]
                    o = qd[:, WIDTH + g * HD:WIDTH + (g + 1) * HD]
                    qs[rows, :] = q
                    gs[rows, :] = o
                    qst[:, rows] = q.T
                    gst[:, rows] = o.T

        first = plan[((z - d + NZ) % NZ * NY + y) * 2 + c] * BLOCK
        pos = first + lax.broadcasted_iota(jnp.int32, (1, BLOCK), 1)
        start = jnp.zeros((1, BLOCK), jnp.int32)
        low = jnp.int32(0)
        end = jnp.int32(0)
        for e in range(DOCS):
            end = end + lengths[e]
            start = jnp.where(end <= pos, end, start)
            low = jnp.where(end <= first, end, low)
        tiles = (first + BLOCK - low // BLOCK * BLOCK + TILE - 1) // TILE
        base = jnp.maximum(first + BLOCK - tiles * TILE, 0)

        def sweep(body, state):
            done = jnp.int32(0)
            for size in SIZES:
                count = (tiles - done) // size
                state = lax.fori_loop(
                    0,
                    count,
                    lambda t, state, done=done, size=size: body(
                        (done + t * size) * TILE, size * TILE, state
                    ),
                    state,
                )
                done = done + count * size
            return state

        def mask(offset, size):
            key_pos = base + offset + lax.broadcasted_iota(jnp.int32, (size, BLOCK), 0)
            allowed = (key_pos >= start) & (key_pos <= pos)
            return jnp.concatenate([allowed] * (PAIR // BLOCK), axis=1)

        def stat(offset, size, state):
            offset = pl.multiple_of(offset, TILE)
            rows = pl.ds(pl.multiple_of(base + offset, BLOCK), size)
            at = pl.ds(offset, size)
            allowed = mask(offset, size)
            k, v = keys[rows, :], values[rows, :]
            result = []
            for p in range(PAIRS):
                cols = slice(p * PAIR, (p + 1) * PAIR)
                total, dot = state[p]
                s = jnp.dot(k, qst[:, cols], preferred_element_type=jnp.float32)
                e = jnp.exp2(jnp.where(allowed, s * EXP_SCALE, NEG))
                scores[at, cols] = e
                g = jnp.dot(v, gst[:, cols], preferred_element_type=jnp.float32)
                probs[at, cols] = g
                result.append((
                    total + jnp.sum(e, axis=0, keepdims=True),
                    dot + jnp.sum(e * g, axis=0, keepdims=True),
                ))
            return tuple(result)

        zero = jnp.zeros((1, PAIR), jnp.float32)
        state = sweep(stat, ((zero, zero),) * PAIRS)
        far_off = jnp.zeros((1, PAIR), jnp.float32)
        for p, (total, dot) in enumerate(state):
            cols = slice(p * PAIR, (p + 1) * PAIR)
            norms[0:1, cols] = 1.0 / total
            norms[1:2, cols] = dot / total
            fine = (total > SMALL_SUM) & (total < LARGE_SUM) & (jnp.abs(dot) < LARGE_SUM)
            far_off = jnp.where(fine, far_off, 1.0)

        @pl.when(jnp.max(far_off) > 0.0)
        def _():
            def stat_shifted(t, state):
                offset = pl.multiple_of(t * TILE, TILE)
                rows = pl.ds(pl.multiple_of(base + offset, BLOCK), TILE)
                at = pl.ds(offset, TILE)
                allowed = mask(offset, TILE)
                k = keys[rows, :]
                result = []
                for p in range(PAIRS):
                    cols = slice(p * PAIR, (p + 1) * PAIR)
                    top, total, dot = state[p]
                    s = jnp.dot(k, qst[:, cols], preferred_element_type=jnp.float32)
                    s = jnp.where(allowed, s * EXP_SCALE, NEG)
                    scores[at, cols] = s
                    new_top = jnp.maximum(top, jnp.max(s, axis=0, keepdims=True))
                    factor = jnp.exp2(top - new_top)
                    e = jnp.exp2(s - new_top)
                    result.append((
                        new_top,
                        total * factor + jnp.sum(e, axis=0, keepdims=True),
                        dot * factor + jnp.sum(e * probs[at, cols], axis=0, keepdims=True),
                    ))
                return tuple(result)

            lowest = jnp.full((1, PAIR), NEG, jnp.float32)
            state = lax.fori_loop(0, tiles, stat_shifted, ((lowest, zero, zero),) * PAIRS)
            for p, (top, total, dot) in enumerate(state):
                cols = slice(p * PAIR, (p + 1) * PAIR)
                norms[0:1, cols] = jnp.ones((1, PAIR), jnp.float32)
                norms[1:2, cols] = dot / total
                norms[2:3, cols] = top + jnp.log2(total)

            def normalise(t, carry):
                at = pl.ds(pl.multiple_of(t * TILE, TILE), TILE)
                for p in range(PAIRS):
                    cols = slice(p * PAIR, (p + 1) * PAIR)
                    scores[at, cols] = jnp.exp2(scores[at, cols] - norms[2:3, cols])
                return carry

            lax.fori_loop(0, tiles, normalise, 0)

        dqt[...] = jnp.zeros((HD, WIDTH), jnp.float32)

        def grad(offset, size, carry):
            offset = pl.multiple_of(offset, TILE)
            rows = pl.ds(pl.multiple_of(base + offset, BLOCK), size)
            at = pl.ds(offset, size)
            kt = keys[rows, :].T
            dk = dkeys[rows, :]
            dv = dvalues[rows, :]
            for p in range(PAIRS):
                cols = slice(p * PAIR, (p + 1) * PAIR)
                prob = scores[at, cols] * norms[0:1, cols]
                ds = prob * (probs[at, cols] - norms[1:2, cols])
                prob = prob.astype(jnp.bfloat16)
                ds = ds.astype(jnp.bfloat16)
                dv = dv + jnp.dot(prob, gs[cols, :], preferred_element_type=jnp.float32)
                dk = dk + jnp.dot(ds, qs[cols, :], preferred_element_type=jnp.float32)
                dqt[:, cols] += jnp.dot(kt, ds, preferred_element_type=jnp.float32)
            dkeys[rows, :] = dk
            dvalues[rows, :] = dv
            return carry

        sweep(grad, 0)
        for k, dq in enumerate(dqs):
            @pl.when(i == k)
            def _(dq=dq):
                for g in range(GROUP):
                    cols = slice(g * HD, (g + 1) * HD)
                    dq[:, cols] = (dqt[:, cols].T * INV_ROOT).astype(dq.dtype)
        return carry

    lax.fori_loop(0, len(distances), block, 0)


def first_kernel(distances, plan, lengths, *refs):
    place = here()
    n = len(distances)
    qds, refs = refs[:n], refs[n:]
    sources, refs = (refs[:NY], refs[NY:2 * NY]), refs[2 * NY:]
    dqs, refs = refs[:n], refs[n:]
    keys, values, dkeys, dvalues = refs[:4]
    for core_rel, y_rel, z_rel, rows in slots(place, -1):
        keys[rows, :] = sources[core_rel][y_rel][z_rel, :, :HD]
        values[rows, :] = sources[core_rel][y_rel][z_rel, :, HD:]

    def clear(t, carry):
        rows = pl.ds(pl.multiple_of(t * TILE, TILE), TILE)
        dkeys[rows, :] = jnp.zeros((TILE, HD), jnp.float32)
        dvalues[rows, :] = jnp.zeros((TILE, HD), jnp.float32)
        return carry

    lax.fori_loop(0, SEQ // TILE, clear, 0)
    attend(place, plan, lengths, distances, qds, dqs, *refs)


def last_kernel(distances, plan, lengths, *refs):
    place = here()
    n = len(distances)
    qds, refs = refs[:n], refs[n:]
    (keys, values, dkeys_in, dvalues_in), refs = refs[:4], refs[4:]
    dqs, (keep, give, dkeys, dvalues), refs = refs[:n], refs[n:n + 4], refs[n + 4:]

    def load(t, carry):
        rows = pl.ds(pl.multiple_of(t * TILE, TILE), TILE)
        dkeys[rows, :] = dkeys_in[rows, :]
        dvalues[rows, :] = dvalues_in[rows, :]
        return carry

    lax.fori_loop(0, SEQ // TILE, load, 0)
    attend(place, plan, lengths, distances, qds, dqs, keys, values, dkeys, dvalues, *refs)
    for core_rel, y_rel, z_rel, rows in slots(place, 1):
        out = (keep, give)[core_rel]
        out[y_rel, z_rel, :, :HD] = (dkeys[rows, :] * INV_ROOT).astype(out.dtype)
        out[y_rel, z_rel, :, HD:] = dvalues[rows, :].astype(out.dtype)


def work_arrays():
    return [
        pltpu.VMEM((MAXTILES * TILE, WIDTH), jnp.float32),
        pltpu.VMEM((MAXTILES * TILE, WIDTH), jnp.float32),
        pltpu.VMEM((WIDTH, HD), jnp.bfloat16),
        pltpu.VMEM((HD, WIDTH), jnp.bfloat16),
        pltpu.VMEM((WIDTH, HD), jnp.bfloat16),
        pltpu.VMEM((HD, WIDTH), jnp.bfloat16),
        pltpu.VMEM((HD, WIDTH), jnp.float32),
        pltpu.VMEM((8, WIDTH), jnp.float32),
    ]


def attend_first(plan, lengths, distances, qds, own, other):
    n = len(distances)
    *dqs, keys, values, dkeys, dvalues = pl.pallas_call(
        functools.partial(first_kernel, distances),
        out_shape=[jax.ShapeDtypeStruct((BLOCK, WIDTH), jnp.bfloat16)] * n
        + [jax.ShapeDtypeStruct((SEQ, HD), jnp.bfloat16)] * 2
        + [jax.ShapeDtypeStruct((SEQ, HD), jnp.float32)] * 2,
        in_specs=[SMEM] * 2 + [VMEM] * (n + 2 * NY),
        out_specs=[VMEM] * (n + 4),
        scratch_shapes=work_arrays(),
        compiler_params=pltpu.CompilerParams(vmem_limit_bytes=VMEM_BYTES),
        cost_estimate=cost(0, 0),
        name="attention_first",
    )(plan, lengths, *qds, *own, *other)
    return dqs, (keys, values, dkeys, dvalues)


def attend_last(plan, lengths, distances, qds, state):
    n = len(distances)
    return pl.pallas_call(
        functools.partial(last_kernel, distances),
        out_shape=[jax.ShapeDtypeStruct((BLOCK, WIDTH), jnp.bfloat16)] * n
        + [jax.ShapeDtypeStruct((NY, NZ, BLOCK, 2 * HD), jnp.bfloat16)] * 2,
        in_specs=[SMEM] * 2 + [VMEM] * (n + 4),
        out_specs=[VMEM] * (n + 2),
        scratch_shapes=[pltpu.VMEM((SEQ, HD), jnp.float32)] * 2 + work_arrays(),
        compiler_params=pltpu.CompilerParams(vmem_limit_bytes=VMEM_BYTES),
        cost_estimate=cost(n * BLOCK_FLOPS, 8 * 2**20),
        name="attention_last",
    )(plan, lengths, *qds, *state)


def shards(queries, keys, values, grad_out, lengths, plan):
    z = lax.shift_right_logical(lax.axis_index("ctx").astype(jnp.int32), 3)

    def kv_part(d):
        at = ((z + d) & (NZ - 1)) * HD
        return jnp.concatenate(
            [lax.dynamic_slice_in_dim(keys, at, HD, 1), lax.dynamic_slice_in_dim(values, at, HD, 1)],
            axis=1,
        )

    with jax.named_scope("spread_keys"):
        row = [kv_part(0)] + [send(kv_part(d), d, 0, 0) for d in (1, 2, 3)]
        qd = pack(queries, grad_out)
        row, qd = lax.optimization_barrier((row, qd))
        row = jnp.stack(row)
        own = [row] + [send(row, 0, d, 0) for d in (1, 2, 3)]
    with jax.named_scope("spread_queries"):
        near = [send(qd[d], d, 0, 0) for d in (1, 3)]
        late, near = lax.optimization_barrier((qd[2], near))
        far = send(late, 2, 0, 0)
    with jax.named_scope("spread_keys"):
        own[1], near = lax.optimization_barrier((own[1], near))
        own[2], near = lax.optimization_barrier((own[2], near))
        own[3], near = lax.optimization_barrier((own[3], near))
        other = [send(part, 0, 0, 1) for part in own]

    with jax.named_scope("attention"):
        (dq0, dq1, dq3), state = attend_first(
            plan, lengths, (0, 1, 3), (qd[0], *near), own, other
        )
        dq2, keep, give = attend_last(plan, lengths, (2,), (far,), state)

    with jax.named_scope("return_keys"):
        both = keep.astype(jnp.float32) + send(give, 0, 0, 1).astype(jnp.float32)
        both, dq1, dq3 = lax.optimization_barrier((both.astype(jnp.bfloat16), dq1, dq3))
        back1, back3 = send(dq1, -1, 0, 0), send(dq3, -3, 0, 0)
        parts = [send(both[d], 0, d, 0) for d in (1, 2, 3)]
        dq2, back1 = lax.optimization_barrier((dq2, back1))
        back2 = send(dq2, -2, 0, 0)
        total = both[0].astype(jnp.float32)
        for part in parts:
            total = total + part.astype(jnp.float32)
        total, back1, back3 = lax.optimization_barrier((total.astype(jnp.bfloat16), back1, back3))
        heads = [total[0]] + [send(total[d], d, 0, 0) for d in (1, 2, 3)]
        grad_query = join_queries((dq0, back1, back2, back3))
        heads, grad_query = lax.optimization_barrier((heads, grad_query))
        return (grad_query, *join_keys(heads))


def solution(mesh):
    rows = P(("dp", "ctx"), None)
    return jax.shard_map(
        shards,
        mesh=mesh,
        in_specs=(rows, rows, rows, rows, P("dp"), P("dp")),
        out_specs=(rows, rows, rows),
        check_vma=False,
    )
```

```python
import functools
import math

import jax
import jax.numpy as jnp
from jax import lax
from jax.experimental import pallas as pl
from jax.experimental.pallas import tpu as pltpu
from jax.sharding import PartitionSpec as P

HD = 128
BLOCK = 128
DOCS = 8
KVH = 4
GROUP = 8
NZ = 4
NY = 4
SEQ = 4096
NBLK = 32
WIDTH = GROUP * HD
TILE = 256
MAXTILES = 9
SIZES = (4, 1)
PAIR = 256
PAIRS = WIDTH // PAIR
NEG = -1e30
SMALL_SUM = 1e-6
LARGE_SUM = 1e30
INV_ROOT = 1.0 / math.sqrt(HD)
EXP_SCALE = INV_ROOT / math.log(2.0)


SMEM = pl.BlockSpec(memory_space=pltpu.SMEM)
VMEM = pl.BlockSpec(memory_space=pltpu.VMEM)
HBM = pl.BlockSpec(memory_space=pltpu.HBM)
SMALL_VMEM_BYTES = 12 * 1024 * 1024
VMEM_BYTES = 40 * 1024 * 1024
BLOCK_FLOPS = 5 * 2 * WIDTH * 1024 * HD


def cost(flops, nbytes):
    return pl.CostEstimate(flops=flops, bytes_accessed=nbytes, transcendentals=0)


def ring(dz, dy, dc):
    return [
        ((z * NY + y) * 2 + c, ((z + dz) % NZ * NY + (y + dy) % NY) * 2 + (c ^ dc))
        for z in range(NZ)
        for y in range(NY)
        for c in range(2)
    ]


def send(x, dz, dy, dc):
    return lax.ppermute(x, "ctx", ring(dz, dy, dc))


def at_head(place, d, width):
    return pl.ds(pl.multiple_of((place[0] + d + NZ) % NZ * width, width), width)


def here():
    me = lax.axis_index("ctx")
    return lax.shift_right_logical(me, 3), lax.shift_right_logical(me, 1) & 3, me & 1


def pack_kernel(width, left, right, *refs):
    outs, sems = refs[:NZ], refs[NZ]
    place = here()
    copies = []
    for d, out in enumerate(outs):
        for half, source in enumerate((left, right)):
            copies.append(pltpu.make_async_copy(
                source.at[:, at_head(place, d, width)],
                out.at[:, half * width:(half + 1) * width],
                sems.at[len(copies)],
            ))
            copies[-1].start()
    for copy in copies:
        copy.wait()


def pack(left, right):
    width = left.shape[1] // KVH
    return pl.pallas_call(
        functools.partial(pack_kernel, width),
        out_shape=[jax.ShapeDtypeStruct((BLOCK, 2 * width), left.dtype)] * NZ,
        in_specs=[HBM] * 2,
        out_specs=[VMEM] * NZ,
        scratch_shapes=[pltpu.SemaphoreType.DMA((2 * NZ,))],
        compiler_params=pltpu.CompilerParams(vmem_limit_bytes=SMALL_VMEM_BYTES),
        cost_estimate=cost(0, 4 * left.size * 2),
        name="pack",
    )(left, right)


def join_queries_kernel(dq0, dq1, dq2, dq3, out, wide, sems):
    place = here()
    copies = []
    for d, part in enumerate((dq0, dq1, dq2, dq3)):
        wide[d] = part[...].astype(wide.dtype)
        copies.append(
            pltpu.make_async_copy(wide.at[d], out.at[:, at_head(place, d, WIDTH)], sems.at[d])
        )
        copies[-1].start()
    for copy in copies:
        copy.wait()


def join_queries(parts):
    return pl.pallas_call(
        join_queries_kernel,
        out_shape=jax.ShapeDtypeStruct((BLOCK, KVH * WIDTH), jnp.float32),
        in_specs=[VMEM] * NZ,
        out_specs=HBM,
        scratch_shapes=[
            pltpu.VMEM((NZ, BLOCK, WIDTH), jnp.float32),
            pltpu.SemaphoreType.DMA((NZ,)),
        ],
        compiler_params=pltpu.CompilerParams(vmem_limit_bytes=SMALL_VMEM_BYTES),
        cost_estimate=cost(0, BLOCK * KVH * WIDTH * 6),
        name="join_queries",
    )(*parts)


def join_keys_kernel(part0, part1, part2, part3, dk, dv):
    place = here()
    for d, part in enumerate((part0, part1, part2, part3)):
        dk[:, at_head(place, -d, HD)] = part[:, :HD].astype(dk.dtype)
        dv[:, at_head(place, -d, HD)] = part[:, HD:].astype(dv.dtype)


def join_keys(parts):
    return pl.pallas_call(
        join_keys_kernel,
        out_shape=[jax.ShapeDtypeStruct((BLOCK, KVH * HD), jnp.float32)] * 2,
        in_specs=[VMEM] * NZ,
        out_specs=[VMEM] * 2,
        compiler_params=pltpu.CompilerParams(vmem_limit_bytes=SMALL_VMEM_BYTES),
        cost_estimate=cost(0, BLOCK * KVH * HD * 12),
        name="join_keys",
    )(*parts)


def slots(place, sign):
    z, y, c = place
    for core_rel in range(2):
        for y_rel in range(NY):
            for z_rel in range(NZ):
                chip = ((z + sign * z_rel) & (NZ - 1)) * NY + ((y + sign * y_rel) & (NY - 1))
                slot = chip * 2 + (c ^ core_rel)
                yield core_rel, y_rel, z_rel, pl.ds(pl.multiple_of(slot * BLOCK, BLOCK), BLOCK)


def attend(
    place, plan, lengths, distances, qds, dqs,
    keys, values, dkeys, dvalues, scores, probs, qs, qst, gs, gst, dqt, norms, before=None,
):
    z, y, c = place[0], place[1], place[2]

    def block(i, carry):
        d = jnp.int32(distances[0])
        for k, qd in enumerate(qds):
            d = jnp.where(i == k, distances[k], d)

            @pl.when(i == k)
            def _(qd=qd):
                for g in range(GROUP):
                    rows = slice(g * BLOCK, (g + 1) * BLOCK)
                    q = qd[:, g * HD:(g + 1) * HD]
                    o = qd[:, WIDTH + g * HD:WIDTH + (g + 1) * HD]
                    qs[rows, :] = q
                    gs[rows, :] = o
                    qst[:, rows] = q.T
                    gst[:, rows] = o.T

        first = plan[((z - d + NZ) % NZ * NY + y) * 2 + c] * BLOCK
        pos = first + lax.broadcasted_iota(jnp.int32, (1, BLOCK), 1)
        start = jnp.zeros((1, BLOCK), jnp.int32)
        low = jnp.int32(0)
        end = jnp.int32(0)
        for e in range(DOCS):
            end = end + lengths[e]
            start = jnp.where(end <= pos, end, start)
            low = jnp.where(end <= first, end, low)
        tiles = (first + BLOCK - low // BLOCK * BLOCK + TILE - 1) // TILE
        base = jnp.maximum(first + BLOCK - tiles * TILE, 0)

        def sweep(body, state):
            done = jnp.int32(0)
            for size in SIZES:
                count = (tiles - done) // size
                state = lax.fori_loop(
                    0,
                    count,
                    lambda t, state, done=done, size=size: body(
                        (done + t * size) * TILE, size * TILE, state
                    ),
                    state,
                )
                done = done + count * size
            return state

        def mask(offset, size):
            key_pos = base + offset + lax.broadcasted_iota(jnp.int32, (size, BLOCK), 0)
            allowed = (key_pos >= start) & (key_pos <= pos)
            return jnp.concatenate([allowed] * (PAIR // BLOCK), axis=1)

        def stat(offset, size, state):
            offset = pl.multiple_of(offset, TILE)
            rows = pl.ds(pl.multiple_of(base + offset, BLOCK), size)
            at = pl.ds(offset, size)
            allowed = mask(offset, size)
            k, v = keys[rows, :], values[rows, :]
            result = []
            for p in range(PAIRS):
                cols = slice(p * PAIR, (p + 1) * PAIR)
                total, dot = state[p]
                s = jnp.dot(k, qst[:, cols], preferred_element_type=jnp.float32)
                e = jnp.exp2(jnp.where(allowed, s * EXP_SCALE, NEG))
                scores[at, cols] = e
                g = jnp.dot(v, gst[:, cols], preferred_element_type=jnp.float32)
                probs[at, cols] = g
                result.append((
                    total + jnp.sum(e, axis=0, keepdims=True),
                    dot + jnp.sum(e * g, axis=0, keepdims=True),
                ))
            return tuple(result)

        zero = jnp.zeros((1, PAIR), jnp.float32)
        state = sweep(stat, ((zero, zero),) * PAIRS)
        far_off = jnp.zeros((1, PAIR), jnp.float32)
        for p, (total, dot) in enumerate(state):
            cols = slice(p * PAIR, (p + 1) * PAIR)
            norms[0:1, cols] = 1.0 / total
            norms[1:2, cols] = dot / total
            fine = (total > SMALL_SUM) & (total < LARGE_SUM) & (jnp.abs(dot) < LARGE_SUM)
            far_off = jnp.where(fine, far_off, 1.0)

        @pl.when(jnp.max(far_off) > 0.0)
        def _():
            def stat_shifted(t, state):
                offset = pl.multiple_of(t * TILE, TILE)
                rows = pl.ds(pl.multiple_of(base + offset, BLOCK), TILE)
                at = pl.ds(offset, TILE)
                allowed = mask(offset, TILE)
                k = keys[rows, :]
                result = []
                for p in range(PAIRS):
                    cols = slice(p * PAIR, (p + 1) * PAIR)
                    top, total, dot = state[p]
                    s = jnp.dot(k, qst[:, cols], preferred_element_type=jnp.float32)
                    s = jnp.where(allowed, s * EXP_SCALE, NEG)
                    scores[at, cols] = s
                    new_top = jnp.maximum(top, jnp.max(s, axis=0, keepdims=True))
                    factor = jnp.exp2(top - new_top)
                    e = jnp.exp2(s - new_top)
                    result.append((
                        new_top,
                        total * factor + jnp.sum(e, axis=0, keepdims=True),
                        dot * factor + jnp.sum(e * probs[at, cols], axis=0, keepdims=True),
                    ))
                return tuple(result)

            lowest = jnp.full((1, PAIR), NEG, jnp.float32)
            state = lax.fori_loop(0, tiles, stat_shifted, ((lowest, zero, zero),) * PAIRS)
            for p, (top, total, dot) in enumerate(state):
                cols = slice(p * PAIR, (p + 1) * PAIR)
                norms[0:1, cols] = jnp.ones((1, PAIR), jnp.float32)
                norms[1:2, cols] = dot / total
                norms[2:3, cols] = top + jnp.log2(total)

            def normalise(t, carry):
                at = pl.ds(pl.multiple_of(t * TILE, TILE), TILE)
                for p in range(PAIRS):
                    cols = slice(p * PAIR, (p + 1) * PAIR)
                    scores[at, cols] = jnp.exp2(scores[at, cols] - norms[2:3, cols])
                return carry

            lax.fori_loop(0, tiles, normalise, 0)

        dqt[...] = jnp.zeros((HD, WIDTH), jnp.float32)

        def grad(offset, size, carry):
            offset = pl.multiple_of(offset, TILE)
            rows = pl.ds(pl.multiple_of(base + offset, BLOCK), size)
            at = pl.ds(offset, size)
            kt = keys[rows, :].T
            dk = (before or (dkeys, dvalues))[0][rows, :]
            dv = (before or (dkeys, dvalues))[1][rows, :]
            for p in range(PAIRS):
                cols = slice(p * PAIR, (p + 1) * PAIR)
                prob = scores[at, cols] * norms[0:1, cols]
                ds = prob * (probs[at, cols] - norms[1:2, cols])
                prob = prob.astype(jnp.bfloat16)
                ds = ds.astype(jnp.bfloat16)
                dv = dv + jnp.dot(prob, gs[cols, :], preferred_element_type=jnp.float32)
                dk = dk + jnp.dot(ds, qs[cols, :], preferred_element_type=jnp.float32)
                dqt[:, cols] += jnp.dot(kt, ds, preferred_element_type=jnp.float32)
            dkeys[rows, :] = dk
            dvalues[rows, :] = dv
            return carry

        sweep(grad, 0)
        for k, dq in enumerate(dqs):
            @pl.when(i == k)
            def _(dq=dq):
                for g in range(GROUP):
                    cols = slice(g * HD, (g + 1) * HD)
                    dq[:, cols] = (dqt[:, cols].T * INV_ROOT).astype(dq.dtype)
        return base, base + tiles * TILE

    zero = jnp.int32(0)
    return lax.fori_loop(0, len(distances), block, (zero, zero))


def first_kernel(distances, plan, lengths, *refs):
    place = here()
    n = len(distances)
    qds, refs = refs[:n], refs[n:]
    sources, refs = (refs[:NY], refs[NY:2 * NY]), refs[2 * NY:]
    dqs, refs = refs[:n], refs[n:]
    keys, values, dkeys, dvalues = refs[:4]
    for core_rel, y_rel, z_rel, rows in slots(place, -1):
        keys[rows, :] = sources[core_rel][y_rel][z_rel, :, :HD]
        values[rows, :] = sources[core_rel][y_rel][z_rel, :, HD:]

    def clear(t, carry):
        rows = pl.ds(pl.multiple_of(t * TILE, TILE), TILE)
        dkeys[rows, :] = jnp.zeros((TILE, HD), jnp.float32)
        dvalues[rows, :] = jnp.zeros((TILE, HD), jnp.float32)
        return carry

    lax.fori_loop(0, SEQ // TILE, clear, 0)
    attend(place, plan, lengths, distances, qds, dqs, *refs)


def last_kernel(distances, plan, lengths, *refs):
    place = here()
    n = len(distances)
    qds, refs = refs[:n], refs[n:]
    (keys, values, dkeys_in, dvalues_in), refs = refs[:4], refs[4:]
    dqs, (keep, give, dkeys, dvalues), refs = refs[:n], refs[n:n + 4], refs[n + 4:]

    low, high = attend(
        place, plan, lengths, distances, qds, dqs, keys, values, dkeys, dvalues, *refs,
        before=(dkeys_in, dvalues_in),
    )
    for core_rel, y_rel, z_rel, rows in slots(place, 1):
        out = (keep, give)[core_rel]
        changed = (rows.start >= low) & (rows.start < high)
        dk = jnp.where(changed, dkeys[rows, :], dkeys_in[rows, :])
        out[y_rel, z_rel, :, :HD] = (dk * INV_ROOT).astype(out.dtype)
        dv = jnp.where(changed, dvalues[rows, :], dvalues_in[rows, :])
        out[y_rel, z_rel, :, HD:] = dv.astype(out.dtype)


def work_arrays():
    return [
        pltpu.VMEM((MAXTILES * TILE, WIDTH), jnp.float32),
        pltpu.VMEM((MAXTILES * TILE, WIDTH), jnp.float32),
        pltpu.VMEM((WIDTH, HD), jnp.bfloat16),
        pltpu.VMEM((HD, WIDTH), jnp.bfloat16),
        pltpu.VMEM((WIDTH, HD), jnp.bfloat16),
        pltpu.VMEM((HD, WIDTH), jnp.bfloat16),
        pltpu.VMEM((HD, WIDTH), jnp.float32),
        pltpu.VMEM((8, WIDTH), jnp.float32),
    ]


def attend_first(plan, lengths, distances, qds, own, other):
    n = len(distances)
    *dqs, keys, values, dkeys, dvalues = pl.pallas_call(
        functools.partial(first_kernel, distances),
        out_shape=[jax.ShapeDtypeStruct((BLOCK, WIDTH), jnp.bfloat16)] * n
        + [jax.ShapeDtypeStruct((SEQ, HD), jnp.bfloat16)] * 2
        + [jax.ShapeDtypeStruct((SEQ, HD), jnp.float32)] * 2,
        in_specs=[SMEM] * 2 + [VMEM] * (n + 2 * NY),
        out_specs=[VMEM] * (n + 4),
        scratch_shapes=work_arrays(),
        compiler_params=pltpu.CompilerParams(vmem_limit_bytes=VMEM_BYTES),
        cost_estimate=cost(0, 0),
        name="attention_first",
    )(plan, lengths, *qds, *own, *other)
    return dqs, (keys, values, dkeys, dvalues)


def attend_last(plan, lengths, distances, qds, state):
    n = len(distances)
    return pl.pallas_call(
        functools.partial(last_kernel, distances),
        out_shape=[jax.ShapeDtypeStruct((BLOCK, WIDTH), jnp.bfloat16)] * n
        + [jax.ShapeDtypeStruct((NY, NZ, BLOCK, 2 * HD), jnp.bfloat16)] * 2,
        in_specs=[SMEM] * 2 + [VMEM] * (n + 4),
        out_specs=[VMEM] * (n + 2),
        scratch_shapes=[pltpu.VMEM((SEQ, HD), jnp.float32)] * 2 + work_arrays(),
        compiler_params=pltpu.CompilerParams(vmem_limit_bytes=VMEM_BYTES),
        cost_estimate=cost(n * BLOCK_FLOPS, 8 * 2**20),
        name="attention_last",
    )(plan, lengths, *qds, *state)


def shards(queries, keys, values, grad_out, lengths, plan):
    z = lax.shift_right_logical(lax.axis_index("ctx").astype(jnp.int32), 3)

    def kv_part(d):
        at = ((z + d) & (NZ - 1)) * HD
        return jnp.concatenate(
            [lax.dynamic_slice_in_dim(keys, at, HD, 1), lax.dynamic_slice_in_dim(values, at, HD, 1)],
            axis=1,
        )

    with jax.named_scope("spread_keys"):
        row = [kv_part(0)] + [send(kv_part(d), d, 0, 0) for d in (1, 2, 3)]
        qd = pack(queries, grad_out)
        row, qd = lax.optimization_barrier((row, qd))
        row = jnp.stack(row)
        own = [row] + [send(row, 0, d, 0) for d in (1, 2, 3)]
    with jax.named_scope("spread_queries"):
        near = [send(qd[d], d, 0, 0) for d in (1, 3)]
        late, near = lax.optimization_barrier((qd[2], near))
        far = send(late, 2, 0, 0)
    with jax.named_scope("spread_keys"):
        own[1], near = lax.optimization_barrier((own[1], near))
        own[2], near = lax.optimization_barrier((own[2], near))
        own[3], near = lax.optimization_barrier((own[3], near))
        other = [send(part, 0, 0, 1) for part in own]

    with jax.named_scope("attention"):
        (dq0, dq1, dq3), state = attend_first(
            plan, lengths, (0, 1, 3), (qd[0], *near), own, other
        )
        dq2, keep, give = attend_last(plan, lengths, (2,), (far,), state)

    with jax.named_scope("return_keys"):
        both = keep.astype(jnp.float32) + send(give, 0, 0, 1).astype(jnp.float32)
        both, dq1, dq3 = lax.optimization_barrier((both.astype(jnp.bfloat16), dq1, dq3))
        back1, back3 = send(dq1, -1, 0, 0), send(dq3, -3, 0, 0)
        parts = [send(both[d], 0, d, 0) for d in (1, 2, 3)]
        dq2, back1 = lax.optimization_barrier((dq2, back1))
        back2 = send(dq2, -2, 0, 0)
        total = both[0].astype(jnp.float32)
        for part in parts:
            total = total + part.astype(jnp.float32)
        total, back1, back3 = lax.optimization_barrier((total.astype(jnp.bfloat16), back1, back3))
        heads = [total[0]] + [send(total[d], d, 0, 0) for d in (1, 2, 3)]
        grad_query = join_queries((dq0, back1, back2, back3))
        heads, grad_query = lax.optimization_barrier((heads, grad_query))
        return (grad_query, *join_keys(heads))


def solution(mesh):
    rows = P(("dp", "ctx"), None)
    return jax.shard_map(
        shards,
        mesh=mesh,
        in_specs=(rows, rows, rows, rows, P("dp"), P("dp")),
        out_specs=(rows, rows, rows),
        check_vma=False,
    )
```
